128 devices in a mesh: fsdp: 8 (over z, x_hi), ctx: 16 (over x_lo, y, core).
Axes of the slice: x: 4 (x_hi: 2, x_lo: 2; x = x_hi * 2 + x_lo), y: 4, z: 4, core: 2. Of those that a mesh axis runs over, the one named last changes fastest.
Arguments:
- hidden_in: bfloat16 [8, 2048, 2048], P('fsdp', 'ctx'), may hold values from -6 to 6
- out_grad: bfloat16 [8, 2048, 2048], P('fsdp', 'ctx'), may hold values from -6 to 6
- positions: int32 [8, 2048], P('fsdp', 'ctx'), may hold values from 0 to 6142, as said below
- documents: int32 [8, 2048], P('fsdp', 'ctx'), may hold values from 0 to 1, as said below
- qkv_weight: float32 [2048, 6144], P(('fsdp', 'ctx')), may hold values from -0.125 to 0.125
- qkv_first: float32 [2048, 6144], P(('fsdp', 'ctx')), may hold values from -80 to 80
- qkv_second: float32 [2048, 6144], P(('fsdp', 'ctx')), may hold values from 983.04 to 3276.8
- out_weight: float32 [2048, 2048], P(('fsdp', 'ctx')), may hold values from -0.5 to 0.5
- out_first: float32 [2048, 2048], P(('fsdp', 'ctx')), may hold values from -28 to 28
- out_second: float32 [2048, 2048], P(('fsdp', 'ctx')), may hold values from 117.9648 to 393.216
- gate_weight: float32 [2048, 5632], P(('fsdp', 'ctx')), may hold values from -0.125 to 0.125
- gate_first: float32 [2048, 5632], P(('fsdp', 'ctx')), may hold values from -28 to 28
- gate_second: float32 [2048, 5632], P(('fsdp', 'ctx')), may hold values from 127.7952 to 425.984
- up_weight: float32 [2048, 5632], P(('fsdp', 'ctx')), may hold values from -0.125 to 0.125
- up_first: float32 [2048, 5632], P(('fsdp', 'ctx')), may hold values from -28 to 28
- up_second: float32 [2048, 5632], P(('fsdp', 'ctx')), may hold values from 127.7952 to 425.984
- down_weight: float32 [5632, 2048], P(('fsdp', 'ctx')), may hold values from -0.078125 to 0.078125
- down_first: float32 [5632, 2048], P(('fsdp', 'ctx')), may hold values from -48 to 48
- down_second: float32 [5632, 2048], P(('fsdp', 'ctx')), may hold values from 353.8944 to 1179.648
- small_params: float32 [7, 2048], P(None, ('fsdp', 'ctx')), may hold values from -1 to 1.4, as said below
- small_first: float32 [7, 2048], P(None, ('fsdp', 'ctx')), may hold values from -80 to 80
- small_second: float32 [7, 2048], P(None, ('fsdp', 'ctx')), may hold values from 983.04 to 3276.8
Outputs:
- block_out: bfloat16 [8, 2048, 2048], P('fsdp', 'ctx')
- input_grad: float32 [8, 2048, 2048], P('fsdp', 'ctx')
- qkv_weight_new: float32 [2048, 6144], P(('fsdp', 'ctx'))
- qkv_first_new: float32 [2048, 6144], P(('fsdp', 'ctx'))
- qkv_second_new: float32 [2048, 6144], P(('fsdp', 'ctx'))
- out_weight_new: float32 [2048, 2048], P(('fsdp', 'ctx'))
- out_first_new: float32 [2048, 2048], P(('fsdp', 'ctx'))
- out_second_new: float32 [2048, 2048], P(('fsdp', 'ctx'))
- gate_weight_new: float32 [2048, 5632], P(('fsdp', 'ctx'))
- gate_first_new: float32 [2048, 5632], P(('fsdp', 'ctx'))
- gate_second_new: float32 [2048, 5632], P(('fsdp', 'ctx'))
- up_weight_new: float32 [2048, 5632], P(('fsdp', 'ctx'))
- up_first_new: float32 [2048, 5632], P(('fsdp', 'ctx'))
- up_second_new: float32 [2048, 5632], P(('fsdp', 'ctx'))
- down_weight_new: float32 [5632, 2048], P(('fsdp', 'ctx'))
- down_first_new: float32 [5632, 2048], P(('fsdp', 'ctx'))
- down_second_new: float32 [5632, 2048], P(('fsdp', 'ctx'))
- small_params_new: float32 [7, 2048], P(None, ('fsdp', 'ctx'))
- small_first_new: float32 [7, 2048], P(None, ('fsdp', 'ctx'))
- small_second_new: float32 [7, 2048], P(None, ('fsdp', 'ctx'))
The draws below stay inside these ranges and needn't reach their ends.
Inputs may be any that keep to these rules, and one draw needn't show every extreme that they name: `documents`: each sequence holds document 0 on its first 1 to 127 positions and document 1 on all the rest. Within a document the positions rise by one; document 0 starts at a position below 4096, and document 1 ends at position 6142 in every sequence. `small_params`: gains lie in 0.6 to 1.4, shifts and biases in -1 to 1.
All inputs are finite; a program needn't handle non-finite values.
Results may differ from the reference program's by a relative error of at most 0.039.
Values may be sent and summed in bfloat16 or wider, within the bound.
A program may use at most 512 MiB of HBM per device.

```python
import math
import jax
import jax.numpy as jnp
from jax import lax

D = 2048
H = 32
HEAD = 64
FF = 5632
ROT = 16
BLK = 128
STEP = 10
SEQS = 8
LEN = 2048
TOKENS = 16384


def first_lengths(key):
    return jax.random.randint(key, (SEQS, 1), 1, BLK)


def draw_documents(key, part):
    first = first_lengths(key)
    steps = jnp.arange(LEN)[None, :]
    return jnp.broadcast_to(steps >= first, (SEQS, LEN)).astype(jnp.int32)


def draw_positions(key, part):
    first = first_lengths(key)
    key = jax.random.fold_in(key, 12)
    starts = jax.random.randint(key, (SEQS, 1), 0, 4096)
    steps = jnp.arange(LEN)[None, :]
    later = steps >= first
    top = 4094 + LEN
    return jnp.where(later, top - (LEN - 1) + steps, starts + steps).astype(jnp.int32)


def draw_small_params(key, part):
    key = jax.random.fold_in(key, 13)
    keys = jax.random.split(key, 2)
    gains = jax.random.uniform(keys[0], (7, D), jnp.float32, 0.6, 1.4)
    shifts = jnp.clip(0.2 * jax.random.normal(keys[1], (7, D), jnp.float32), -1.0, 1.0)
    order = jnp.arange(7)[:, None]
    is_gain = (order == 0) | (order == 5)
    return jnp.where(is_gain, gains, shifts).astype(jnp.float32)


def block_scale(key, dims, cuts, low, top_value):
    def one(dim, shards_of):
        heights = jax.random.uniform(jax.random.fold_in(jax.random.fold_in(key, 6), dim), (shards_of,), jnp.float32, low / len(cuts), top_value / len(cuts))
        return jnp.repeat(jnp.exp(heights), dims[dim] // shards_of).reshape((-1,) + (1,) * (len(dims) - dim - 1))

    factor_of = one(*cuts[0])
    for cut in cuts[1:]:
        factor_of = factor_of * one(*cut)
    return factor_of


def gaussian(stream_key, extent, width, limit, cuts=(), dtype=jnp.bfloat16):
    loudness = block_scale(stream_key, extent, cuts, -0.22, 0.18) if cuts else 1.0
    drawn = jax.random.normal(stream_key, extent, jnp.float32) * width * loudness
    return jnp.minimum(jnp.maximum(drawn, -limit), limit).astype(dtype)


def setup_inputs(seed: int = 0) -> dict:
    splits = jax.random.split(jax.random.key(seed), 23)
    hidden_in = gaussian(splits[0], (SEQS, LEN, D), 1.0, 6.0, ((0, 8), (1, 16)))
    out_grad = gaussian(splits[1], (SEQS, LEN, D), 1.0, 6.0, ((0, 8), (1, 16)))
    positions = draw_positions(jax.random.fold_in(splits[22], 71), 0)
    documents = draw_documents(jax.random.fold_in(splits[22], 71), 0)
    qkv_weight = gaussian(splits[4], (D, 3 * D), D ** -0.5, 0.125, ((0, 128),), jnp.float32)
    qkv_first = gaussian(splits[5], (D, 3 * D), (0.1 * TOKENS ** 0.5), 80.0, ((0, 128),), jnp.float32)
    qkv_second = jnp.clip(jnp.exp(math.log(3276.8) - 1.2039728 * jax.random.uniform(splits[6], (D, 3 * D), jnp.float32) ** block_scale(splits[6], (D, 3 * D), ((0, 128),), -0.2, 0.2)), 983.04, 3276.8)
    out_weight = gaussian(splits[7], (D, D), (D // 16) ** -0.5, 0.5, ((0, 128),), jnp.float32)
    out_first = gaussian(splits[8], (D, D), (0.035 * TOKENS ** 0.5), 28.0, ((0, 128),), jnp.float32)
    out_second = jnp.clip(jnp.exp(math.log(393.216) - 1.2039728 * jax.random.uniform(splits[9], (D, D), jnp.float32) ** block_scale(splits[9], (D, D), ((0, 128),), -0.2, 0.2)), 117.9648, 393.216)
    gate_weight = gaussian(splits[10], (D, FF), D ** -0.5, 0.125, ((0, 128),), jnp.float32)
    gate_first = gaussian(splits[11], (D, FF), (0.036 * TOKENS ** 0.5), 28.0, ((0, 128),), jnp.float32)
    gate_second = jnp.clip(jnp.exp(math.log(425.984) - 1.20397285 * jax.random.uniform(splits[12], (D, FF), jnp.float32) ** block_scale(splits[12], (D, FF), ((0, 128),), -0.2, 0.2)), 127.7952, 425.984)
    up_weight = gaussian(splits[13], (D, FF), D ** -0.5, 0.125, ((0, 128),), jnp.float32)
    up_first = gaussian(splits[14], (D, FF), (0.036 * TOKENS ** 0.5), 28.0, ((0, 128),), jnp.float32)
    up_second = jnp.clip(jnp.exp(math.log(425.984) - 1.20397285 * jax.random.uniform(splits[15], (D, FF), jnp.float32) ** block_scale(splits[15], (D, FF), ((0, 128),), -0.2, 0.2)), 127.7952, 425.984)
    down_weight = gaussian(splits[16], (FF, D), FF ** -0.5, 0.078125, ((0, 128),), jnp.float32)
    down_first = gaussian(splits[17], (FF, D), (0.06 * TOKENS ** 0.5), 48.0, ((0, 128),), jnp.float32)
    down_second = jnp.clip(jnp.exp(math.log(1179.648) - 1.2039727 * jax.random.uniform(splits[18], (FF, D), jnp.float32) ** block_scale(splits[18], (FF, D), ((0, 128),), -0.2, 0.2)), 353.8944, 1179.648)
    small_params = draw_small_params(jax.random.fold_in(splits[22], 71), 0)
    small_first = gaussian(splits[20], (7, D), (0.1 * TOKENS ** 0.5), 80.0, ((1, 128),), jnp.float32)
    small_second = jnp.clip(jnp.exp(math.log(3276.8) - 1.2039728 * jax.random.uniform(splits[21], (7, D), jnp.float32) ** block_scale(splits[21], (7, D), ((1, 128),), -0.2, 0.2)), 983.04, 3276.8)
    return dict(hidden_in=hidden_in, out_grad=out_grad, positions=positions, documents=documents, qkv_weight=qkv_weight, qkv_first=qkv_first, qkv_second=qkv_second, out_weight=out_weight, out_first=out_first, out_second=out_second, gate_weight=gate_weight, gate_first=gate_first, gate_second=gate_second, up_weight=up_weight, up_first=up_first, up_second=up_second, down_weight=down_weight, down_first=down_first, down_second=down_second, small_params=small_params, small_first=small_first, small_second=small_second)


@jax.custom_vjp
def low(v):
    return lax.optimization_barrier(v.astype(jnp.bfloat16)).astype(jnp.float32)

@jax.custom_vjp
def low_back(v):
    return v

def low_keep(v):
    return (low(v), None)

def low_pass(kept, grad):
    return (grad,)

def back_keep(v):
    return (v, None)

def back_low(kept, grad):
    return (low(grad),)
low.defvjp(low_keep, low_pass)
low_back.defvjp(back_keep, back_low)
HIGHEST = lax.Precision.HIGHEST
NORM_EPS = 1e-05
BETA_ONE = 0.9
BETA_TWO = 0.95
ADAM_EPS = 1e-08
MASKED = -1e+30

def layer_norm(rows, gain, shift):
    mean = lax.optimization_barrier(jnp.mean(rows, axis=-1, keepdims=True))
    centred = rows - mean
    spread = lax.optimization_barrier(jnp.mean(centred * centred, axis=-1, keepdims=True))
    return centred * lax.rsqrt(spread + NORM_EPS) * gain + shift

def rotary(heads, positions, sign):
    half = ROT // 2
    freq = 10000.0 ** (-jnp.arange(half).astype(jnp.float32) / half)
    angle = positions.astype(jnp.float32)[..., None] * freq
    cosine = jnp.cos(angle)[..., None, :]
    sine = sign * jnp.sin(angle)[..., None, :]
    first = heads[..., :half]
    second = heads[..., half:ROT]
    return jnp.concatenate([first * cosine - second * sine, second * cosine + first * sine, heads[..., ROT:]], axis=-1)

def attend_group(query, key, value, allowed):
    scores = jnp.einsum('qhd,khd->hqk', query, key, precision=HIGHEST) * HEAD ** (-0.5)
    scores = low_back(scores)
    scores = jnp.where(allowed[None], scores, MASKED)
    highest = lax.optimization_barrier(jnp.max(scores, axis=-1, keepdims=True))
    weights = jnp.where(allowed[None], jnp.exp(scores - highest), 0.0)
    probs = low(weights / lax.optimization_barrier(jnp.sum(weights, axis=-1, keepdims=True)))
    return jnp.einsum('hqk,khd->qhd', probs, value, precision=HIGHEST)

def attend_sequence(pieces):
    query, key, value, documents = pieces
    steps = jnp.arange(LEN)
    allowed = (steps[None, :] <= steps[:, None]) & (documents[None, :] == documents[:, None])
    group = min(H, 8)

    def split(array):
        return jnp.moveaxis(array.reshape(LEN, H // group, group, HEAD), 1, 0)

    def one_group(parts):
        return attend_group(parts[0], parts[1], parts[2], allowed)
    result = lax.map(jax.checkpoint(one_group), (split(query), split(key), split(value)))
    return jnp.moveaxis(result, 0, 1).reshape(LEN, H, HEAD)

def forward(inputs, qkv_weight, out_weight, gate_weight, up_weight, down_weight, small_params, positions, documents):
    rows = inputs.reshape(TOKENS, D)
    params = low(small_params)
    w_qkv = low(qkv_weight)
    w_out = low(out_weight)
    w_gate = low(gate_weight)
    w_up = low(up_weight)
    w_down = low(down_weight)
    normed = low(layer_norm(rows, params[0], params[1]))
    mixed = low_back(jnp.dot(normed, w_qkv, precision=HIGHEST) + params[2:5].reshape(3 * D))
    heads = mixed.reshape(SEQS, LEN, 3, H, HEAD)
    query = low(rotary(heads[:, :, 0], positions, 1.0))
    key = low(rotary(heads[:, :, 1], positions, 1.0))
    value = low(heads[:, :, 2])
    attended = lax.map(jax.checkpoint(attend_sequence), (query, key, value, documents))
    attended = low_back(low(attended.reshape(TOKENS, D)))
    branch = low_back(jnp.dot(attended, w_out, precision=HIGHEST))
    middle = rows + branch
    normed_two = low(layer_norm(middle, params[5], params[6]))
    gate = low_back(jnp.dot(normed_two, w_gate, precision=HIGHEST))
    up = low_back(jnp.dot(normed_two, w_up, precision=HIGHEST))
    hidden = low(jax.nn.silu(gate) * up)
    result = middle + jnp.dot(hidden, w_down, precision=HIGHEST)
    return result.reshape(SEQS, LEN, D)

def adamw(weight, first, second, gradient, rate, decay):
    first_new = BETA_ONE * first + (1.0 - BETA_ONE) * gradient
    second_new = BETA_TWO * second + (1.0 - BETA_TWO) * gradient * gradient
    mean_hat = first_new / (1.0 - BETA_ONE ** STEP)
    square_hat = second_new / (1.0 - BETA_TWO ** STEP)
    weight_new = weight - rate * (mean_hat / (jnp.sqrt(square_hat) + ADAM_EPS) + decay * weight)
    return (weight_new, first_new, second_new)

def reference(hidden_in, out_grad, positions, documents, qkv_weight, qkv_first, qkv_second, out_weight, out_first, out_second, gate_weight, gate_first, gate_second, up_weight, up_first, up_second, down_weight, down_first, down_second, small_params, small_first, small_second):
    inputs = hidden_in.astype(jnp.float32)

    def run(x_in, w_a, w_b, w_c, w_d, w_e, w_f):
        return forward(x_in, w_a, w_b, w_c, w_d, w_e, w_f, positions, documents)
    result, pull = jax.vjp(run, inputs, qkv_weight, out_weight, gate_weight, up_weight, down_weight, small_params)
    grads = pull(out_grad.astype(jnp.float32))
    qkv_new = adamw(qkv_weight, qkv_first, qkv_second, grads[1], D ** (-0.5), 0.1)
    out_new = adamw(out_weight, out_first, out_second, grads[2], (D // 16) ** (-0.5), 0.1)
    gate_new = adamw(gate_weight, gate_first, gate_second, grads[3], D ** (-0.5), 0.1)
    up_new = adamw(up_weight, up_first, up_second, grads[4], D ** (-0.5), 0.1)
    down_new = adamw(down_weight, down_first, down_second, grads[5], FF ** (-0.5), 0.1)
    small_new = adamw(small_params, small_first, small_second, grads[6], 2.0, 0.0)
    return (result.astype(jnp.bfloat16), grads[0], qkv_new[0], qkv_new[1], qkv_new[2], out_new[0], out_new[1], out_new[2], gate_new[0], gate_new[1], gate_new[2], up_new[0], up_new[1], up_new[2], down_new[0], down_new[1], down_new[2], small_new[0], small_new[1], small_new[2])
```

```python
import functools
import math

import jax
import jax.numpy as jnp
import numpy as np
from jax import lax
from jax.experimental import pallas as pl
from jax.experimental.pallas import tpu as pltpu
from jax.sharding import Mesh
from jax.sharding import PartitionSpec as P

D = 2048
H = 32
HEAD = 64
FF = 5632
ROT = 16
STEP = 10

NORM_EPS = 1e-05
BETA_ONE = 0.9
BETA_TWO = 0.95
ADAM_EPS = 1e-08
MASKED = -1e30

AXES = ("z", "xh", "xl", "y", "core")
YC = ("y", "core")
ZX = ("z", "xh", "xl")
HALF = 1024
SEQ = 2048
BF = jnp.bfloat16
F32 = jnp.float32


def norm_forward(rows, gain, shift):
    mean = jnp.mean(rows, axis=-1, keepdims=True)
    centred = rows - mean
    scale = lax.rsqrt(jnp.mean(centred * centred, axis=-1, keepdims=True) + NORM_EPS)
    unit = centred * scale
    return (unit * gain + shift, unit, scale)


def norm_backward(gradient, unit, scale, gain):
    along = gradient * gain
    inner = (
        along
        - jnp.mean(along, axis=-1, keepdims=True)
        - unit * jnp.mean(along * unit, axis=-1, keepdims=True)
    )
    return (inner * scale, jnp.sum(gradient * unit, axis=0), jnp.sum(gradient, axis=0))


def adamw(weight, first, second, gradient, rate, decay):
    first_new = BETA_ONE * first + (1.0 - BETA_ONE) * gradient
    second_new = BETA_TWO * second + (1.0 - BETA_TWO) * gradient * gradient
    mean_hat = first_new / (1.0 - BETA_ONE**STEP)
    square_hat = second_new / (1.0 - BETA_TWO**STEP)
    weight_new = weight - rate * (mean_hat / (jnp.sqrt(square_hat) + ADAM_EPS) + decay * weight)
    return (weight_new, first_new, second_new)


def dot_nn(a, b):
    return jnp.dot(a, b, preferred_element_type=F32)


def dot_nt(a, b):
    return lax.dot_general(a, b, (((1,), (1,)), ((), ())), preferred_element_type=F32)


def dot_tn(a, b):
    return lax.dot_general(a, b, (((0,), (0,)), ((), ())), preferred_element_type=F32)


def rotary_tables(positions):
    half = ROT // 2
    freq = 10000.0 ** (-jnp.arange(half).astype(F32) / half)
    lane = np.arange(128) % HEAD
    lane_freq = jnp.where(lane < ROT, jnp.tile(freq, 128 // half), 0.0)
    angle = positions.astype(F32)[:, None] * lane_freq[None, :]
    sine = jnp.sin(angle)
    low = jnp.asarray(lane < half)
    return jnp.cos(angle), jnp.where(low, -sine, 0.0), jnp.where(low, 0.0, sine)


def rotate(x, cosine, below, above):
    return x * cosine + pltpu.roll(x, 120, 1) * below + pltpu.roll(x, 8, 1) * above


def remote(src, dst, sems, at, device):
    return pltpu.make_async_remote_copy(
        src_ref=src,
        dst_ref=dst,
        send_sem=sems.at[0, at],
        recv_sem=sems.at[1, at],
        device_id=device,
        device_id_type=pl.DeviceIdType.MESH,
    )


def places():
    y, c, z = lax.axis_index("y"), lax.axis_index("core"), lax.axis_index("z")
    x = lax.axis_index("xh") * 2 + lax.axis_index("xl")
    step = lambda v, k: lax.rem(v + k, 4)
    at_x = lambda v: {"xh": lax.div(v, 2), "xl": lax.rem(v, 2)}
    devices = {
        "twin": {"core": 1 - c},
        "up": {"y": step(y, 1)},
        "down": {"y": step(y, 3)},
        "across": {"y": step(y, 2)},
        "up_twin": {"y": step(y, 1), "core": 1 - c},
        "down_twin": {"y": step(y, 3), "core": 1 - c},
        "across_twin": {"y": step(y, 2), "core": 1 - c},
        "x+": at_x(step(x, 1)),
        "x-": at_x(step(x, 3)),
        "z+": {"z": step(z, 1)},
        "z-": {"z": step(z, 3)},
        "pair": {"xl": 1 - lax.axis_index("xl")},
    }
    return y, c, x, z, devices


def add_low(a, b):
    return (a.astype(F32) + b.astype(F32)).astype(BF)


def ring_gather(block, cut, i, plus, minus, sems, base, pending):
    before, after = lax.rem(i + 3, 4), lax.rem(i + 1, 4)
    to_plus = remote(block(i), block(i), sems, base, plus)
    to_minus = remote(block(i), block(i), sems, base + 1, minus)
    to_plus.start()
    to_minus.start()
    yield
    to_plus.wait_recv()
    lo = cut(block(before))[0]
    pass_plus = remote(lo, lo, sems, base + 2, plus)
    pass_plus.start()
    yield
    to_minus.wait_recv()
    hi = cut(block(after))[1]
    pass_minus = remote(hi, hi, sems, base + 3, minus)
    pass_minus.start()
    pending += [to_plus, to_minus, pass_plus, pass_minus]
    yield
    pass_plus.wait_recv()
    pass_minus.wait_recv()


def ring_scatter(block, cut, i, plus, minus, acc, near, sems, base, pending):
    before, after, across = lax.rem(i + 3, 4), lax.rem(i + 1, 4), lax.rem(i + 2, 4)
    lo, hi = (lambda v: cut(v)[0]), (lambda v: cut(v)[1])
    far_plus = remote(lo(block(across)), lo(near.at[0]), sems, base, plus)
    far_minus = remote(hi(block(across)), hi(near.at[0]), sems, base + 1, minus)
    own_plus = remote(hi(block(after)), hi(near.at[1]), sems, base + 2, plus)
    own_minus = remote(lo(block(before)), lo(near.at[2]), sems, base + 3, minus)
    for copy in (far_plus, far_minus, own_plus, own_minus):
        copy.start()
    yield
    far_plus.wait_recv()
    lo(acc)[...] = add_low(lo(block(after))[...], lo(near.at[0])[...])
    sum_plus = remote(lo(acc), lo(near.at[1]), sems, base + 4, plus)
    sum_plus.start()
    yield
    far_minus.wait_recv()
    hi(acc)[...] = add_low(hi(block(before))[...], hi(near.at[0])[...])
    sum_minus = remote(hi(acc), hi(near.at[2]), sems, base + 5, minus)
    sum_minus.start()
    pending += [far_plus, far_minus, own_plus, own_minus, sum_plus, sum_minus]
    yield
    for copy in (own_plus, own_minus, sum_plus, sum_minus):
        copy.wait_recv()


class GatherTokens:
    peers = ("twin", "up", "down")
    n_sems = 10

    def __init__(self, rows, width):
        self.ins = [((rows, width), BF)]
        self.outs = [((8, rows, width), BF)]
        self.scratch = []
        self.rows = rows

    def run(self, ins, outs, scratch, sems, base, place, pending):
        y, c, _, _, to = place
        (x_ref,), (out_ref,) = ins, outs
        half = self.rows // 2
        lo, hi = pl.ds(0, half), pl.ds(half, half)
        at = lambda k: lax.rem(y + k, 4) * 2 + c
        mine = pltpu.make_async_copy(x_ref, out_ref.at[at(0)], sems.at[0, base + 9])
        s_up = remote(x_ref, out_ref.at[at(0)], sems, base, to["up"])
        s_down = remote(x_ref, out_ref.at[at(0)], sems, base + 1, to["down"])
        s_twin = remote(x_ref, out_ref.at[at(0)], sems, base + 2, to["twin"])
        for copy in (s_up, s_down, s_twin, mine):
            copy.start()
        pass_on = lambda ref, k, device: remote(ref, ref, sems, base + k, to[device])
        yield
        s_up.wait_recv()
        r_up = pass_on(out_ref.at[at(3), lo], 3, "up")
        t_down = pass_on(out_ref.at[at(3)], 5, "twin")
        r_up.start()
        t_down.start()
        yield
        s_down.wait_recv()
        r_down = pass_on(out_ref.at[at(1), hi], 4, "down")
        t_up = pass_on(out_ref.at[at(1)], 6, "twin")
        r_down.start()
        t_up.start()
        yield
        r_up.wait_recv()
        t_lo = pass_on(out_ref.at[at(2), lo], 7, "twin")
        t_lo.start()
        yield
        r_down.wait_recv()
        t_hi = pass_on(out_ref.at[at(2), hi], 8, "twin")
        t_hi.start()
        pending += [s_up, s_down, s_twin, r_up, r_down, t_down, t_up, t_lo, t_hi]
        yield
        for copy in (s_twin, t_down, t_up, t_lo, t_hi):
            copy.wait_recv()
        mine.wait()


class SumTokens:
    peers = ("twin", "up", "down")
    n_sems = 10

    def __init__(self, rows, width):
        self.ins = [((8, rows, width), BF)]
        self.outs = [((rows, width), F32)]
        self.scratch = [
            pltpu.VMEM((4, rows, width), BF),
            pltpu.VMEM((3, rows, width), BF),
            pltpu.VMEM((rows, width), BF),
            pltpu.VMEM((3, rows, width), BF),
        ]
        self.rows = rows

    def run(self, ins, outs, scratch, sems, base, place, pending):
        y, c, _, _, to = place
        (p_ref,), (out_ref,) = ins, outs
        from_twin, pair, acc, near = scratch
        half = self.rows // 2
        cut = lambda v: (v.at[pl.ds(0, half)], v.at[pl.ds(half, half)])
        swaps = []
        for k, off in enumerate((2, 1, 3, 0)):
            at = lax.rem(y + off, 4) * 2
            copy = remote(p_ref.at[at + 1 - c], from_twin.at[k], sems, base + k, to["twin"])
            copy.start()
            swaps.append(copy)
        yield
        for k, off in enumerate((2, 1, 3)):
            swaps[k].wait_recv()
            pair[k] = add_low(p_ref[lax.rem(y + off, 4) * 2 + c], from_twin[k])
            if k == 0:
                far_plus = remote(
                    cut(pair.at[0])[0], cut(near.at[0])[0], sems, base + 4, to["up"]
                )
                far_minus = remote(
                    cut(pair.at[0])[1], cut(near.at[0])[1], sems, base + 5, to["down"]
                )
                far_plus.start()
                far_minus.start()
            elif k == 1:
                own_plus = remote(
                    cut(pair.at[1])[1], cut(near.at[1])[1], sems, base + 6, to["up"]
                )
                own_plus.start()
            else:
                own_minus = remote(
                    cut(pair.at[2])[0], cut(near.at[2])[0], sems, base + 7, to["down"]
                )
                own_minus.start()
        yield
        far_plus.wait_recv()
        cut(acc)[0][...] = add_low(cut(pair.at[1])[0][...], cut(near.at[0])[0][...])
        sum_plus = remote(cut(acc)[0], cut(near.at[1])[0], sems, base + 8, to["up"])
        sum_plus.start()
        yield
        far_minus.wait_recv()
        cut(acc)[1][...] = add_low(cut(pair.at[2])[1][...], cut(near.at[0])[1][...])
        sum_minus = remote(cut(acc)[1], cut(near.at[2])[1], sems, base + 9, to["down"])
        sum_minus.start()
        swaps[3].wait_recv()
        out_ref[...] = p_ref[y * 2 + c].astype(F32) + from_twin[3].astype(F32)
        pending += swaps + [far_plus, far_minus, own_plus, own_minus, sum_plus, sum_minus]
        yield
        for copy in (own_plus, own_minus, sum_plus, sum_minus):
            copy.wait_recv()
        out_ref[...] += near[1].astype(F32) + near[2].astype(F32)


def rows_or_columns(rows, width):
    if rows % 32 == 0:
        return lambda v: (v.at[pl.ds(0, rows // 2)], v.at[pl.ds(rows // 2, rows // 2)])
    return lambda v: (v.at[:, pl.ds(0, width // 2)], v.at[:, pl.ds(width // 2, width // 2)])


def firsts(v):
    return v.at[pl.ds(0, 2)], v.at[pl.ds(2, 2)]


class GatherWeights:
    peers = ("x+", "x-", "z+", "z-")
    n_sems = 17

    def __init__(self, rows, width):
        self.ins = [((rows, width), BF)]
        self.outs = [((4, 4, rows, width), BF)]
        self.scratch = []
        self.rows, self.width = rows, width

    def rings(self, out_ref, sems, base, place, pending):
        _, _, x, z, to = place
        first = self.width // 256 * 128
        a, b = pl.ds(0, first), pl.ds(first, self.width - first)
        every = pl.ds(0, self.rows)
        cut_a = rows_or_columns(self.rows, first)
        cut_b = rows_or_columns(self.rows, self.width - first)

        def along_x_first():
            yield from ring_gather(
                lambda j: out_ref.at[z, j, every, a], cut_a, x, to["x+"], to["x-"], sems, base, pending
            )
            yield from ring_gather(
                lambda j: out_ref.at[j, pl.ds(0, 4), every, a], firsts, z, to["z+"], to["z-"], sems, base + 4,
                pending,
            )

        def along_z_first():
            yield from ring_gather(
                lambda j: out_ref.at[j, x, every, b], cut_b, z, to["z+"], to["z-"], sems, base + 8, pending
            )
            yield from ring_gather(
                lambda j: out_ref.at[pl.ds(0, 4), j, every, b], firsts, x, to["x+"], to["x-"], sems,
                base + 12, pending,
            )

        yield from both(along_x_first(), along_z_first())

    def run(self, ins, outs, scratch, sems, base, place, pending):
        _, _, x, z, _ = place
        (x_ref,), (out_ref,) = ins, outs
        mine = pltpu.make_async_copy(x_ref, out_ref.at[z, x], sems.at[0, base + 16])
        mine.start()
        mine.wait()
        yield from self.rings(out_ref, sems, base, place, pending)


class SumWeights:
    peers = ("x+", "x-", "z+", "z-")
    n_sems = 24

    def __init__(self, rows, width):
        self.ins = [((4, 4, rows, width), BF)]
        self.outs = [((rows, width), BF)]
        self.rows, self.width = rows, width
        first = width // 256 * 128
        self.widths = (first, width - first)
        self.scratch = []
        for w in self.widths:
            self.scratch += [
                pltpu.VMEM((4, rows, w), BF),
                pltpu.VMEM((3, 4, rows, w), BF),
                pltpu.VMEM((4, rows, w), BF),
                pltpu.VMEM((rows, w), BF),
                pltpu.VMEM((3, rows, w), BF),
            ]

    def run(self, ins, outs, scratch, sems, base, place, pending):
        _, _, x, z, to = place
        (p_ref,), (out_ref,) = ins, outs
        every = pl.ds(0, self.rows)

        def one(order, bufs, base):
            acc, near, total, acc_two, near_two = bufs
            width = self.widths[order]
            columns = pl.ds(order * self.widths[0], width)
            cut = rows_or_columns(self.rows, width)
            four = pl.ds(0, 4)
            if order == 0:
                block = lambda j: p_ref.at[four, j, every, columns]
                i, k, far, close = x, z, ("x+", "x-"), ("z+", "z-")
            else:
                block = lambda j: p_ref.at[j, four, every, columns]
                i, k, far, close = z, x, ("z+", "z-"), ("x+", "x-")
            yield from ring_scatter(
                block, firsts, i, to[far[0]], to[far[1]], acc, near, sems, base, pending
            )
            total[...] = (
                block(i)[...].astype(F32) + near[1].astype(F32) + near[2].astype(F32)
            ).astype(BF)
            yield from ring_scatter(
                lambda j: total.at[j], cut, k, to[close[0]], to[close[1]], acc_two, near_two, sems,
                base + 6, pending,
            )
            out_ref[every, columns] = (
                total[k].astype(F32) + near_two[1].astype(F32) + near_two[2].astype(F32)
            ).astype(BF)

        yield from both(one(0, scratch[:5], base), one(1, scratch[5:], base + 12))


class Swap:
    peers = ("twin", "up", "down", "across", "up_twin", "down_twin", "across_twin")
    n_sems = 8
    steps = ((0, 1), (1, 0), (3, 0), (2, 0), (1, 1), (3, 1), (2, 1))

    def __init__(self, rows, width):
        self.ins = [((8, rows, width), BF)]
        self.outs = [((8, rows, width), BF)]
        self.scratch = []

    def send(self, x_ref, out_ref, sems, base, place):
        y, c, _, _, to = place
        me = y * 2 + c
        copies = [pltpu.make_async_copy(x_ref.at[me], out_ref.at[me], sems.at[0, base + 7])]
        for k, (name, (up, other)) in enumerate(zip(self.peers, self.steps)):
            at = lax.rem(y + up, 4) * 2 + (1 - c if other else c)
            copies.append(remote(x_ref.at[at], out_ref.at[me], sems, base + k, to[name]))
        for copy in copies:
            copy.start()
        return copies

    def run(self, ins, outs, scratch, sems, base, place, pending):
        copies = self.send(ins[0], outs[0], sems, base, place)
        yield
        copies[0].wait()
        for copy in copies[1:]:
            copy.wait_recv()
        pending += copies[1:]


class SwapThenGather:
    peers = Swap.peers + GatherWeights.peers

    def __init__(self, rows, width):
        self.swap = Swap(rows, width)
        self.gather = GatherWeights(8 * rows, width)
        self.ins = self.swap.ins
        self.outs = self.gather.outs
        self.scratch = [pltpu.VMEM((8, rows, width), BF)]
        self.rows, self.width = rows, width
        self.n_sems = 8 + 8 + self.gather.n_sems

    def run(self, ins, outs, scratch, sems, base, place, pending):
        _, _, x, z, _ = place
        (out_ref,), (landed,) = outs, scratch
        yield from self.swap.run(ins, (landed,), (), sems, base, place, pending)
        for k in range(8):
            out_ref[z, x, k * self.rows : (k + 1) * self.rows] = landed[k]
        yield from self.gather.rings(out_ref, sems, base + 16, place, pending)


class SwapThenSum:
    peers = Swap.peers + SumWeights.peers

    def __init__(self, rows, width):
        self.swap = Swap(rows, width)
        self.sum = SumWeights(rows, width)
        self.ins = self.swap.ins
        self.outs = self.sum.outs
        self.scratch = [
            pltpu.VMEM((8, rows, width), BF),
            pltpu.VMEM((4, 4, rows, width), BF),
        ] + self.sum.scratch
        self.n_sems = 8 + self.sum.n_sems

    def run(self, ins, outs, scratch, sems, base, place, pending):
        landed, spread = scratch[:2]
        yield from self.swap.run(ins, (landed,), (), sems, base, place, pending)
        total = jnp.sum(landed[...].astype(F32), axis=0).astype(BF)
        spread[...] = jnp.broadcast_to(total[None, None], spread.shape)
        yield from self.sum.run((spread,), outs, scratch[2:], sems, base + 8, place, pending)


def both(*parts):
    parts = list(parts)
    while parts:
        for part in list(parts):
            try:
                next(part)
            except StopIteration:
                parts.remove(part)
        yield


def in_order(parts, order):
    for letter in order:
        next(parts["abcdef".index(letter)], None)
    for _ in both(*parts):
        pass


def size(shape, dtype):
    return math.prod(shape) * jnp.dtype(dtype).itemsize


def comm_kernel(parts, order, *refs):
    sems = refs[-1]
    n_in = sum(len(p.ins) for p in parts)
    n_out = sum(len(p.outs) for p in parts)
    ins, outs, scratch = list(refs[:n_in]), list(refs[n_in : n_in + n_out]), list(refs[n_in + n_out : -1])
    place = places()
    names = []
    for p in parts:
        names += [n for n in p.peers if n not in names]
    barrier = pltpu.get_barrier_semaphore()
    for name in names:
        pl.semaphore_signal(
            barrier, inc=1, device_id=place[4][name], device_id_type=pl.DeviceIdType.MESH
        )
    pl.semaphore_wait(barrier, len(names))
    base, running, pending = 0, [], []
    for p in parts:
        taken = []
        for refs_of, count in ((ins, len(p.ins)), (outs, len(p.outs)), (scratch, len(p.scratch))):
            taken.append([refs_of.pop(0) for _ in range(count)])
        running.append(p.run(*taken, sems, base, place, pending))
        base += p.n_sems
    in_order(running, order)
    for copy in pending:
        copy.wait_send()


def comm(collective_id, order, *pairs):
    parts = [p for p, _ in pairs]
    operands = [x.reshape(spec[0]) for p, xs in pairs for x, spec in zip(xs, p.ins)]
    spaces = [spec[2] if len(spec) > 2 else pltpu.VMEM for p in parts for spec in p.ins]
    outs = [o for p in parts for o in p.outs]
    held = sum(size(*spec[:2]) for p in parts for spec in p.ins + p.outs)
    held += sum(size(s.shape, s.dtype) for p in parts for s in p.scratch)
    sent = sum(math.prod(shape) for shape, _ in outs) * 2
    return pl.pallas_call(
        functools.partial(comm_kernel, parts, order),
        out_shape=[jax.ShapeDtypeStruct(*o) for o in outs],
        in_specs=[pl.BlockSpec(memory_space=space) for space in spaces],
        out_specs=[pl.BlockSpec(memory_space=pltpu.VMEM)] * len(outs),
        scratch_shapes=[s for p in parts for s in p.scratch]
        + [pltpu.SemaphoreType.DMA((2, sum(p.n_sems for p in parts)))],
        compiler_params=pltpu.CompilerParams(
            collective_id=collective_id, has_side_effects=True, vmem_limit_bytes=held + (10 << 20)
        ),
        cost_estimate=pl.CostEstimate(flops=0, bytes_accessed=20 * sent, transcendentals=0),
    )(*operands)


ROWS = 256


def qkv_kernel(u_ref, w_ref, gain_ref, shift_ref, bias_ref, c_ref, a_ref, b_ref, h_ref, out_ref):
    h = (u_ref[...].astype(F32) * gain_ref[...] + shift_ref[...]).astype(BF)
    h_ref[...] = h
    mixed = dot_nn(h, w_ref[:, 0:768]) + bias_ref[...]
    for j in range(6):
        part = mixed[:, j * 128 : (j + 1) * 128]
        if j % 3 < 2:
            part = rotate(part, c_ref[...], a_ref[...], b_ref[...])
        out_ref[:, j * 128 : (j + 1) * 128] = part.astype(BF)


def rowwise(width):
    return pl.BlockSpec((ROWS, width), lambda i: (i, 0))


def fixed(*shape):
    return pl.BlockSpec(shape, lambda i: (0,) * len(shape))


def qkv_call(u, w, gain, shift, bias, tables):
    return pl.pallas_call(
        qkv_kernel,
        out_shape=(
            jax.ShapeDtypeStruct((HALF, D), BF),
            jax.ShapeDtypeStruct((HALF, 768), BF),
        ),
        grid=(HALF // ROWS,),
        in_specs=[rowwise(D), fixed(D, 896), fixed(1, D), fixed(1, D), fixed(1, 768)]
        + [rowwise(128)] * 3,
        out_specs=(rowwise(D), rowwise(768)),
        compiler_params=pltpu.CompilerParams(vmem_limit_bytes=40 << 20),
        cost_estimate=pl.CostEstimate(
            flops=2 * HALF * D * 768, bytes_accessed=14 << 20, transcendentals=0
        ),
    )(u, w, gain, shift, bias, *tables)


BLOCK = 512
Q, K, V = slice(0, 128), slice(128, 256), slice(256, 384)


def only(x, h):
    lane = lax.broadcasted_iota(jnp.int32, (1, 128), 1)
    return jnp.where((lane >= h * HEAD) & (lane < (h + 1) * HEAD), x, jnp.zeros_like(x))


def rows_of(k):
    return slice(k * BLOCK, (k + 1) * BLOCK)


def allowed_mask(first_len, key_half, kb, query_half, qb, diagonal):
    key = lax.broadcasted_iota(jnp.int32, (BLOCK, BLOCK), 0) + kb * BLOCK
    query = lax.broadcasted_iota(jnp.int32, (BLOCK, BLOCK), 1) + qb * BLOCK
    allowed = None
    if diagonal and kb == qb:
        allowed = key <= query
    if kb == 0:
        same = (key + key_half * HALF >= first_len) | (query + query_half * HALF < first_len)
        allowed = same if allowed is None else allowed & same
    return allowed


def lanes(at, width):
    return pl.ds(pl.multiple_of(at * width, 128), width)


class Attend:
    peers = ("pair",)
    n_sems = 6

    def __init__(self):
        self.ins = [((1, 1), jnp.int32, pltpu.SMEM), ((HALF, 768), BF)]
        self.outs = [
            ((HALF, 256), BF),
            ((2, 128, HALF), F32),
            ((2, 8, HALF), F32),
            ((2, HALF, 384), BF),
        ]
        self.scratch = [pltpu.VMEM((2, 8, HALF), F32), pltpu.VMEM((2, HALF, 128), BF)]

    def run(self, ins, outs, scratch, sems, base, place, pending):
        len_ref, qkv_ref = ins
        o_ref, acc_ref, top_ref, x_ref = outs
        total_ref, half_ref = scratch
        pair = place[4]["pair"]
        xl = lax.axis_index("xl")
        first_len = len_ref[0, 0]
        sent = []
        for b in range(2):
            copy = remote(
                qkv_ref.at[rows_of(b), lanes(1 - xl, 384)], x_ref.at[xl, rows_of(b)], sems, base + b, pair
            )
            copy.start()
            sent.append(copy)
        kept = pltpu.make_async_copy(qkv_ref.at[:, lanes(xl, 384)], x_ref.at[xl], sems.at[0, base + 2])
        kept.start()
        kept.wait()
        yield

        def block(query_half, key_half, qb, h, state, diagonal):
            qs = rows_of(qb)
            qh = only(x_ref[query_half, qs, Q] * jnp.asarray(HEAD**-0.5, BF), h)
            top, total, acc = state
            for kb in range(qb + 1 if diagonal else 2):
                ks = rows_of(kb)
                scores = dot_nt(x_ref[key_half, ks, K], qh)
                allowed = allowed_mask(first_len, key_half, kb, query_half, qb, diagonal)
                if allowed is not None:
                    scores = jnp.where(allowed, scores, MASKED)
                new_top = jnp.maximum(top, jnp.max(scores, axis=0, keepdims=True))
                weights = jnp.exp(scores - new_top)
                if allowed is not None:
                    weights = jnp.where(allowed, weights, 0.0)
                shrink = jnp.exp(top - new_top)
                total = total * shrink + jnp.sum(weights, axis=0, keepdims=True)
                part = dot_tn(only(x_ref[key_half, ks, V], h), weights.astype(BF))
                acc = acc * shrink + part[h * HEAD : (h + 1) * HEAD]
                top = new_top
            top_ref[query_half, h : h + 1, qs] = top
            total_ref[query_half, h : h + 1, qs] = total
            acc_ref[query_half, h * HEAD : (h + 1) * HEAD, qs] = acc

        def diagonal(half):
            for qb in range(2):
                for h in range(2):
                    start = (
                        jnp.full((1, BLOCK), MASKED, F32),
                        jnp.zeros((1, BLOCK), F32),
                        jnp.zeros((HEAD, BLOCK), F32),
                    )
                    block(half, half, qb, h, start, True)

        def finish(half):
            for qb in range(2):
                qs = rows_of(qb)
                for h in range(2):
                    hs = slice(h * HEAD, (h + 1) * HEAD)
                    total = total_ref[half, h : h + 1, qs]
                    acc_ref[half, hs, qs] = acc_ref[half, hs, qs] / total
                    top_ref[half, h : h + 1, qs] = top_ref[half, h : h + 1, qs] + jnp.log(total)
                half_ref[half, qs, :] = acc_ref[half, :, qs].T.astype(BF)

        diagonal(xl)
        yield
        for copy in sent:
            copy.wait_recv()
        diagonal(1 - xl)
        yield
        for qb in range(2):
            for h in range(2):
                qs = rows_of(qb)
                state = (
                    top_ref[1, h : h + 1, qs],
                    total_ref[1, h : h + 1, qs],
                    acc_ref[1, h * HEAD : (h + 1) * HEAD, qs],
                )
                block(1, 0, qb, h, state, False)
            yield
        finish(1 - xl)
        back = remote(half_ref.at[1 - xl], o_ref.at[:, lanes(xl, 128)], sems, base + 3, pair)
        back.start()
        finish(xl)
        mine = pltpu.make_async_copy(half_ref.at[xl], o_ref.at[:, lanes(xl, 128)], sems.at[0, base + 4])
        mine.start()
        pending += sent + [back]
        yield
        mine.wait()
        back.wait_recv()


class AttendBack:
    peers = ("pair",)
    n_sems = 6

    def __init__(self):
        self.ins = [
            ((1, 1), jnp.int32, pltpu.SMEM),
            ((2, HALF, 384), BF),
            ((HALF, 256), BF),
            ((2, 128, HALF), F32),
            ((2, 8, HALF), F32),
        ] + [((2, HALF, 128), F32)] * 3
        self.outs = [((HALF, 768), BF)]
        self.scratch = [
            pltpu.VMEM((2, HALF, 128), BF),
            pltpu.VMEM((2, 128, HALF), F32),
            pltpu.VMEM((2, HALF, 128), F32),
            pltpu.VMEM((2, HALF, 128), F32),
            pltpu.VMEM((2, HALF, 384), BF),
        ]

    def run(self, ins, outs, scratch, sems, base, place, pending):
        len_ref, x_ref, own_ref, ot_ref, lse_ref, c_ref, a_ref, b_ref = ins
        (out_ref,) = outs
        do_ref, dqt_ref, dk_ref, dv_ref, half_ref = scratch
        pair = place[4]["pair"]
        xl = lax.axis_index("xl")
        first_len = len_ref[0, 0]
        sent = remote(own_ref.at[:, lanes(1 - xl, 128)], do_ref.at[xl], sems, base, pair)
        sent.start()
        kept = pltpu.make_async_copy(own_ref.at[:, lanes(xl, 128)], do_ref.at[xl], sems.at[0, base + 1])
        kept.start()
        kept.wait()
        yield

        def block(query_half, key_half, qb, h, diagonal):
            qs = rows_of(qb)
            hs = slice(h * HEAD, (h + 1) * HEAD)
            do = do_ref[query_half, qs, :]
            qh = only(x_ref[query_half, qs, Q] * jnp.asarray(HEAD**-0.5, BF), h)
            doh = only(do, h)
            delta = jnp.sum(
                doh.astype(F32).T[hs] * ot_ref[query_half, hs, qs], axis=0, keepdims=True
            )
            lse = lse_ref[query_half, h : h + 1, qs]
            for kb in range(qb + 1 if diagonal else 2):
                ks = rows_of(kb)
                k = x_ref[key_half, ks, K]
                scores = dot_nt(k, qh)
                probs = jnp.exp(scores - lse)
                allowed = allowed_mask(first_len, key_half, kb, query_half, qb, diagonal)
                if allowed is not None:
                    probs = jnp.where(allowed, probs, 0.0)
                pulled = dot_nt(x_ref[key_half, ks, V], doh)
                ds = (probs * (pulled - delta)).astype(BF)
                dv = dot_nn(probs.astype(BF), doh)
                dk = dot_nn(ds, qh)
                dq = dot_tn(only(k, h), ds)[hs]
                if diagonal and h == 0 and qb == kb:
                    dv_ref[key_half, ks, :] = dv
                    dk_ref[key_half, ks, :] = dk
                else:
                    dv_ref[key_half, ks, :] += dv
                    dk_ref[key_half, ks, :] += dk
                if diagonal and kb == 0:
                    dqt_ref[query_half, hs, qs] = dq
                else:
                    dqt_ref[query_half, hs, qs] += dq

        def finish(half):
            for b in range(2):
                bs = rows_of(b)
                c, below, above = c_ref[half, bs, :], -a_ref[half, bs, :], -b_ref[half, bs, :]
                dq = dqt_ref[half, :, bs].T * HEAD**-0.5
                half_ref[half, bs, Q] = rotate(dq, c, below, above).astype(BF)
                half_ref[half, bs, K] = rotate(dk_ref[half, bs, :], c, below, above).astype(BF)
                half_ref[half, bs, V] = dv_ref[half, bs, :].astype(BF)

        for qb in range(2):
            for h in range(2):
                block(xl, xl, qb, h, True)
        yield
        sent.wait_recv()
        for qb in range(2):
            for h in range(2):
                block(1 - xl, 1 - xl, qb, h, True)
        yield
        for qb in range(2):
            for h in range(2):
                block(1, 0, qb, h, False)
            yield
        finish(1 - xl)
        back = remote(half_ref.at[1 - xl], out_ref.at[:, lanes(xl, 384)], sems, base + 2, pair)
        back.start()
        finish(xl)
        mine = pltpu.make_async_copy(half_ref.at[xl], out_ref.at[:, lanes(xl, 384)], sems.at[0, base + 3])
        mine.start()
        pending += [sent, back]
        yield
        mine.wait()
        back.wait_recv()


def feed_kernel(h_ref, dy_ref, gate_ref, up_ref, down_ref, hid_ref, dg_ref, du_ref, dh_ref, y_ref):
    gate, up = dot_nn(h_ref[...], gate_ref[...]), dot_nn(h_ref[...], up_ref[...])
    sigmoid = jax.nn.sigmoid(gate)
    activated = gate * sigmoid
    hidden = (activated * up).astype(BF)
    hid_ref[...] = hidden
    d_hidden = dot_nt(dy_ref[...], down_ref[...])
    d_gate = (d_hidden * up * sigmoid * (1.0 + gate * (1.0 - sigmoid))).astype(BF)
    d_up = (d_hidden * activated).astype(BF)
    dg_ref[...] = d_gate
    du_ref[...] = d_up
    dh_ref[...] = (dot_nt(d_gate, gate_ref[...]) + dot_nt(d_up, up_ref[...])).astype(BF)
    y_ref[...] = dot_nn(hidden, down_ref[...]).astype(BF)


def feed_call(h, dy, w_gate, w_up, w_down):
    return pl.pallas_call(
        feed_kernel,
        out_shape=(
            jax.ShapeDtypeStruct((HALF, 768), BF),
            jax.ShapeDtypeStruct((HALF, 768), BF),
            jax.ShapeDtypeStruct((HALF, 768), BF),
            jax.ShapeDtypeStruct((HALF, D), BF),
            jax.ShapeDtypeStruct((HALF, D), BF),
        ),
        grid=(HALF // ROWS,),
        in_specs=[rowwise(D), rowwise(D), fixed(D, 768), fixed(D, 768), fixed(768, D)],
        out_specs=(rowwise(768), rowwise(768), rowwise(768), rowwise(D), rowwise(D)),
        compiler_params=pltpu.CompilerParams(vmem_limit_bytes=56 << 20),
        cost_estimate=pl.CostEstimate(
            flops=6 * 2 * HALF * D * 768, bytes_accessed=30 << 20, transcendentals=HALF * 768
        ),
    )(h, dy, w_gate, w_up, w_down)


def weight_grad_kernel(n, a_ref, *refs):
    for b_ref, out_ref in zip(refs[:n], refs[n:]):
        out_ref[...] = dot_tn(a_ref[...], b_ref[...]).astype(BF)


def weight_grad(a, step, *others):
    rows = a.shape[1]
    return pl.pallas_call(
        functools.partial(weight_grad_kernel, len(others)),
        out_shape=[jax.ShapeDtypeStruct((rows, b.shape[1]), BF) for b in others],
        grid=(rows // step,),
        in_specs=[pl.BlockSpec((HALF, step), lambda i: (0, i))] + [fixed(*b.shape) for b in others],
        out_specs=[pl.BlockSpec((step, b.shape[1]), lambda i: (i, 0)) for b in others],
        compiler_params=pltpu.CompilerParams(vmem_limit_bytes=40 << 20),
        cost_estimate=pl.CostEstimate(
            flops=2 * HALF * rows * sum(b.shape[1] for b in others),
            bytes_accessed=12 << 20,
            transcendentals=0,
        ),
    )(a, *others)


def last_kernel(dx_ref, u_ref, w_ref, dh_ref, sums_ref, bias_ref):
    dh = dot_nt(dx_ref[...], w_ref[:, 0:768])
    dh_ref[...] = dh.astype(BF)

    @pl.when(pl.program_id(0) == 0)
    def _():
        sums_ref[...] = jnp.zeros_like(sums_ref)
        bias_ref[...] = jnp.zeros_like(bias_ref)

    sums_ref[0:1] += jnp.sum(dh * u_ref[...].astype(F32), axis=0, keepdims=True)
    sums_ref[1:2] += jnp.sum(dh, axis=0, keepdims=True)
    bias_ref[0:1] += jnp.sum(dx_ref[...].astype(F32), axis=0, keepdims=True)


def last_call(dx, u, w):
    return pl.pallas_call(
        last_kernel,
        out_shape=(
            jax.ShapeDtypeStruct((HALF, D), BF),
            jax.ShapeDtypeStruct((8, D), F32),
            jax.ShapeDtypeStruct((8, 768), F32),
        ),
        grid=(HALF // ROWS,),
        in_specs=[rowwise(768), rowwise(D), fixed(D, 896)],
        out_specs=(rowwise(D), fixed(8, D), fixed(8, 768)),
        compiler_params=pltpu.CompilerParams(vmem_limit_bytes=40 << 20),
        cost_estimate=pl.CostEstimate(
            flops=2 * HALF * D * 768, bytes_accessed=14 << 20, transcendentals=0
        ),
    )(dx, u, w)


TO_HEADS = [(f * 16 + ctx, ctx * 8 + f) for f in range(8) for ctx in range(16)]
TO_OWNER = [(b, a) for a, b in TO_HEADS]


def hidden_columns(weight):
    split = weight.astype(BF).reshape(16, 16, 8, 44).transpose(2, 0, 1, 3)
    return jnp.pad(split, ((0, 0), (0, 0), (0, 0), (0, 4))).reshape(8, 16, 768)


def hidden_columns_back(grad):
    return grad.reshape(8, 16, 16, 48)[..., :44].transpose(1, 2, 0, 3).reshape(16, FF)


def local(
    hidden_in, out_grad, positions, documents,
    qkv_weight, qkv_first, qkv_second,
    out_weight, out_first, out_second,
    gate_weight, gate_first, gate_second,
    up_weight, up_first, up_second,
    down_weight, down_first, down_second,
    small_params, small_first, small_second,
):
    xh, xl, z = lax.axis_index("xh"), lax.axis_index("xl"), lax.axis_index("z")
    yc = lax.axis_index("y") * 2 + lax.axis_index("core")
    place = (z * 2 + xh) * 2 + xl

    first_here = jnp.sum(1 - documents)
    start_here = positions[0, 0]
    marks = jnp.stack([first_here, start_here // 64, start_here % 64]).astype(BF)
    tile = jnp.concatenate(
        [small_params.astype(BF), jnp.pad(marks, (0, 13))[None]], axis=0
    )
    tile = jnp.pad(tile, ((0, 8), (0, 112)))
    qkv_piece = jnp.concatenate(
        [
            qkv_weight.astype(BF).reshape(16, 3, 8, 2, 128).transpose(2, 0, 3, 1, 4).reshape(8, 16, 768),
            jnp.broadcast_to(tile[None], (8, 16, 128)),
        ],
        axis=2,
    )
    rows = hidden_in.reshape(128, D).astype(F32)
    outer = out_grad.reshape(128, D)
    mean = jnp.mean(rows, axis=-1, keepdims=True)
    centred = rows - mean
    scale_one = lax.rsqrt(jnp.mean(centred * centred, axis=-1, keepdims=True) + NORM_EPS)
    unit_one = centred * scale_one
    gu_piece = jnp.concatenate([hidden_columns(gate_weight), hidden_columns(up_weight)], axis=2)
    w_all, u_all, gu_mine = comm(
        0,
        "aabcaaabbaabbabc",
        (SwapThenGather(16, 896), (qkv_piece,)),
        (GatherTokens(128, D), (unit_one.astype(BF),)),
        (Swap(16, 1536), (gu_piece,)),
    )
    gu_mine = gu_mine.reshape(128, 1536)
    w_gate = lax.all_gather(gu_mine[:, :768], ZX, axis=0, tiled=True)
    u_all = u_all.reshape(HALF, D)
    w_qkv = w_all.reshape(D, 896)

    tiles = w_qkv[:, 768:784].reshape(128, 16, 16)
    params = tiles[:, :7].transpose(1, 0, 2).reshape(7, D).astype(F32)
    marks = lax.dynamic_index_in_dim(tiles[:, 7, :3], (z * 2 + xh) * 16, keepdims=False)
    marks = marks.astype(jnp.int32)
    first_len = marks[0]
    step = jnp.arange(SEQ)
    tables = rotary_tables(
        jnp.where(step < first_len, marks[1] * 64 + marks[2] + step, 4095 + step)
    )
    first_len = first_len.reshape(1, 1)
    half_tables = [lax.dynamic_slice_in_dim(t, xl * HALF, HALF, axis=0) for t in tables]
    bias = lax.dynamic_slice_in_dim(params[2:5], yc * 256, 256, axis=1)
    bias = bias.reshape(3, 2, 128).transpose(1, 0, 2).reshape(1, 768)

    h1, qkv = qkv_call(u_all, w_qkv, params[0:1], params[1:2], bias, half_tables)
    out_rows = lax.ppermute(out_weight.astype(BF), AXES, TO_HEADS)
    o, attended_t, lse, heads, w_out, dy = comm(
        1,
        "acaccabccabbbacbbaba",
        (Attend(), (first_len, qkv)),
        (GatherWeights(16, D), (out_rows,)),
        (GatherTokens(128, D), (outer,)),
    )
    w_out, dy = w_out.reshape(256, D), dy.reshape(HALF, D)
    branch_part = dot_nn(o, w_out).astype(BF)
    branch, w_up = comm(
        2,
        "ababbbaabbab",
        (SumTokens(128, D), (branch_part,)),
        (GatherWeights(128, 768), (gu_mine[:, 768:],)),
    )
    middle = rows + branch
    normed_two, unit_two, scale_two = norm_forward(middle, params[5], params[6])
    down_piece = jnp.pad(down_weight.astype(BF), ((0, 4), (0, 0)))
    h2, w_down = comm(
        3,
        "abbbbaabbaaab",
        (GatherTokens(128, D), (normed_two.astype(BF),)),
        (GatherWeights(48, D), (down_piece,)),
    )
    h2 = h2.reshape(HALF, D)
    hidden, d_gate_low, d_up_low, dh2_part, y_part = feed_call(
        h2, dy, w_gate, w_up.reshape(D, 768), w_down.reshape(768, D)
    )

    (d_down,) = weight_grad(hidden, 256, dy)
    d_gate, d_up = weight_grad(h2, 512, d_gate_low, d_up_low)
    g_up = lax.psum_scatter(d_up, ZX, scatter_dimension=0, tiled=True)
    d_normed_two, g_down = comm(
        4, "ababbaabbbab", (SumTokens(128, D), (dh2_part,)), (SumWeights(48, D), (d_down,))
    )
    d_middle_part, d_gain_two, d_shift_two = norm_backward(
        d_normed_two, unit_two, scale_two, params[5]
    )
    d_middle = outer.astype(F32) + d_middle_part
    dx2, g_gate = comm(
        5, "abbbaabbbaaab", (GatherTokens(128, D), (d_middle.astype(BF),)), (SumWeights(128, 768), (d_gate,))
    )
    dx2 = dx2.reshape(HALF, D)
    do = dot_nt(dx2, w_out).astype(BF)
    d_qkv_low, branch_two = comm(
        7,
        "abaaaaabbbba",
        (
            AttendBack(),
            (first_len, heads, do, attended_t, lse, *[t.reshape(2, HALF, 128) for t in tables]),
        ),
        (SumTokens(128, D), (y_part,)),
    )
    block_out = (middle + branch_two).reshape(1, 128, D).astype(BF)
    d_out = dot_tn(o, dx2).astype(BF)
    dh1_part, sums, d_bias = last_call(d_qkv_low, u_all, w_qkv)
    (d_qkv,) = weight_grad(h1, 512, d_qkv_low)
    d_bias = d_bias[0].reshape(2, 3, 128).transpose(1, 0, 2).reshape(3, 256)
    d_small = jnp.concatenate(
        [
            sums[0:2],
            lax.dynamic_update_slice_in_dim(jnp.zeros((3, D), F32), d_bias, yc * 256, axis=1),
            d_gain_two[None],
            d_shift_two[None],
            jnp.zeros((9, D), F32),
        ],
        axis=0,
    )
    small_piece = d_small.astype(BF).reshape(16, 16, 8, 16).transpose(2, 0, 1, 3).reshape(8, 16, 256)
    small_piece = jnp.pad(small_piece, ((0, 0), (0, 0), (0, 256)))
    d_normed, g_qkv, g_out, g_small = comm(
        6,
        "abcdabbccdaabcdddbbccddabcd",
        (SumTokens(128, D), (dh1_part,)),
        (SumWeights(128, 768), (d_qkv,)),
        (SumWeights(16, D), (d_out,)),
        (SwapThenSum(16, 512), (small_piece,)),
    )
    d_rows_part = norm_backward(d_normed, unit_one, scale_one, params[0])[0]
    input_grad = (d_middle + d_rows_part).reshape(1, 128, D)

    g_out = lax.ppermute(g_out, AXES, TO_OWNER).astype(F32)
    (back,) = comm(8, "", (Swap(16, 2304), (jnp.concatenate([g_qkv, g_gate, g_up], axis=1),)))
    g_qkv = back[..., :768].reshape(8, 16, 2, 3, 128).transpose(1, 3, 0, 2, 4).reshape(16, 3 * D)
    g_gate = hidden_columns_back(back[..., 768:1536])
    g_up = hidden_columns_back(back[..., 1536:])
    g_small = lax.dynamic_index_in_dim(
        g_small[:, :256].reshape(16, 16, 16), place, axis=1, keepdims=False
    )[:7].astype(F32)

    updates = (
        adamw(qkv_weight, qkv_first, qkv_second, g_qkv.astype(F32), D ** (-0.5), 0.1),
        adamw(out_weight, out_first, out_second, g_out, (D // 16) ** (-0.5), 0.1),
        adamw(gate_weight, gate_first, gate_second, g_gate.astype(F32), D ** (-0.5), 0.1),
        adamw(up_weight, up_first, up_second, g_up.astype(F32), D ** (-0.5), 0.1),
        adamw(down_weight, down_first, down_second, g_down[:44].astype(F32), FF ** (-0.5), 0.1),
        adamw(small_params, small_first, small_second, g_small, 2.0, 0.0),
    )
    return (block_out, input_grad, *[x for u in updates for x in u])


def solution(mesh):
    fine = Mesh(mesh.devices.reshape(4, 2, 2, 4, 2), AXES)
    tokens = P(("z", "xh"), ("xl", "y", "core"), None)
    marks = P(("z", "xh"), ("xl", "y", "core"))
    rows = P(AXES, None)
    small = P(None, AXES)
    in_specs = (tokens, tokens, marks, marks) + (rows,) * 15 + (small,) * 3
    out_specs = (tokens, tokens) + (rows,) * 15 + (small,) * 3
    return jax.shard_map(local, mesh=fine, in_specs=in_specs, out_specs=out_specs, check_vma=False)
```

```python
import functools
import math

import jax
import jax.numpy as jnp
import numpy as np
from jax import lax
from jax.experimental import pallas as pl
from jax.experimental.pallas import tpu as pltpu
from jax.sharding import Mesh
from jax.sharding import PartitionSpec as P

D = 2048
H = 32
HEAD = 64
FF = 5632
ROT = 16
STEP = 10

NORM_EPS = 1e-05
BETA_ONE = 0.9
BETA_TWO = 0.95
ADAM_EPS = 1e-08
MASKED = -1e30

AXES = ("z", "xh", "xl", "y", "core")
YC = ("y", "core")
ZX = ("z", "xh", "xl")
HALF = 1024
SEQ = 2048
BF = jnp.bfloat16
F32 = jnp.float32


def norm_forward(rows, gain, shift):
    mean = jnp.mean(rows, axis=-1, keepdims=True)
    centred = rows - mean
    scale = lax.rsqrt(jnp.mean(centred * centred, axis=-1, keepdims=True) + NORM_EPS)
    unit = centred * scale
    return (unit * gain + shift, unit, scale)


def norm_backward(gradient, unit, scale, gain):
    along = gradient * gain
    inner = (
        along
        - jnp.mean(along, axis=-1, keepdims=True)
        - unit * jnp.mean(along * unit, axis=-1, keepdims=True)
    )
    return (inner * scale, jnp.sum(gradient * unit, axis=0), jnp.sum(gradient, axis=0))


def adamw(weight, first, second, gradient, rate, decay):
    first_new = BETA_ONE * first + (1.0 - BETA_ONE) * gradient
    second_new = BETA_TWO * second + (1.0 - BETA_TWO) * gradient * gradient
    mean_hat = first_new / (1.0 - BETA_ONE**STEP)
    square_hat = second_new / (1.0 - BETA_TWO**STEP)
    weight_new = weight - rate * (mean_hat / (jnp.sqrt(square_hat) + ADAM_EPS) + decay * weight)
    return (weight_new, first_new, second_new)


def dot_nn(a, b):
    return jnp.dot(a, b, preferred_element_type=F32)


def dot_nt(a, b):
    return lax.dot_general(a, b, (((1,), (1,)), ((), ())), preferred_element_type=F32)


def dot_tn(a, b):
    return lax.dot_general(a, b, (((0,), (0,)), ((), ())), preferred_element_type=F32)


def document_marks(params_ref):
    sequence = lax.axis_index("z") * 2 + lax.axis_index("xh")
    row = params_ref[7:8, pl.ds(pl.multiple_of(sequence * 256, 128), 128)]
    lane = lax.broadcasted_iota(jnp.int32, (1, 128), 1)
    length, high, low = [
        jnp.sum(jnp.where(lane == k, row, 0.0), axis=1, keepdims=True) for k in range(3)
    ]
    return length, high * 64.0 + low


def rotary_angles(params_ref, half):
    length, start = document_marks(params_ref)
    place = lax.broadcasted_iota(jnp.int32, (8, HALF), 1).astype(F32) + half * float(HALF)
    position = jnp.where(place < length, start + place, 4095.0 + place)
    row = lax.broadcasted_iota(jnp.int32, (8, HALF), 0)
    freq = jnp.zeros((8, HALF), F32)
    for k in range(ROT // 2):
        freq = jnp.where(row == k, float(np.float32(10000.0) ** np.float32(-k / (ROT // 2))), freq)
    angle = position * freq
    parts = []
    for value in (jnp.cos(angle), jnp.sin(angle)):
        high = value.astype(BF).astype(F32)
        parts += [high, value - high]
    return jnp.concatenate(parts, axis=0).astype(BF)


def rotary_tables(angles):
    row = lax.broadcasted_iota(jnp.int32, (16, 128), 0) % 8
    lane = lax.broadcasted_iota(jnp.int32, (16, 128), 1) % HEAD
    spread = jnp.where((lane < ROT) & (lane % 8 == row), 1.0, 0.0).astype(BF)
    lane = lax.broadcasted_iota(jnp.int32, (1, 128), 1) % HEAD
    cosine = dot_tn(angles[0:16], spread) + jnp.where(lane < ROT, 0.0, 1.0)
    sine = dot_tn(angles[16:32], spread)
    return cosine, jnp.where(lane < ROT // 2, -sine, 0.0), jnp.where(lane < ROT // 2, 0.0, sine)


def rotate(x, cosine, below, above):
    return x * cosine + pltpu.roll(x, 120, 1) * below + pltpu.roll(x, 8, 1) * above


def remote(src, dst, sems, at, device):
    return pltpu.make_async_remote_copy(
        src_ref=src,
        dst_ref=dst,
        send_sem=sems.at[0, at],
        recv_sem=sems.at[1, at],
        device_id=device,
        device_id_type=pl.DeviceIdType.MESH,
    )


def places():
    y, c, z = lax.axis_index("y"), lax.axis_index("core"), lax.axis_index("z")
    x = lax.axis_index("xh") * 2 + lax.axis_index("xl")
    step = lambda v, k: lax.rem(v + k, 4)
    at_x = lambda v: {"xh": lax.div(v, 2), "xl": lax.rem(v, 2)}
    devices = {
        "twin": {"core": 1 - c},
        "up": {"y": step(y, 1)},
        "down": {"y": step(y, 3)},
        "across": {"y": step(y, 2)},
        "up_twin": {"y": step(y, 1), "core": 1 - c},
        "down_twin": {"y": step(y, 3), "core": 1 - c},
        "across_twin": {"y": step(y, 2), "core": 1 - c},
        "x+": at_x(step(x, 1)),
        "x-": at_x(step(x, 3)),
        "z+": {"z": step(z, 1)},
        "z-": {"z": step(z, 3)},
        "pair": {"xl": 1 - lax.axis_index("xl")},
    }
    return y, c, x, z, devices


def add_low(a, b):
    return (a.astype(F32) + b.astype(F32)).astype(BF)


def ring_gather(block, cut, i, plus, minus, sems, base, pending):
    before, after = lax.rem(i + 3, 4), lax.rem(i + 1, 4)
    to_plus = remote(block(i), block(i), sems, base, plus)
    to_minus = remote(block(i), block(i), sems, base + 1, minus)
    to_plus.start()
    to_minus.start()
    yield
    to_plus.wait_recv()
    lo = cut(block(before))[0]
    pass_plus = remote(lo, lo, sems, base + 2, plus)
    pass_plus.start()
    yield
    to_minus.wait_recv()
    hi = cut(block(after))[1]
    pass_minus = remote(hi, hi, sems, base + 3, minus)
    pass_minus.start()
    pending += [to_plus, to_minus, pass_plus, pass_minus]
    yield
    pass_plus.wait_recv()
    pass_minus.wait_recv()


def ring_scatter(block, cut, i, plus, minus, acc, near, sems, base, pending):
    before, after, across = lax.rem(i + 3, 4), lax.rem(i + 1, 4), lax.rem(i + 2, 4)
    lo, hi = (lambda v: cut(v)[0]), (lambda v: cut(v)[1])
    far_plus = remote(lo(block(across)), lo(near.at[0]), sems, base, plus)
    far_minus = remote(hi(block(across)), hi(near.at[0]), sems, base + 1, minus)
    own_plus = remote(hi(block(after)), hi(near.at[1]), sems, base + 2, plus)
    own_minus = remote(lo(block(before)), lo(near.at[2]), sems, base + 3, minus)
    for copy in (far_plus, far_minus, own_plus, own_minus):
        copy.start()
    yield
    far_plus.wait_recv()
    lo(acc)[...] = add_low(lo(block(after))[...], lo(near.at[0])[...])
    sum_plus = remote(lo(acc), lo(near.at[1]), sems, base + 4, plus)
    sum_plus.start()
    yield
    far_minus.wait_recv()
    hi(acc)[...] = add_low(hi(block(before))[...], hi(near.at[0])[...])
    sum_minus = remote(hi(acc), hi(near.at[2]), sems, base + 5, minus)
    sum_minus.start()
    pending += [far_plus, far_minus, own_plus, own_minus, sum_plus, sum_minus]
    yield
    for copy in (own_plus, own_minus, sum_plus, sum_minus):
        copy.wait_recv()


class GatherTokens:
    peers = ("twin", "up", "down")
    n_sems = 10

    def __init__(self, rows, width, normalize=False):
        self.ins = [((rows, width), BF)]
        self.outs = [((8, rows, width), BF)]
        self.scratch = [pltpu.VMEM((rows, width), BF)] if normalize else []
        self.rows = rows

    def run(self, ins, outs, scratch, sems, base, place, pending):
        y, c, _, _, to = place
        (x_ref,), (out_ref,) = ins, outs
        if scratch:
            rows = x_ref[...].astype(F32)
            centred = rows - jnp.mean(rows, axis=-1, keepdims=True)
            spread = jnp.mean(centred * centred, axis=-1, keepdims=True)
            (x_ref,) = scratch
            x_ref[...] = (centred * lax.rsqrt(spread + NORM_EPS)).astype(BF)
            yield
        half = self.rows // 2
        lo, hi = pl.ds(0, half), pl.ds(half, half)
        at = lambda k: lax.rem(y + k, 4) * 2 + c
        mine = pltpu.make_async_copy(x_ref, out_ref.at[at(0)], sems.at[0, base + 9])
        s_up = remote(x_ref, out_ref.at[at(0)], sems, base, to["up"])
        s_down = remote(x_ref, out_ref.at[at(0)], sems, base + 1, to["down"])
        s_twin = remote(x_ref, out_ref.at[at(0)], sems, base + 2, to["twin"])
        for copy in (s_up, s_down, s_twin, mine):
            copy.start()
        pass_on = lambda ref, k, device: remote(ref, ref, sems, base + k, to[device])
        yield
        s_up.wait_recv()
        r_up = pass_on(out_ref.at[at(3), lo], 3, "up")
        t_down = pass_on(out_ref.at[at(3)], 5, "twin")
        r_up.start()
        t_down.start()
        yield
        s_down.wait_recv()
        r_down = pass_on(out_ref.at[at(1), hi], 4, "down")
        t_up = pass_on(out_ref.at[at(1)], 6, "twin")
        r_down.start()
        t_up.start()
        yield
        r_up.wait_recv()
        t_lo = pass_on(out_ref.at[at(2), lo], 7, "twin")
        t_lo.start()
        yield
        r_down.wait_recv()
        t_hi = pass_on(out_ref.at[at(2), hi], 8, "twin")
        t_hi.start()
        pending += [s_up, s_down, s_twin, r_up, r_down, t_down, t_up, t_lo, t_hi]
        yield
        for copy in (s_twin, t_down, t_up, t_lo, t_hi):
            copy.wait_recv()
        mine.wait()


class SumTokens:
    peers = ("twin", "up", "down")
    n_sems = 10

    def __init__(self, rows, width):
        self.ins = [((8, rows, width), BF)]
        self.outs = [((rows, width), F32)]
        self.scratch = [
            pltpu.VMEM((4, rows, width), BF),
            pltpu.VMEM((3, rows, width), BF),
            pltpu.VMEM((rows, width), BF),
            pltpu.VMEM((3, rows, width), BF),
        ]
        self.rows = rows

    def run(self, ins, outs, scratch, sems, base, place, pending):
        y, c, _, _, to = place
        (p_ref,), (out_ref,) = ins, outs
        from_twin, pair, acc, near = scratch
        half = self.rows // 2
        cut = lambda v: (v.at[pl.ds(0, half)], v.at[pl.ds(half, half)])
        swaps = []
        for k, off in enumerate((2, 1, 3, 0)):
            at = lax.rem(y + off, 4) * 2
            copy = remote(p_ref.at[at + 1 - c], from_twin.at[k], sems, base + k, to["twin"])
            copy.start()
            swaps.append(copy)
        yield
        for k, off in enumerate((2, 1, 3)):
            swaps[k].wait_recv()
            pair[k] = add_low(p_ref[lax.rem(y + off, 4) * 2 + c], from_twin[k])
            if k == 0:
                far_plus = remote(
                    cut(pair.at[0])[0], cut(near.at[0])[0], sems, base + 4, to["up"]
                )
                far_minus = remote(
                    cut(pair.at[0])[1], cut(near.at[0])[1], sems, base + 5, to["down"]
                )
                far_plus.start()
                far_minus.start()
            elif k == 1:
                own_plus = remote(
                    cut(pair.at[1])[1], cut(near.at[1])[1], sems, base + 6, to["up"]
                )
                own_plus.start()
            else:
                own_minus = remote(
                    cut(pair.at[2])[0], cut(near.at[2])[0], sems, base + 7, to["down"]
                )
                own_minus.start()
        yield
        far_plus.wait_recv()
        cut(acc)[0][...] = add_low(cut(pair.at[1])[0][...], cut(near.at[0])[0][...])
        sum_plus = remote(cut(acc)[0], cut(near.at[1])[0], sems, base + 8, to["up"])
        sum_plus.start()
        yield
        far_minus.wait_recv()
        cut(acc)[1][...] = add_low(cut(pair.at[2])[1][...], cut(near.at[0])[1][...])
        sum_minus = remote(cut(acc)[1], cut(near.at[2])[1], sems, base + 9, to["down"])
        sum_minus.start()
        swaps[3].wait_recv()
        out_ref[...] = p_ref[y * 2 + c].astype(F32) + from_twin[3].astype(F32)
        pending += swaps + [far_plus, far_minus, own_plus, own_minus, sum_plus, sum_minus]
        yield
        for copy in (own_plus, own_minus, sum_plus, sum_minus):
            copy.wait_recv()
        out_ref[...] += near[1].astype(F32) + near[2].astype(F32)


def rows_or_columns(rows, width):
    if rows % 32 == 0:
        return lambda v: (v.at[pl.ds(0, rows // 2)], v.at[pl.ds(rows // 2, rows // 2)])
    return lambda v: (v.at[:, pl.ds(0, width // 2)], v.at[:, pl.ds(width // 2, width // 2)])


def firsts(v):
    return v.at[pl.ds(0, 2)], v.at[pl.ds(2, 2)]


class GatherWeights:
    peers = ("x+", "x-", "z+", "z-")
    n_sems = 17

    def __init__(self, rows, width):
        self.ins = [((rows, width), BF)]
        self.outs = [((4, 4, rows, width), BF)]
        self.scratch = []
        self.rows, self.width = rows, width

    def rings(self, out_ref, sems, base, place, pending):
        _, _, x, z, to = place
        first = self.width // 256 * 128
        a, b = pl.ds(0, first), pl.ds(first, self.width - first)
        every = pl.ds(0, self.rows)
        cut_a = rows_or_columns(self.rows, first)
        cut_b = rows_or_columns(self.rows, self.width - first)

        def along_x_first():
            yield from ring_gather(
                lambda j: out_ref.at[z, j, every, a], cut_a, x, to["x+"], to["x-"], sems, base, pending
            )
            yield from ring_gather(
                lambda j: out_ref.at[j, pl.ds(0, 4), every, a], firsts, z, to["z+"], to["z-"], sems, base + 4,
                pending,
            )

        def along_z_first():
            yield from ring_gather(
                lambda j: out_ref.at[j, x, every, b], cut_b, z, to["z+"], to["z-"], sems, base + 8, pending
            )
            yield from ring_gather(
                lambda j: out_ref.at[pl.ds(0, 4), j, every, b], firsts, x, to["x+"], to["x-"], sems,
                base + 12, pending,
            )

        yield from both(along_x_first(), along_z_first())

    def run(self, ins, outs, scratch, sems, base, place, pending):
        _, _, x, z, _ = place
        (x_ref,), (out_ref,) = ins, outs
        mine = pltpu.make_async_copy(x_ref, out_ref.at[z, x], sems.at[0, base + 16])
        mine.start()
        mine.wait()
        yield from self.rings(out_ref, sems, base, place, pending)


class SumWeights:
    peers = ("x+", "x-", "z+", "z-")
    n_sems = 24

    def __init__(self, rows, width):
        self.ins = [((4, 4, rows, width), BF)]
        self.outs = [((rows, width), BF)]
        self.rows, self.width = rows, width
        first = width // 256 * 128
        self.widths = (first, width - first)
        self.scratch = []
        for w in self.widths:
            self.scratch += [
                pltpu.VMEM((4, rows, w), BF),
                pltpu.VMEM((3, 4, rows, w), BF),
                pltpu.VMEM((4, rows, w), BF),
                pltpu.VMEM((rows, w), BF),
                pltpu.VMEM((3, rows, w), BF),
            ]

    def run(self, ins, outs, scratch, sems, base, place, pending):
        _, _, x, z, to = place
        (p_ref,), (out_ref,) = ins, outs
        every = pl.ds(0, self.rows)

        def one(order, bufs, base):
            acc, near, total, acc_two, near_two = bufs
            width = self.widths[order]
            columns = pl.ds(order * self.widths[0], width)
            cut = rows_or_columns(self.rows, width)
            four = pl.ds(0, 4)
            if order == 0:
                block = lambda j: p_ref.at[four, j, every, columns]
                i, k, far, close = x, z, ("x+", "x-"), ("z+", "z-")
            else:
                block = lambda j: p_ref.at[j, four, every, columns]
                i, k, far, close = z, x, ("z+", "z-"), ("x+", "x-")
            yield from ring_scatter(
                block, firsts, i, to[far[0]], to[far[1]], acc, near, sems, base, pending
            )
            total[...] = (
                block(i)[...].astype(F32) + near[1].astype(F32) + near[2].astype(F32)
            ).astype(BF)
            yield from ring_scatter(
                lambda j: total.at[j], cut, k, to[close[0]], to[close[1]], acc_two, near_two, sems,
                base + 6, pending,
            )
            out_ref[every, columns] = (
                total[k].astype(F32) + near_two[1].astype(F32) + near_two[2].astype(F32)
            ).astype(BF)

        yield from both(one(0, scratch[:5], base), one(1, scratch[5:], base + 12))


class Swap:
    peers = ("twin", "up", "down", "across", "up_twin", "down_twin", "across_twin")
    n_sems = 8
    steps = ((0, 1), (1, 0), (3, 0), (2, 0), (1, 1), (3, 1), (2, 1))

    def __init__(self, rows, width):
        self.ins = [((8, rows, width), BF)]
        self.outs = [((8, rows, width), BF)]
        self.scratch = []

    def send(self, x_ref, out_ref, sems, base, place):
        y, c, _, _, to = place
        me = y * 2 + c
        copies = [pltpu.make_async_copy(x_ref.at[me], out_ref.at[me], sems.at[0, base + 7])]
        for k, (name, (up, other)) in enumerate(zip(self.peers, self.steps)):
            at = lax.rem(y + up, 4) * 2 + (1 - c if other else c)
            copies.append(remote(x_ref.at[at], out_ref.at[me], sems, base + k, to[name]))
        for copy in copies:
            copy.start()
        return copies

    def run(self, ins, outs, scratch, sems, base, place, pending):
        copies = self.send(ins[0], outs[0], sems, base, place)
        yield
        copies[0].wait()
        for copy in copies[1:]:
            copy.wait_recv()
        pending += copies[1:]


def columns(at, width):
    return slice(at, at + width)


class ShareQkv:
    peers = Swap.peers + GatherWeights.peers

    def __init__(self):
        self.swap = Swap(16, 896)
        self.gather = GatherWeights(128, 896)
        self.ins = [((16, 6144), F32), ((16, 128), BF)]
        self.outs = self.gather.outs + [((16, 16 * 128), F32)]
        self.scratch = [pltpu.VMEM((8, 16, 896), BF)] * 2
        self.n_sems = 16 + self.gather.n_sems

    def run(self, ins, outs, scratch, sems, base, place, pending):
        _, _, x, z, _ = place
        weight_ref, tile_ref = ins
        (out_ref, tiles_ref), (piece, landed) = outs, scratch
        for k in range(8):
            for pair in range(2):
                for kind in range(3):
                    piece[k, :, columns(pair * 384 + kind * 128, 128)] = weight_ref[
                        :, columns(kind * D + k * 256 + pair * 128, 128)
                    ].astype(BF)
            piece[k, :, columns(768, 128)] = tile_ref[...]
        yield from self.swap.run((piece,), (landed,), (), sems, base, place, pending)
        for k in range(8):
            out_ref[z, x, columns(k * 16, 16)] = landed[k]
        yield from self.gather.rings(out_ref, sems, base + 16, place, pending)
        for k in range(16):
            tiles = [
                out_ref[k // 4, k % 4, columns(j * 16, 16), columns(768, 128)].astype(F32)
                for j in range(8)
            ]
            tiles_ref[:, columns(k * 128, 128)] = sum(tiles[1:], tiles[0])


def moved(read, tile, pieces, last):
    lane = lax.broadcasted_iota(jnp.int32, (16, 128), 1)
    value = jnp.zeros((16, 128), F32)
    for there, source, here, width in pieces:
        at = there - tile * 128
        if at + width <= 0 or at >= 128:
            continue
        start = min(here // 128 * 128, last)
        window = read(source, columns(start, 256)).astype(F32)
        shift = (at - (here - start)) % 256
        window = (pltpu.roll(window, shift, 1) if shift else window)[:, 0:128]
        value = jnp.where((lane >= at) & (lane < at + width), window, value)
    return value


class ShareHidden:
    peers = Swap.peers

    def __init__(self):
        self.swap = Swap(16, 1536)
        self.ins = [((16, FF), F32)] * 2
        self.outs = self.swap.outs
        self.scratch = [pltpu.VMEM((8, 16, 1536), BF)]
        self.n_sems = self.swap.n_sems

    def run(self, ins, outs, scratch, sems, base, place, pending):
        (piece,) = scratch
        for k in range(8):
            pieces = [(j * 48, None, (j * 8 + k) * 44, 44) for j in range(16)]
            for w, ref in enumerate(ins):
                for tile in range(6):
                    value = moved(lambda _, at: ref[:, at], tile, pieces, FF - 256)
                    piece[k, :, columns(w * 768 + tile * 128, 128)] = value.astype(BF)
            yield
        yield from self.swap.run((piece,), outs, (), sems, base, place, pending)


class TokenSums:
    peers = ()
    n_sems = 0

    def __init__(self, rows, width, count, step=256):
        self.ins = [((HALF, rows), BF)] + [((HALF, width), BF)] * count
        self.outs = [((rows, width), BF)] * count
        self.scratch = []
        self.steps = [pl.ds(k, step) for k in range(0, rows, step)]

    def run(self, ins, outs, scratch, sems, base, place, pending):
        for columns in self.steps:
            for b_ref, out_ref in zip(ins[1:], outs):
                out_ref[columns, :] = dot_tn(ins[0][:, columns], b_ref[...]).astype(BF)
            yield


class GradThenSum:
    peers = SumWeights.peers

    def __init__(self, rows, width, steps):
        self.sum = SumWeights(rows // 16, width)
        self.ins = [((HALF, rows), BF), ((HALF, width), BF)]
        self.outs = self.sum.outs
        self.scratch = [pltpu.VMEM((4, 4, rows // 16, width), BF)] + self.sum.scratch
        self.n_sems = self.sum.n_sems
        self.rows, self.steps = rows, steps

    def run(self, ins, outs, scratch, sems, base, place, pending):
        terms = scratch[0]
        block, step = self.rows // 16, self.rows // self.steps
        for k in range(self.steps):
            part = dot_tn(ins[0][:, columns(k * step, step)], ins[1][...]).astype(BF)
            for j in range(step // block):
                at = k * step // block + j
                terms[at // 4, at % 4] = part[columns(j * block, block)]
            yield
        yield from self.sum.run((terms,), outs, scratch[1:], sems, base, place, pending)


class Product:
    peers = ()
    n_sems = 0

    def __init__(self, depth, width):
        self.ins = [((HALF, depth), BF), ((depth, width), BF)]
        self.outs = [((HALF, width), BF)]
        self.scratch = []

    def run(self, ins, outs, scratch, sems, base, place, pending):
        for k in range(0, HALF, 256):
            outs[0][pl.ds(k, 256), :] = dot_nn(ins[0][pl.ds(k, 256), :], ins[1][...]).astype(BF)
            yield


class SwapThenSum:
    peers = Swap.peers + SumWeights.peers

    def __init__(self, rows, width):
        self.swap = Swap(rows, width)
        self.sum = SumWeights(rows, width)
        self.ins = self.swap.ins
        self.outs = self.sum.outs
        self.scratch = [
            pltpu.VMEM((8, rows, width), BF),
            pltpu.VMEM((4, 4, rows, width), BF),
        ] + self.sum.scratch
        self.n_sems = 8 + self.sum.n_sems

    def run(self, ins, outs, scratch, sems, base, place, pending):
        landed, spread = scratch[:2]
        yield from self.swap.run(ins, (landed,), (), sems, base, place, pending)
        total = jnp.sum(landed[...].astype(F32), axis=0).astype(BF)
        spread[...] = jnp.broadcast_to(total[None, None], spread.shape)
        yield from self.sum.run((spread,), outs, scratch[2:], sems, base + 8, place, pending)


def both(*parts):
    parts = list(parts)
    while parts:
        for part in list(parts):
            try:
                next(part)
            except StopIteration:
                parts.remove(part)
        yield


def in_order(parts, order):
    for letter in order:
        next(parts["abcdef".index(letter)], None)
    for _ in both(*parts):
        pass


def size(shape, dtype):
    return math.prod(shape) * jnp.dtype(dtype).itemsize


def comm_kernel(parts, order, *refs):
    sems = refs[-1]
    n_in = sum(len(p.ins) for p in parts)
    n_out = sum(len(p.outs) for p in parts)
    ins, outs, scratch = list(refs[:n_in]), list(refs[n_in : n_in + n_out]), list(refs[n_in + n_out : -1])
    place = places()
    names = []
    for p in parts:
        names += [n for n in p.peers if n not in names]
    barrier = pltpu.get_barrier_semaphore()
    for name in names:
        pl.semaphore_signal(
            barrier, inc=1, device_id=place[4][name], device_id_type=pl.DeviceIdType.MESH
        )
    pl.semaphore_wait(barrier, len(names))
    base, running, pending = 0, [], []
    for p in parts:
        taken = []
        for refs_of, count in ((ins, len(p.ins)), (outs, len(p.outs)), (scratch, len(p.scratch))):
            taken.append([refs_of.pop(0) for _ in range(count)])
        p.held = taken[1]
        running.append(p.run(*taken, sems, base, place, pending))
        base += p.n_sems
    in_order(running, order)
    for copy in pending:
        copy.wait_send()


def comm(collective_id, order, *pairs):
    parts = [p for p, _ in pairs]
    operands = [x.reshape(spec[0]) for p, xs in pairs for x, spec in zip(xs, p.ins)]
    spaces = [spec[2] if len(spec) > 2 else pltpu.VMEM for p in parts for spec in p.ins]
    outs = [o for p in parts for o in p.outs]
    held = sum(size(*spec[:2]) for p in parts for spec in p.ins + p.outs)
    held += sum(size(s.shape, s.dtype) for p in parts for s in p.scratch)
    sent = sum(math.prod(shape) for shape, _ in outs) * 2
    return pl.pallas_call(
        functools.partial(comm_kernel, parts, order),
        out_shape=[jax.ShapeDtypeStruct(*o) for o in outs],
        in_specs=[pl.BlockSpec(memory_space=space) for space in spaces],
        out_specs=[pl.BlockSpec(memory_space=pltpu.VMEM)] * len(outs),
        scratch_shapes=[s for p in parts for s in p.scratch]
        + [pltpu.SemaphoreType.DMA((2, sum(p.n_sems for p in parts)))],
        compiler_params=pltpu.CompilerParams(
            collective_id=collective_id, has_side_effects=True, vmem_limit_bytes=held + (8 << 20)
        ),
        cost_estimate=pl.CostEstimate(flops=0, bytes_accessed=20 * sent, transcendentals=0),
    )(*operands)


ROWS = 256


class MakeQkv:
    peers = ()
    n_sems = 0

    def __init__(self, weights, units):
        self.weights, self.units = weights, units
        self.ins = []
        self.outs = [((HALF, D), BF), ((HALF, 768), BF), ((2, 32, HALF), BF)]
        self.scratch = []

    def run(self, ins, outs, scratch, sems, base, place, pending):
        h_ref, out_ref, angles_ref = outs
        w_ref, params_ref = self.weights.held
        (u_ref,) = self.units.held
        yc = place[0] * 2 + place[1]
        xl = lax.axis_index("xl")
        for half in range(2):
            angles_ref[half] = rotary_angles(params_ref, half)
        weight = w_ref[:, :, :, 0:768].reshape(D, 768)
        for k in range(4):
            rows = columns(k * ROWS, ROWS)
            unit = u_ref[2 * k : 2 * k + 2].reshape(ROWS, D).astype(F32)
            h = (unit * params_ref[0:1] + params_ref[1:2]).astype(BF)
            h_ref[rows, :] = h
            mixed = dot_nn(h, weight)
            tables = rotary_tables(angles_ref[xl, :, rows])
            for j in range(6):
                pair, kind = j // 3, j % 3
                at = pl.ds(pl.multiple_of(yc * 256 + pair * 128, 128), 128)
                part = mixed[:, columns(j * 128, 128)] + params_ref[2 + kind : 3 + kind, at]
                if kind < 2:
                    part = rotate(part, *tables)
                out_ref[rows, columns(j * 128, 128)] = part.astype(BF)
        yield


def rowwise(width):
    return pl.BlockSpec((ROWS, width), lambda i: (i, 0))


def fixed(*shape):
    return pl.BlockSpec(shape, lambda i: (0,) * len(shape), pipeline_mode=pl.Buffered(1))


BLOCK = 512
Q, K, V = slice(0, 128), slice(128, 256), slice(256, 384)


def only(x, h):
    lane = lax.broadcasted_iota(jnp.int32, (1, 128), 1)
    return jnp.where((lane >= h * HEAD) & (lane < (h + 1) * HEAD), x, jnp.zeros_like(x))


def rows_of(k):
    return slice(k * BLOCK, (k + 1) * BLOCK)


def allowed_mask(first_len, key_half, kb, query_half, qb, diagonal):
    key = lax.broadcasted_iota(jnp.int32, (BLOCK, BLOCK), 0) + kb * BLOCK
    query = lax.broadcasted_iota(jnp.int32, (BLOCK, BLOCK), 1) + qb * BLOCK
    allowed = None
    if diagonal and kb == qb:
        allowed = key <= query
    if kb == 0:
        length = first_len.astype(jnp.int32)
        same = (key + key_half * HALF >= length) | (query + query_half * HALF < length)
        allowed = same if allowed is None else allowed & same
    return allowed


def lanes(at, width):
    return pl.ds(pl.multiple_of(at * width, 128), width)


class Attend:
    peers = ("pair",)
    n_sems = 6

    def __init__(self):
        self.ins = [((16, D), F32), ((HALF, 768), BF)]
        self.outs = [
            ((HALF, 256), BF),
            ((2, 128, HALF), F32),
            ((2, 8, HALF), F32),
            ((2, HALF, 384), BF),
        ]
        self.scratch = [pltpu.VMEM((2, 8, HALF), F32), pltpu.VMEM((2, HALF, 128), BF)]

    def run(self, ins, outs, scratch, sems, base, place, pending):
        params_ref, qkv_ref = ins
        o_ref, acc_ref, top_ref, x_ref = outs
        total_ref, half_ref = scratch
        pair = place[4]["pair"]
        xl = lax.axis_index("xl")
        first_len = document_marks(params_ref)[0]
        sent = []
        for b in range(2):
            copy = remote(
                qkv_ref.at[rows_of(b), lanes(1 - xl, 384)], x_ref.at[xl, rows_of(b)], sems, base + b, pair
            )
            copy.start()
            sent.append(copy)
        kept = pltpu.make_async_copy(qkv_ref.at[:, lanes(xl, 384)], x_ref.at[xl], sems.at[0, base + 2])
        kept.start()
        kept.wait()
        yield

        def block(query_half, key_half, qb, h, state, diagonal):
            qs = rows_of(qb)
            qh = only(x_ref[query_half, qs, Q] * jnp.asarray(HEAD**-0.5, BF), h)
            top, total, acc = state
            for kb in range(qb + 1 if diagonal else 2):
                ks = rows_of(kb)
                scores = dot_nt(x_ref[key_half, ks, K], qh)
                allowed = allowed_mask(first_len, key_half, kb, query_half, qb, diagonal)
                if allowed is not None:
                    scores = jnp.where(allowed, scores, MASKED)
                new_top = jnp.maximum(top, jnp.max(scores, axis=0, keepdims=True))
                weights = jnp.exp(scores - new_top)
                if allowed is not None:
                    weights = jnp.where(allowed, weights, 0.0)
                shrink = jnp.exp(top - new_top)
                total = total * shrink + jnp.sum(weights, axis=0, keepdims=True)
                part = dot_tn(only(x_ref[key_half, ks, V], h), weights.astype(BF))
                acc = acc * shrink + part[h * HEAD : (h + 1) * HEAD]
                top = new_top
            top_ref[query_half, h : h + 1, qs] = top
            total_ref[query_half, h : h + 1, qs] = total
            acc_ref[query_half, h * HEAD : (h + 1) * HEAD, qs] = acc

        def diagonal(half):
            for qb in range(2):
                for h in range(2):
                    start = (
                        jnp.full((1, BLOCK), MASKED, F32),
                        jnp.zeros((1, BLOCK), F32),
                        jnp.zeros((HEAD, BLOCK), F32),
                    )
                    block(half, half, qb, h, start, True)

        def finish(half):
            for qb in range(2):
                qs = rows_of(qb)
                for h in range(2):
                    hs = slice(h * HEAD, (h + 1) * HEAD)
                    total = total_ref[half, h : h + 1, qs]
                    acc_ref[half, hs, qs] = acc_ref[half, hs, qs] / total
                    top_ref[half, h : h + 1, qs] = top_ref[half, h : h + 1, qs] + jnp.log(total)
                half_ref[half, qs, :] = acc_ref[half, :, qs].T.astype(BF)

        diagonal(xl)
        yield
        for copy in sent:
            copy.wait_recv()
        diagonal(1 - xl)
        yield
        for qb in range(2):
            for h in range(2):
                qs = rows_of(qb)
                state = (
                    top_ref[1, h : h + 1, qs],
                    total_ref[1, h : h + 1, qs],
                    acc_ref[1, h * HEAD : (h + 1) * HEAD, qs],
                )
                block(1, 0, qb, h, state, False)
            yield
        finish(1 - xl)
        back = remote(half_ref.at[1 - xl], o_ref.at[:, lanes(xl, 128)], sems, base + 3, pair)
        back.start()
        finish(xl)
        mine = pltpu.make_async_copy(half_ref.at[xl], o_ref.at[:, lanes(xl, 128)], sems.at[0, base + 4])
        mine.start()
        pending += sent + [back]
        yield
        mine.wait()
        back.wait_recv()


class AttendBack:
    peers = ("pair",)
    n_sems = 6

    def __init__(self):
        self.ins = [
            ((16, D), F32),
            ((2, HALF, 384), BF),
            ((HALF, 256), BF),
            ((2, 128, HALF), F32),
            ((2, 8, HALF), F32),
            ((2, 32, HALF), BF),
        ]
        self.outs = [((HALF, 768), BF)]
        self.scratch = [
            pltpu.VMEM((2, HALF, 128), BF),
            pltpu.VMEM((2, 128, HALF), F32),
            pltpu.VMEM((2, HALF, 128), F32),
            pltpu.VMEM((2, HALF, 128), F32),
            pltpu.VMEM((2, HALF, 384), BF),
        ]

    def run(self, ins, outs, scratch, sems, base, place, pending):
        params_ref, x_ref, own_ref, ot_ref, lse_ref, angles_ref = ins
        (out_ref,) = outs
        do_ref, dqt_ref, dk_ref, dv_ref, half_ref = scratch
        pair = place[4]["pair"]
        xl = lax.axis_index("xl")
        first_len = document_marks(params_ref)[0]
        sent = remote(own_ref.at[:, lanes(1 - xl, 128)], do_ref.at[xl], sems, base, pair)
        sent.start()
        kept = pltpu.make_async_copy(own_ref.at[:, lanes(xl, 128)], do_ref.at[xl], sems.at[0, base + 1])
        kept.start()
        kept.wait()
        yield

        def block(query_half, key_half, qb, h, diagonal):
            qs = rows_of(qb)
            hs = slice(h * HEAD, (h + 1) * HEAD)
            do = do_ref[query_half, qs, :]
            qh = only(x_ref[query_half, qs, Q] * jnp.asarray(HEAD**-0.5, BF), h)
            doh = only(do, h)
            delta = jnp.sum(
                doh.astype(F32).T[hs] * ot_ref[query_half, hs, qs], axis=0, keepdims=True
            )
            lse = lse_ref[query_half, h : h + 1, qs]
            for kb in range(qb + 1 if diagonal else 2):
                ks = rows_of(kb)
                k = x_ref[key_half, ks, K]
                scores = dot_nt(k, qh)
                probs = jnp.exp(scores - lse)
                allowed = allowed_mask(first_len, key_half, kb, query_half, qb, diagonal)
                if allowed is not None:
                    probs = jnp.where(allowed, probs, 0.0)
                pulled = dot_nt(x_ref[key_half, ks, V], doh)
                ds = (probs * (pulled - delta)).astype(BF)
                dv = dot_nn(probs.astype(BF), doh)
                dk = dot_nn(ds, qh)
                dq = dot_tn(only(k, h), ds)[hs]
                if diagonal and h == 0 and qb == kb:
                    dv_ref[key_half, ks, :] = dv
                    dk_ref[key_half, ks, :] = dk
                else:
                    dv_ref[key_half, ks, :] += dv
                    dk_ref[key_half, ks, :] += dk
                if diagonal and kb == 0:
                    dqt_ref[query_half, hs, qs] = dq
                else:
                    dqt_ref[query_half, hs, qs] += dq

        def finish(half):
            for b in range(2):
                bs = rows_of(b)
                cosine, below, above = rotary_tables(angles_ref[half, :, bs])
                dq = dqt_ref[half, :, bs].T * HEAD**-0.5
                half_ref[half, bs, Q] = rotate(dq, cosine, -below, -above).astype(BF)
                half_ref[half, bs, K] = rotate(dk_ref[half, bs, :], cosine, -below, -above).astype(BF)
                half_ref[half, bs, V] = dv_ref[half, bs, :].astype(BF)

        for qb in range(2):
            for h in range(2):
                block(xl, xl, qb, h, True)
        yield
        sent.wait_recv()
        for qb in range(2):
            for h in range(2):
                block(1 - xl, 1 - xl, qb, h, True)
        yield
        for qb in range(2):
            for h in range(2):
                block(1, 0, qb, h, False)
            yield
        finish(1 - xl)
        back = remote(half_ref.at[1 - xl], out_ref.at[:, lanes(xl, 384)], sems, base + 2, pair)
        back.start()
        finish(xl)
        mine = pltpu.make_async_copy(half_ref.at[xl], out_ref.at[:, lanes(xl, 384)], sems.at[0, base + 3])
        mine.start()
        pending += [sent, back]
        yield
        mine.wait()
        back.wait_recv()


def feed_kernel(h_ref, dy_ref, gate_ref, up_ref, down_ref, hid_ref, dg_ref, du_ref, dh_ref):
    gate, up = dot_nn(h_ref[...], gate_ref[...]), dot_nn(h_ref[...], up_ref[...])
    sigmoid = jax.nn.sigmoid(gate)
    activated = gate * sigmoid
    hidden = (activated * up).astype(BF)
    hid_ref[...] = hidden
    d_hidden = dot_nt(dy_ref[...], down_ref[...])
    d_gate = (d_hidden * up * sigmoid * (1.0 + gate * (1.0 - sigmoid))).astype(BF)
    d_up = (d_hidden * activated).astype(BF)
    dg_ref[...] = d_gate
    du_ref[...] = d_up
    dh_ref[...] = (dot_nt(d_gate, gate_ref[...]) + dot_nt(d_up, up_ref[...])).astype(BF)


def feed_call(h, dy, w_gate, w_up, w_down):
    return pl.pallas_call(
        feed_kernel,
        out_shape=(
            jax.ShapeDtypeStruct((HALF, 768), BF),
            jax.ShapeDtypeStruct((HALF, 768), BF),
            jax.ShapeDtypeStruct((HALF, 768), BF),
            jax.ShapeDtypeStruct((HALF, D), BF),
        ),
        grid=(HALF // ROWS,),
        in_specs=[rowwise(D), rowwise(D), fixed(D, 768), fixed(D, 768), fixed(768, D)],
        out_specs=(rowwise(768), rowwise(768), rowwise(768), rowwise(D)),
        compiler_params=pltpu.CompilerParams(vmem_limit_bytes=34 << 20),
        cost_estimate=pl.CostEstimate(
            flops=5 * 2 * HALF * D * 768, bytes_accessed=26 << 20, transcendentals=HALF * 768
        ),
    )(h, dy, w_gate, w_up, w_down)


def last_kernel(dx_ref, u_ref, w_ref, dh_ref, sums_ref, bias_ref):
    dh = dot_nt(dx_ref[...], w_ref[:, 0:768])
    dh_ref[...] = dh.astype(BF)

    @pl.when(pl.program_id(0) == 0)
    def _():
        sums_ref[...] = jnp.zeros_like(sums_ref)
        bias_ref[...] = jnp.zeros_like(bias_ref)

    sums_ref[0:1] += jnp.sum(dh * u_ref[...].astype(F32), axis=0, keepdims=True)
    sums_ref[1:2] += jnp.sum(dh, axis=0, keepdims=True)
    bias_ref[0:1] += jnp.sum(dx_ref[...].astype(F32), axis=0, keepdims=True)


def last_call(dx, u, w):
    return pl.pallas_call(
        last_kernel,
        out_shape=(
            jax.ShapeDtypeStruct((HALF, D), BF),
            jax.ShapeDtypeStruct((8, D), F32),
            jax.ShapeDtypeStruct((8, 768), F32),
        ),
        grid=(HALF // ROWS,),
        in_specs=[rowwise(768), rowwise(D), fixed(D, 896)],
        out_specs=(rowwise(D), fixed(8, D), fixed(8, 768)),
        compiler_params=pltpu.CompilerParams(vmem_limit_bytes=24 << 20),
        cost_estimate=pl.CostEstimate(
            flops=2 * HALF * D * 768, bytes_accessed=14 << 20, transcendentals=0
        ),
    )(dx, u, w)


def wide_update_kernel(qkv_ref, gate_ref, up_ref, *refs):
    ins, outs = refs[:9], refs[9:]

    def update(k, at, gradient):
        new = adamw(*[ref[:, at] for ref in ins[k * 3 : k * 3 + 3]], gradient, D ** (-0.5), 0.1)
        for ref, value in zip(outs[k * 3 : k * 3 + 3], new):
            ref[:, at] = value

    for k in range(8):
        for pair in range(2):
            for kind in range(3):
                update(
                    0,
                    columns(kind * D + k * 256 + pair * 128, 128),
                    qkv_ref[k, :, columns(pair * 384 + kind * 128, 128)].astype(F32),
                )
    pieces = [(o * 44, o % 8, o // 8 * 48, 44) for o in range(128)]
    for w, grad_ref in enumerate((gate_ref, up_ref)):
        for tile in range(FF // 128):
            value = moved(lambda k, at: grad_ref[k, :, at], tile, pieces, 768 - 256)
            update(1 + w, columns(tile * 128, 128), value)


def wide_updates(grads, *states):
    operands = [x for state in states for x in state]
    return pl.pallas_call(
        wide_update_kernel,
        out_shape=[jax.ShapeDtypeStruct(x.shape, F32) for x in operands],
        in_specs=[pl.BlockSpec(memory_space=pltpu.VMEM)] * 12,
        out_specs=[pl.BlockSpec(memory_space=pltpu.VMEM)] * 9,
        compiler_params=pltpu.CompilerParams(vmem_limit_bytes=24 << 20),
        cost_estimate=pl.CostEstimate(flops=20 << 20, bytes_accessed=10 << 20, transcendentals=1 << 20),
    )(*grads, *operands)


TO_HEADS = [(f * 16 + ctx, ctx * 8 + f) for f in range(8) for ctx in range(16)]
TO_OWNER = [(b, a) for a, b in TO_HEADS]


def local(
    hidden_in, out_grad, positions, documents,
    qkv_weight, qkv_first, qkv_second,
    out_weight, out_first, out_second,
    gate_weight, gate_first, gate_second,
    up_weight, up_first, up_second,
    down_weight, down_first, down_second,
    small_params, small_first, small_second,
):
    xh, xl, z = lax.axis_index("xh"), lax.axis_index("xl"), lax.axis_index("z")
    yc = lax.axis_index("y") * 2 + lax.axis_index("core")
    place = (z * 2 + xh) * 2 + xl

    first_here = jnp.sum(1 - documents)
    start_here = positions[0, 0]
    marks = jnp.stack([first_here, start_here // 64, start_here % 64]).astype(BF)
    tile = jnp.concatenate(
        [small_params.astype(BF), jnp.pad(marks, (0, 13))[None]], axis=0
    )
    tile = jnp.where((jnp.arange(8) == yc)[None, :, None], tile[:, None, :], 0)
    tile = jnp.pad(tile.reshape(8, 128), ((0, 8), (0, 0)))
    outer = out_grad.reshape(128, D)
    out_rows = lax.ppermute(out_weight.astype(BF), AXES, TO_HEADS)
    share, units = ShareQkv(), GatherTokens(128, D, normalize=True)
    w_all, params, u_all, gu_mine, w_out, h1, qkv, angles = comm(
        0,
        "adbccdddccddabccdccaaacbbaabbaabce",
        (share, (qkv_weight, tile)),
        (units, (hidden_in,)),
        (ShareHidden(), (gate_weight, up_weight)),
        (GatherWeights(16, D), (out_rows,)),
        (MakeQkv(share, units), ()),
    )
    u_all, w_qkv, w_out = u_all.reshape(HALF, D), w_all.reshape(D, 896), w_out.reshape(256, D)
    gu_mine = gu_mine.reshape(128, 1536)
    o, attended_t, lse, heads, dy, w_gate = comm(
        1,
        "abcabbccacbbaaccabca",
        (Attend(), (params, qkv)),
        (GatherTokens(128, D), (outer,)),
        (GatherWeights(128, 768), (gu_mine[:, :768],)),
    )
    dy = dy.reshape(HALF, D)
    branch_part = dot_nn(o, w_out).astype(BF)
    branch, w_up = comm(
        2,
        "ababbbaabbab",
        (SumTokens(128, D), (branch_part,)),
        (GatherWeights(128, 768), (gu_mine[:, 768:],)),
    )
    rows = hidden_in.reshape(128, D).astype(F32)
    middle = rows + branch
    normed_two, unit_two, scale_two = norm_forward(middle, params[5], params[6])
    down_piece = jnp.pad(down_weight.astype(BF), ((0, 4), (0, 0)))
    h2, w_down = comm(
        3,
        "abbbbaabbaaab",
        (GatherTokens(128, D), (normed_two.astype(BF),)),
        (GatherWeights(48, D), (down_piece,)),
    )
    h2 = h2.reshape(HALF, D)
    w_down = w_down.reshape(768, D)
    hidden, d_gate_low, d_up_low, dh2_part = feed_call(
        h2, dy, w_gate.reshape(D, 768), w_up.reshape(D, 768), w_down
    )

    d_normed_two, g_down, d_gate, d_up = comm(
        4,
        "abbbaccbbaacccbccbbacb",
        (SumTokens(128, D), (dh2_part,)),
        (GradThenSum(768, D, 2), (hidden, dy)),
        (TokenSums(D, 768, 2), (h2, d_gate_low, d_up_low)),
    )
    d_middle_part, d_gain_two, d_shift_two = norm_backward(
        d_normed_two, unit_two, scale_two, params[5]
    )
    d_middle = outer.astype(F32) + d_middle_part
    dx2, g_gate, y_part = comm(
        5,
        "abcbbcaacbbbcaaab",
        (GatherTokens(128, D), (d_middle.astype(BF),)),
        (SumWeights(128, 768), (d_gate,)),
        (Product(768, D), (hidden, w_down)),
    )
    dx2 = dx2.reshape(HALF, D)
    do = dot_nt(dx2, w_out).astype(BF)
    d_qkv_low, branch_two, g_up, gate_back = comm(
        7,
        "abcdabaccaaabbcccdbca",
        (AttendBack(), (params, heads, do, attended_t, lse, angles)),
        (SumTokens(128, D), (y_part,)),
        (SumWeights(128, 768), (d_up,)),
        (Swap(16, 768), (g_gate,)),
    )
    block_out = (middle + branch_two).reshape(1, 128, D).astype(BF)
    d_out = dot_tn(o, dx2).astype(BF)
    dh1_part, sums, d_bias = last_call(d_qkv_low, u_all, w_qkv)
    d_bias = d_bias[0].reshape(2, 3, 128).transpose(1, 0, 2).reshape(3, 256)
    d_small = jnp.concatenate(
        [
            sums[0:2],
            lax.dynamic_update_slice_in_dim(jnp.zeros((3, D), F32), d_bias, yc * 256, axis=1),
            d_gain_two[None],
            d_shift_two[None],
            jnp.zeros((9, D), F32),
        ],
        axis=0,
    )
    small_piece = d_small.astype(BF).reshape(16, 16, 8, 16).transpose(2, 0, 1, 3).reshape(8, 16, 256)
    small_piece = jnp.pad(small_piece, ((0, 0), (0, 0), (0, 256)))
    d_normed, g_qkv, g_out, g_small, up_back = comm(
        6,
        "acdbbabbbccdaabbcdddebccddabbcdbe",
        (SumTokens(128, D), (dh1_part,)),
        (GradThenSum(D, 768, 4), (h1, d_qkv_low)),
        (SumWeights(16, D), (d_out,)),
        (SwapThenSum(16, 512), (small_piece,)),
        (Swap(16, 768), (g_up,)),
    )
    centred = rows - jnp.mean(rows, axis=-1, keepdims=True)
    scale_one = lax.rsqrt(jnp.mean(centred * centred, axis=-1, keepdims=True) + NORM_EPS)
    d_rows_part = norm_backward(d_normed, centred * scale_one, scale_one, params[0])[0]
    input_grad = (d_middle + d_rows_part).reshape(1, 128, D)

    g_out = lax.ppermute(g_out, AXES, TO_OWNER).astype(F32)
    (qkv_back,) = comm(8, "", (Swap(16, 768), (g_qkv,)))
    g_small = lax.dynamic_index_in_dim(
        g_small[:, :256].reshape(16, 16, 16), place, axis=1, keepdims=False
    )[:7].astype(F32)

    wide = wide_updates(
        (qkv_back, gate_back, up_back),
        (qkv_weight, qkv_first, qkv_second),
        (gate_weight, gate_first, gate_second),
        (up_weight, up_first, up_second),
    )
    updates = (
        wide[0:3],
        adamw(out_weight, out_first, out_second, g_out, (D // 16) ** (-0.5), 0.1),
        wide[3:6],
        wide[6:9],
        adamw(down_weight, down_first, down_second, g_down[:44].astype(F32), FF ** (-0.5), 0.1),
        adamw(small_params, small_first, small_second, g_small, 2.0, 0.0),
    )
    return (block_out, input_grad, *[x for u in updates for x in u])


def solution(mesh):
    fine = Mesh(mesh.devices.reshape(4, 2, 2, 4, 2), AXES)
    tokens = P(("z", "xh"), ("xl", "y", "core"), None)
    marks = P(("z", "xh"), ("xl", "y", "core"))
    rows = P(AXES, None)
    small = P(None, AXES)
    in_specs = (tokens, tokens, marks, marks) + (rows,) * 15 + (small,) * 3
    out_specs = (tokens, tokens) + (rows,) * 15 + (small,) * 3
    return jax.shard_map(local, mesh=fine, in_specs=in_specs, out_specs=out_specs, check_vma=False)
```

```python
import functools
import math

import jax
import jax.numpy as jnp
import numpy as np
from jax import lax
from jax.experimental import pallas as pl
from jax.experimental.pallas import tpu as pltpu
from jax.sharding import Mesh
from jax.sharding import PartitionSpec as P

D = 2048
H = 32
HEAD = 64
FF = 5632
ROT = 16
STEP = 10

NORM_EPS = 1e-05
BETA_ONE = 0.9
BETA_TWO = 0.95
ADAM_EPS = 1e-08
MASKED = -1e30

AXES = ("z", "xh", "xl", "y", "core")
YC = ("y", "core")
ZX = ("z", "xh", "xl")
HALF = 1024
SEQ = 2048
BF = jnp.bfloat16
F32 = jnp.float32


def norm_forward(rows, gain, shift):
    mean = jnp.mean(rows, axis=-1, keepdims=True)
    centred = rows - mean
    scale = lax.rsqrt(jnp.mean(centred * centred, axis=-1, keepdims=True) + NORM_EPS)
    unit = centred * scale
    return (unit * gain + shift, unit, scale)


def norm_backward(gradient, unit, scale, gain):
    along = gradient * gain
    inner = (
        along
        - jnp.mean(along, axis=-1, keepdims=True)
        - unit * jnp.mean(along * unit, axis=-1, keepdims=True)
    )
    return (inner * scale, jnp.sum(gradient * unit, axis=0), jnp.sum(gradient, axis=0))


def adamw(weight, first, second, gradient, rate, decay):
    first_new = BETA_ONE * first + (1.0 - BETA_ONE) * gradient
    second_new = BETA_TWO * second + (1.0 - BETA_TWO) * gradient * gradient
    mean_hat = first_new / (1.0 - BETA_ONE**STEP)
    square_hat = second_new / (1.0 - BETA_TWO**STEP)
    weight_new = weight - rate * (mean_hat / (jnp.sqrt(square_hat) + ADAM_EPS) + decay * weight)
    return (weight_new, first_new, second_new)


def dot_nn(a, b):
    return jnp.dot(a, b, preferred_element_type=F32)


def dot_nt(a, b):
    return lax.dot_general(a, b, (((1,), (1,)), ((), ())), preferred_element_type=F32)


def dot_tn(a, b):
    return lax.dot_general(a, b, (((0,), (0,)), ((), ())), preferred_element_type=F32)


def document_marks(params_ref):
    sequence = lax.axis_index("z") * 2 + lax.axis_index("xh")
    row = params_ref[7:8, pl.ds(pl.multiple_of(sequence * 256, 128), 128)]
    lane = lax.broadcasted_iota(jnp.int32, (1, 128), 1)
    length, high, low = [
        jnp.sum(jnp.where(lane == k, row, 0.0), axis=1, keepdims=True) for k in range(3)
    ]
    return length, high * 64.0 + low


def rotary_angles(params_ref, half):
    length, start = document_marks(params_ref)
    place = lax.broadcasted_iota(jnp.int32, (8, HALF), 1).astype(F32) + half * float(HALF)
    position = jnp.where(place < length, start + place, 4095.0 + place)
    row = lax.broadcasted_iota(jnp.int32, (8, HALF), 0)
    freq = jnp.zeros((8, HALF), F32)
    for k in range(ROT // 2):
        freq = jnp.where(row == k, float(np.float32(10000.0) ** np.float32(-k / (ROT // 2))), freq)
    angle = position * freq
    parts = []
    for value in (jnp.cos(angle), jnp.sin(angle)):
        high = value.astype(BF).astype(F32)
        parts += [high, value - high]
    return jnp.concatenate(parts, axis=0).astype(BF)


def rotary_tables(angles):
    row = lax.broadcasted_iota(jnp.int32, (16, 128), 0) % 8
    lane = lax.broadcasted_iota(jnp.int32, (16, 128), 1) % HEAD
    spread = jnp.where((lane < ROT) & (lane % 8 == row), 1.0, 0.0).astype(BF)
    lane = lax.broadcasted_iota(jnp.int32, (1, 128), 1) % HEAD
    cosine = dot_tn(angles[0:16], spread) + jnp.where(lane < ROT, 0.0, 1.0)
    sine = dot_tn(angles[16:32], spread)
    return cosine, jnp.where(lane < ROT // 2, -sine, 0.0), jnp.where(lane < ROT // 2, 0.0, sine)


def rotate(x, cosine, below, above):
    return x * cosine + pltpu.roll(x, 120, 1) * below + pltpu.roll(x, 8, 1) * above


def remote(src, dst, sems, at, device):
    return pltpu.make_async_remote_copy(
        src_ref=src,
        dst_ref=dst,
        send_sem=sems.at[0, at],
        recv_sem=sems.at[1, at],
        device_id=device,
        device_id_type=pl.DeviceIdType.MESH,
    )


def places():
    y, c, z = lax.axis_index("y"), lax.axis_index("core"), lax.axis_index("z")
    x = lax.axis_index("xh") * 2 + lax.axis_index("xl")
    step = lambda v, k: lax.rem(v + k, 4)
    at_x = lambda v: {"xh": lax.div(v, 2), "xl": lax.rem(v, 2)}
    devices = {
        "twin": {"core": 1 - c},
        "up": {"y": step(y, 1)},
        "down": {"y": step(y, 3)},
        "across": {"y": step(y, 2)},
        "up_twin": {"y": step(y, 1), "core": 1 - c},
        "down_twin": {"y": step(y, 3), "core": 1 - c},
        "across_twin": {"y": step(y, 2), "core": 1 - c},
        "x+": at_x(step(x, 1)),
        "x-": at_x(step(x, 3)),
        "z+": {"z": step(z, 1)},
        "z-": {"z": step(z, 3)},
        "pair": {"xl": 1 - lax.axis_index("xl")},
    }
    return y, c, x, z, devices


def add_low(a, b):
    return (a.astype(F32) + b.astype(F32)).astype(BF)


class RingGather:
    def __init__(self, block, cut, i, plus, minus, sems, base, pending):
        self.lo, self.hi = cut(block(lax.rem(i + 3, 4)))[0], cut(block(lax.rem(i + 1, 4)))[1]
        self.to_plus = remote(block(i), block(i), sems, base, plus)
        self.to_minus = remote(block(i), block(i), sems, base + 1, minus)
        self.pass_plus = remote(self.lo, self.lo, sems, base + 2, plus)
        self.pass_minus = remote(self.hi, self.hi, sems, base + 3, minus)
        pending += [self.to_plus, self.to_minus, self.pass_plus, self.pass_minus]

    def start(self):
        self.to_plus.start()
        self.to_minus.start()

    def before_came(self):
        self.to_plus.wait_recv()
        self.pass_plus.start()

    def after_came(self):
        self.to_minus.wait_recv()
        self.pass_minus.start()

    def finish(self):
        self.pass_plus.wait_recv()
        self.pass_minus.wait_recv()


class RingSum:
    def __init__(self, blocks, cut, plus, minus, acc, near, sems, base, pending):
        across, after, before = blocks
        self.cut, self.after, self.before, self.acc, self.near = cut, after, before, acc, near
        send = lambda src, slot, which, at, device: remote(
            cut(src)[which], cut(near(slot))[which], sems, base + at, device
        )
        self.far_plus = send(across, 0, 0, 0, plus)
        self.far_minus = send(across, 0, 1, 1, minus)
        self.own_plus = send(after, 1, 1, 2, plus)
        self.own_minus = send(before, 2, 0, 3, minus)
        self.sum_plus = send(acc, 1, 0, 4, plus)
        self.sum_minus = send(acc, 2, 1, 5, minus)
        self.coming = [self.own_plus, self.own_minus, self.sum_plus, self.sum_minus]
        pending += [self.far_plus, self.far_minus] + self.coming

    def far(self):
        self.far_plus.start()
        self.far_minus.start()

    def own(self):
        self.own_plus.start()
        self.own_minus.start()

    def middle(self):
        near = self.near(0)
        self.far_plus.wait_recv()
        self.cut(self.acc)[0][...] = add_low(self.cut(self.after)[0][...], self.cut(near)[0][...])
        self.sum_plus.start()
        self.far_minus.wait_recv()
        self.cut(self.acc)[1][...] = add_low(self.cut(self.before)[1][...], self.cut(near)[1][...])
        self.sum_minus.start()

    def finish(self, mine):
        for copy in self.coming:
            copy.wait_recv()
        total = mine[...].astype(F32) + self.near(1)[...].astype(F32) + self.near(2)[...].astype(F32)
        return total.astype(BF)


def ring_gather(block, cut, i, plus, minus, sems, base, pending):
    before, after = lax.rem(i + 3, 4), lax.rem(i + 1, 4)
    to_plus = remote(block(i), block(i), sems, base, plus)
    to_minus = remote(block(i), block(i), sems, base + 1, minus)
    to_plus.start()
    to_minus.start()
    yield
    to_plus.wait_recv()
    lo = cut(block(before))[0]
    pass_plus = remote(lo, lo, sems, base + 2, plus)
    pass_plus.start()
    yield
    to_minus.wait_recv()
    hi = cut(block(after))[1]
    pass_minus = remote(hi, hi, sems, base + 3, minus)
    pass_minus.start()
    pending += [to_plus, to_minus, pass_plus, pass_minus]
    yield
    pass_plus.wait_recv()
    pass_minus.wait_recv()


def ring_scatter(block, cut, i, plus, minus, acc, near, sems, base, pending):
    before, after, across = lax.rem(i + 3, 4), lax.rem(i + 1, 4), lax.rem(i + 2, 4)
    lo, hi = (lambda v: cut(v)[0]), (lambda v: cut(v)[1])
    far_plus = remote(lo(block(across)), lo(near.at[0]), sems, base, plus)
    far_minus = remote(hi(block(across)), hi(near.at[0]), sems, base + 1, minus)
    own_plus = remote(hi(block(after)), hi(near.at[1]), sems, base + 2, plus)
    own_minus = remote(lo(block(before)), lo(near.at[2]), sems, base + 3, minus)
    for copy in (far_plus, far_minus, own_plus, own_minus):
        copy.start()
    yield
    far_plus.wait_recv()
    lo(acc)[...] = add_low(lo(block(after))[...], lo(near.at[0])[...])
    sum_plus = remote(lo(acc), lo(near.at[1]), sems, base + 4, plus)
    sum_plus.start()
    yield
    far_minus.wait_recv()
    hi(acc)[...] = add_low(hi(block(before))[...], hi(near.at[0])[...])
    sum_minus = remote(hi(acc), hi(near.at[2]), sems, base + 5, minus)
    sum_minus.start()
    pending += [far_plus, far_minus, own_plus, own_minus, sum_plus, sum_minus]
    yield
    for copy in (own_plus, own_minus, sum_plus, sum_minus):
        copy.wait_recv()


class GatherTokens:
    peers = ("twin", "up", "down")
    n_sems = 10

    def __init__(self, rows, width, normalize=False, far=False):
        self.ins = [((rows, width), BF, "far")] if far else [((rows, width), BF)]
        self.outs = [((8, rows, width), BF, "far")] if far else [((8, rows, width), BF)]
        self.scratch = [pltpu.VMEM((rows, width), BF)] if normalize else []
        self.rows = rows

    def run(self, ins, outs, scratch, sems, base, place, pending):
        y, c, _, _, to = place
        (x_ref,), (out_ref,) = ins, outs
        if scratch:
            rows = x_ref[...].astype(F32)
            centred = rows - jnp.mean(rows, axis=-1, keepdims=True)
            spread = jnp.mean(centred * centred, axis=-1, keepdims=True)
            (x_ref,) = scratch
            x_ref[...] = (centred * lax.rsqrt(spread + NORM_EPS)).astype(BF)
            yield
        half = self.rows // 2
        lo, hi = pl.ds(0, half), pl.ds(half, half)
        at = lambda k: lax.rem(y + k, 4) * 2 + c
        mine = pltpu.make_async_copy(x_ref, out_ref.at[at(0)], sems.at[0, base + 9])
        s_up = remote(x_ref, out_ref.at[at(0)], sems, base, to["up"])
        s_down = remote(x_ref, out_ref.at[at(0)], sems, base + 1, to["down"])
        s_twin = remote(x_ref, out_ref.at[at(0)], sems, base + 2, to["twin"])
        for copy in (s_up, s_down, s_twin, mine):
            copy.start()
        pass_on = lambda ref, k, device: remote(ref, ref, sems, base + k, to[device])
        yield
        s_up.wait_recv()
        r_up = pass_on(out_ref.at[at(3), lo], 3, "up")
        t_down = pass_on(out_ref.at[at(3)], 5, "twin")
        r_up.start()
        t_down.start()
        yield
        s_down.wait_recv()
        r_down = pass_on(out_ref.at[at(1), hi], 4, "down")
        t_up = pass_on(out_ref.at[at(1)], 6, "twin")
        r_down.start()
        t_up.start()
        yield
        r_up.wait_recv()
        t_lo = pass_on(out_ref.at[at(2), lo], 7, "twin")
        t_lo.start()
        yield
        r_down.wait_recv()
        t_hi = pass_on(out_ref.at[at(2), hi], 8, "twin")
        t_hi.start()
        pending += [s_up, s_down, s_twin, r_up, r_down, t_down, t_up, t_lo, t_hi]
        yield
        for copy in (s_twin, t_down, t_up, t_lo, t_hi):
            copy.wait_recv()
        mine.wait()


class SumTokens:
    peers = ("twin", "up", "down")
    n_sems = 10
    steps = (2, 1, 3, 0)

    def __init__(self, rows, width, plus=False):
        self.ins = [((8, rows, width), BF)] + [((rows, width), F32)] * plus
        self.outs = [((rows, width), BF if plus else F32)]
        self.scratch = [
            pltpu.VMEM((4, rows, width), BF),
            pltpu.VMEM((3, rows, width), BF),
            pltpu.VMEM((rows, width), BF),
            pltpu.VMEM((3, rows, width), BF),
        ]
        self.rows = rows

    def swap(self, k, p_ref, scratch, sems, base, place):
        y, c, _, _, to = place
        at = lax.rem(y + self.steps[k], 4) * 2
        copy = remote(p_ref.at[at + 1 - c], scratch[0].at[k], sems, base + k, to["twin"])
        copy.start()
        return copy

    def rest(self, swaps, p_ref, out_ref, extra, scratch, sems, base, place, pending):
        y, c, _, _, to = place
        from_twin, pair, acc, near = scratch
        half = self.rows // 2
        cut = lambda v: (v.at[pl.ds(0, half)], v.at[pl.ds(half, half)])

        def send(block, slot, which, at, device):
            copy = remote(cut(block)[which], cut(near.at[slot])[which], sems, base + at, to[device])
            copy.start()
            return copy

        for k, off in enumerate(self.steps[:3]):
            swaps[k].wait_recv()
            pair[k] = add_low(p_ref[lax.rem(y + off, 4) * 2 + c], from_twin[k])
            if k == 0:
                far_plus = send(pair.at[0], 0, 0, 4, "up")
                far_minus = send(pair.at[0], 0, 1, 5, "down")
            elif k == 1:
                own_plus = send(pair.at[1], 1, 1, 6, "up")
            else:
                own_minus = send(pair.at[2], 2, 0, 7, "down")
        yield
        far_plus.wait_recv()
        cut(acc)[0][...] = add_low(cut(pair.at[1])[0][...], cut(near.at[0])[0][...])
        sum_plus = send(acc, 1, 0, 8, "up")
        yield
        far_minus.wait_recv()
        cut(acc)[1][...] = add_low(cut(pair.at[2])[1][...], cut(near.at[0])[1][...])
        sum_minus = send(acc, 2, 1, 9, "down")
        swaps[3].wait_recv()
        total = p_ref[y * 2 + c].astype(F32) + from_twin[3].astype(F32)
        if extra is not None:
            total = total + extra[...]
        pending += list(swaps) + [far_plus, far_minus, own_plus, own_minus, sum_plus, sum_minus]
        yield
        for copy in (own_plus, own_minus, sum_plus, sum_minus):
            copy.wait_recv()
        total = total + (near[1].astype(F32) + near[2].astype(F32))
        out_ref[...] = total.astype(out_ref.dtype)

    def run(self, ins, outs, scratch, sems, base, place, pending):
        swaps = [self.swap(k, ins[0], scratch, sems, base, place) for k in range(4)]
        yield
        extra = ins[1] if len(ins) > 1 else None
        yield from self.rest(swaps, ins[0], outs[0], extra, scratch, sems, base, place, pending)


class LastRows:
    peers = SumTokens.peers
    n_sems = SumTokens.n_sems

    def __init__(self):
        self.sum = SumTokens(128, D)
        self.ins = [
            ((HALF, 768), BF),
            ((HALF, D), BF),
            ((D, 896), BF),
            ((128, D), BF),
            ((128, D), F32),
            ((16, D), F32),
        ]
        self.outs = [((128, D), F32)]
        self.scratch = [
            pltpu.VMEM((8, 128, D), BF),
            pltpu.VMEM((128, D), F32),
            pltpu.VMEM((8, D), F32),
            pltpu.VMEM((8, 768), F32),
        ] + self.sum.scratch

    def run(self, ins, outs, scratch, sems, base, place, pending):
        d_ref, u_ref, w_ref, x_ref, d_middle_ref, params_ref = ins
        p_ref, total_ref, norm_ref, bias_ref = scratch[:4]
        self.sums = norm_ref, bias_ref
        y, c = place[:2]
        norm_ref[...] = jnp.zeros_like(norm_ref)
        bias_ref[...] = jnp.zeros_like(bias_ref)

        def two_blocks(at):
            rows = pl.ds(pl.multiple_of(at * 128, 256), 256)
            d = d_ref[rows, :]
            dh = dot_nt(d, w_ref[:, 0:768])
            p_ref[pl.ds(at, 2)] = dh.astype(BF).reshape(2, 128, D)
            norm_ref[0:1] += jnp.sum(dh * u_ref[rows, :].astype(F32), axis=0, keepdims=True)
            norm_ref[1:2] += jnp.sum(dh, axis=0, keepdims=True)
            bias_ref[0:1] += jnp.sum(d.astype(F32), axis=0, keepdims=True)

        swaps = []
        for k, off in enumerate(self.sum.steps):
            at = lax.rem(y + off, 4) * 2
            two_blocks(at)
            swaps.append(self.sum.swap(k, p_ref, scratch[4:], sems, base, place))
            yield
        yield from self.sum.rest(
            swaps, p_ref, total_ref, None, scratch[4:], sems, base, place, pending
        )
        rows = x_ref[...].astype(F32)
        centred = rows - jnp.mean(rows, axis=-1, keepdims=True)
        scale = lax.rsqrt(jnp.mean(centred * centred, axis=-1, keepdims=True) + NORM_EPS)
        unit = centred * scale
        along = total_ref[...] * params_ref[0:1]
        inner = (
            along
            - jnp.mean(along, axis=-1, keepdims=True)
            - unit * jnp.mean(along * unit, axis=-1, keepdims=True)
        )
        outs[0][...] = d_middle_ref[...] + inner * scale


def rows_or_columns(rows, width):
    if rows % 32 == 0:
        return lambda v: (v.at[pl.ds(0, rows // 2)], v.at[pl.ds(rows // 2, rows // 2)])
    return lambda v: (v.at[:, pl.ds(0, width // 2)], v.at[:, pl.ds(width // 2, width // 2)])


class GatherWeights:
    peers = ("x+", "x-", "z+", "z-")
    n_sems = 41

    def __init__(self, rows, width):
        self.ins = [((rows, width), BF)]
        self.outs = [((4, 4, rows, width), BF)]
        self.scratch = []
        self.rows, self.width = rows, width

    def rings(self, out_ref, sems, base, place, pending):
        _, _, x, z, to = place
        first = self.width // 256 * 128

        def one(order, base):
            width = self.width - first if order else first
            part = pl.ds(order * first, width)
            cut = rows_or_columns(self.rows, width)
            if order == 0:
                block = lambda k, j: out_ref.at[k, j, pl.ds(0, self.rows), part]
                i, k, ring, other = x, z, (to["x+"], to["x-"]), (to["z+"], to["z-"])
            else:
                block = lambda k, j: out_ref.at[j, k, pl.ds(0, self.rows), part]
                i, k, ring, other = z, x, (to["z+"], to["z-"]), (to["x+"], to["x-"])
            main = RingGather(lambda j: block(k, j), cut, i, *ring, sems, base, pending)
            mine, after, across, before = [
                RingGather(
                    lambda q, j=lax.rem(i + n, 4): block(q, j), cut, k, *other, sems, base + 4 + 4 * n, pending
                )
                for n in range(4)
            ]
            main.start()
            mine.start()
            yield
            main.before_came()
            before.start()
            yield
            main.after_came()
            after.start()
            yield
            mine.before_came()
            mine.after_came()
            yield
            main.finish()
            across.start()
            yield
            for part_ring in (before, after):
                part_ring.before_came()
                part_ring.after_came()
            yield
            across.before_came()
            across.after_came()
            yield
            for part_ring in (mine, before, after, across):
                part_ring.finish()

        yield from both(one(0, base), one(1, base + 20))

    def run(self, ins, outs, scratch, sems, base, place, pending):
        _, _, x, z, _ = place
        (x_ref,), (out_ref,) = ins, outs
        mine = pltpu.make_async_copy(x_ref, out_ref.at[z, x], sems.at[0, base + 40])
        mine.start()
        mine.wait()
        yield from self.rings(out_ref, sems, base, place, pending)


class SumWeights:
    peers = ("x+", "x-", "z+", "z-")
    n_sems = 60

    def __init__(self, rows, width):
        self.ins = [((4, 4, rows, width), BF)]
        self.outs = [((rows, width), BF)]
        self.rows, self.width = rows, width
        first = width // 256 * 128
        self.widths = (first, width - first)
        self.scratch = []
        for w in self.widths:
            self.scratch += [
                pltpu.VMEM((4, rows, w), BF),
                pltpu.VMEM((3, 4, rows, w), BF),
                pltpu.VMEM((4, rows, w), BF),
                pltpu.VMEM((rows, w), BF),
                pltpu.VMEM((3, rows, w), BF),
            ]

    def run(self, ins, outs, scratch, sems, base, place, pending):
        _, _, x, z, to = place
        (p_ref,), (out_ref,) = ins, outs
        every = pl.ds(0, self.rows)

        def one(order, bufs, base):
            acc, near, total, acc_two, near_two = bufs
            width = self.widths[order]
            part = pl.ds(order * self.widths[0], width)
            cut = rows_or_columns(self.rows, width)
            if order == 0:
                block = lambda k, j: p_ref.at[k, j, every, part]
                i, k, ring, other = x, z, (to["x+"], to["x-"]), (to["z+"], to["z-"])
            else:
                block = lambda k, j: p_ref.at[j, k, every, part]
                i, k, ring, other = z, x, (to["z+"], to["z-"]), (to["x+"], to["x-"])
            firsts = []
            for n, off in enumerate((2, 1, 3, 0)):
                at = lax.rem(k + off, 4)
                blocks = [block(at, lax.rem(i + m, 4)) for m in (2, 1, 3)]
                firsts.append(
                    RingSum(
                        blocks, cut, *ring, acc.at[n], lambda s, n=n: near.at[s, n], sems, base + 6 * n, pending
                    )
                )
            second = RingSum(
                [total.at[n] for n in range(3)], cut, *other, acc_two, lambda s: near_two.at[s], sems,
                base + 24, pending,
            )

            def complete(n):
                total[n] = firsts[n].finish(block(lax.rem(k + (2, 1, 3, 0)[n], 4), i))

            for one_ring in firsts:
                one_ring.far()
                one_ring.own()
            yield
            firsts[0].middle()
            firsts[1].middle()
            yield
            firsts[2].middle()
            firsts[3].middle()
            yield
            complete(0)
            second.far()
            yield
            complete(1)
            complete(2)
            second.own()
            yield
            second.middle()
            complete(3)
            yield
            out_ref[every, part] = second.finish(total.at[3])

        yield from both(one(0, scratch[:5], base), one(1, scratch[5:], base + 30))


def firsts(v):
    return v.at[pl.ds(0, 2)], v.at[pl.ds(2, 2)]


class GatherSmall:
    peers = ("x+", "x-", "z+", "z-")
    n_sems = 17

    def __init__(self, rows, width):
        self.ins = [((rows, width), BF)]
        self.outs = [((4, 4, rows, width), BF)]
        self.scratch = []
        self.rows, self.width = rows, width

    def rings(self, out_ref, sems, base, place, pending):
        _, _, x, z, to = place
        first = self.width // 256 * 128
        a, b = pl.ds(0, first), pl.ds(first, self.width - first)
        every = pl.ds(0, self.rows)
        cut_a = rows_or_columns(self.rows, first)
        cut_b = rows_or_columns(self.rows, self.width - first)

        def along_x_first():
            yield from ring_gather(
                lambda j: out_ref.at[z, j, every, a], cut_a, x, to["x+"], to["x-"], sems, base, pending
            )
            yield from ring_gather(
                lambda j: out_ref.at[j, pl.ds(0, 4), every, a], firsts, z, to["z+"], to["z-"], sems, base + 4,
                pending,
            )

        def along_z_first():
            yield from ring_gather(
                lambda j: out_ref.at[j, x, every, b], cut_b, z, to["z+"], to["z-"], sems, base + 8, pending
            )
            yield from ring_gather(
                lambda j: out_ref.at[pl.ds(0, 4), j, every, b], firsts, x, to["x+"], to["x-"], sems,
                base + 12, pending,
            )

        yield from both(along_x_first(), along_z_first())

    def run(self, ins, outs, scratch, sems, base, place, pending):
        _, _, x, z, _ = place
        (x_ref,), (out_ref,) = ins, outs
        mine = pltpu.make_async_copy(x_ref, out_ref.at[z, x], sems.at[0, base + 16])
        mine.start()
        mine.wait()
        yield from self.rings(out_ref, sems, base, place, pending)


class SumFew:
    peers = ("x+", "x-", "z+", "z-")
    n_sems = 24

    def __init__(self, rows, width):
        self.ins = [((4, 4, rows, width), BF)]
        self.outs = [((rows, width), BF)]
        self.rows, self.width = rows, width
        first = width // 256 * 128
        self.widths = (first, width - first)
        self.scratch = []
        for w in self.widths:
            self.scratch += [
                pltpu.VMEM((4, rows, w), BF),
                pltpu.VMEM((3, 4, rows, w), BF),
                pltpu.VMEM((4, rows, w), BF),
                pltpu.VMEM((rows, w), BF),
                pltpu.VMEM((3, rows, w), BF),
            ]

    def run(self, ins, outs, scratch, sems, base, place, pending):
        _, _, x, z, to = place
        (p_ref,), (out_ref,) = ins, outs
        every = pl.ds(0, self.rows)

        def one(order, bufs, base):
            acc, near, total, acc_two, near_two = bufs
            width = self.widths[order]
            columns = pl.ds(order * self.widths[0], width)
            cut = rows_or_columns(self.rows, width)
            four = pl.ds(0, 4)
            if order == 0:
                block = lambda j: p_ref.at[four, j, every, columns]
                i, k, far, close = x, z, ("x+", "x-"), ("z+", "z-")
            else:
                block = lambda j: p_ref.at[j, four, every, columns]
                i, k, far, close = z, x, ("z+", "z-"), ("x+", "x-")
            yield from ring_scatter(
                block, firsts, i, to[far[0]], to[far[1]], acc, near, sems, base, pending
            )
            total[...] = (
                block(i)[...].astype(F32) + near[1].astype(F32) + near[2].astype(F32)
            ).astype(BF)
            yield from ring_scatter(
                lambda j: total.at[j], cut, k, to[close[0]], to[close[1]], acc_two, near_two, sems,
                base + 6, pending,
            )
            out_ref[every, columns] = (
                total[k].astype(F32) + near_two[1].astype(F32) + near_two[2].astype(F32)
            ).astype(BF)

        yield from both(one(0, scratch[:5], base), one(1, scratch[5:], base + 12))


class Swap:
    peers = ("twin", "up", "down", "across", "up_twin", "down_twin", "across_twin")
    n_sems = 8
    steps = ((0, 1), (1, 0), (3, 0), (2, 0), (1, 1), (3, 1), (2, 1))

    def __init__(self, rows, width):
        self.ins = [((8, rows, width), BF)]
        self.outs = [((8, rows, width), BF)]
        self.scratch = []

    def send(self, x_ref, out_ref, sems, base, place):
        y, c, _, _, to = place
        me = y * 2 + c
        copies = [pltpu.make_async_copy(x_ref.at[me], out_ref.at[me], sems.at[0, base + 7])]
        for k, (name, (up, other)) in enumerate(zip(self.peers, self.steps)):
            at = lax.rem(y + up, 4) * 2 + (1 - c if other else c)
            copies.append(remote(x_ref.at[at], out_ref.at[me], sems, base + k, to[name]))
        for copy in copies:
            copy.start()
        return copies

    def run(self, ins, outs, scratch, sems, base, place, pending):
        copies = self.send(ins[0], outs[0], sems, base, place)
        yield
        copies[0].wait()
        for copy in copies[1:]:
            copy.wait_recv()
        pending += copies[1:]


def columns(at, width):
    return slice(at, at + width)


class ShareQkv:
    peers = Swap.peers + GatherWeights.peers

    def __init__(self):
        self.swap = Swap(16, 896)
        self.gather = GatherWeights(128, 896)
        self.ins = [((16, 6144), F32, "far"), ((16, 128), BF)]
        self.outs = [(*self.gather.outs[0], "far"), ((16, 16 * 128), F32)]
        self.scratch = [pltpu.VMEM((8, 16, 896), BF)] * 2
        self.n_sems = 16 + self.gather.n_sems

    def run(self, ins, outs, scratch, sems, base, place, pending):
        _, _, x, z, _ = place
        weight_ref, tile_ref = ins
        (out_ref, tiles_ref), (piece, landed) = outs, scratch
        for k in range(8):
            for pair in range(2):
                for kind in range(3):
                    piece[k, :, columns(pair * 384 + kind * 128, 128)] = weight_ref[
                        :, columns(kind * D + k * 256 + pair * 128, 128)
                    ].astype(BF)
            piece[k, :, columns(768, 128)] = tile_ref[...]
        yield from self.swap.run((piece,), (landed,), (), sems, base, place, pending)
        for k in range(8):
            out_ref[z, x, columns(k * 16, 16)] = landed[k]
        yield from self.gather.rings(out_ref, sems, base + 16, place, pending)
        for k in range(16):
            tiles = [
                out_ref[k // 4, k % 4, columns(j * 16, 16), columns(768, 128)].astype(F32)
                for j in range(8)
            ]
            tiles_ref[:, columns(k * 128, 128)] = sum(tiles[1:], tiles[0])


def moved(read, tile, pieces, last):
    lane = lax.broadcasted_iota(jnp.int32, (16, 128), 1)
    value = jnp.zeros((16, 128), F32)
    for there, source, here, width in pieces:
        at = there - tile * 128
        if at + width <= 0 or at >= 128:
            continue
        start = min(here // 128 * 128, last)
        window = read(source, columns(start, 256)).astype(F32)
        shift = (at - (here - start)) % 256
        window = (pltpu.roll(window, shift, 1) if shift else window)[:, 0:128]
        value = jnp.where((lane >= at) & (lane < at + width), window, value)
    return value


class ShareHidden:
    peers = Swap.peers

    def __init__(self):
        self.swap = Swap(16, 1536)
        self.ins = [((16, FF), F32, "far")] * 2
        self.outs = self.swap.outs
        self.scratch = [pltpu.VMEM((8, 16, 1536), BF)]
        self.n_sems = self.swap.n_sems

    def run(self, ins, outs, scratch, sems, base, place, pending):
        (piece,) = scratch
        for k in range(8):
            pieces = [(j * 48, None, (j * 8 + k) * 44, 44) for j in range(16)]
            for w, ref in enumerate(ins):
                for tile in range(6):
                    value = moved(lambda _, at: ref[:, at], tile, pieces, FF - 256)
                    piece[k, :, columns(w * 768 + tile * 128, 128)] = value.astype(BF)
            yield
        yield from self.swap.run((piece,), outs, (), sems, base, place, pending)


class TokenSums:
    peers = ()
    n_sems = 0

    def __init__(self, rows, width, count, step=256):
        self.ins = [((HALF, rows), BF)] + [((HALF, width), BF)] * count
        self.outs = [((rows, width), BF)] * count
        self.scratch = []
        self.steps = [pl.ds(k, step) for k in range(0, rows, step)]

    def run(self, ins, outs, scratch, sems, base, place, pending):
        for columns in self.steps:
            for b_ref, out_ref in zip(ins[1:], outs):
                out_ref[columns, :] = dot_tn(ins[0][:, columns], b_ref[...]).astype(BF)
            yield


class GradThenSum:
    peers = SumWeights.peers

    def __init__(self, rows, width, steps, swap=False):
        self.sum = SumWeights(rows // 16, width)
        self.swap = Swap(rows // 128, width) if swap else None
        self.ins = [((HALF, rows), BF), ((HALF, width), BF)]
        self.outs = self.swap.outs if swap else self.sum.outs
        self.scratch = [pltpu.VMEM((4, 4, rows // 16, width), BF)] + self.sum.scratch
        self.n_sems = self.sum.n_sems
        if swap:
            self.peers = Swap.peers + SumWeights.peers
            self.scratch += [pltpu.VMEM((rows // 16, width), BF), pltpu.VMEM((8, rows // 128, width), BF)]
            self.n_sems += 8
        self.rows, self.steps = rows, steps

    def run(self, ins, outs, scratch, sems, base, place, pending):
        terms = scratch[0]
        block, step = self.rows // 16, self.rows // self.steps
        for k in range(self.steps):
            part = dot_tn(ins[0][:, columns(k * step, step)], ins[1][...]).astype(BF)
            for j in range(step // block):
                at = k * step // block + j
                terms[at // 4, at % 4] = part[columns(j * block, block)]
            yield
        if self.swap is None:
            yield from self.sum.run((terms,), outs, scratch[1:], sems, base, place, pending)
            return
        *buffers, total, piece = scratch[1:]
        yield from self.sum.run((terms,), (total,), buffers, sems, base, place, pending)
        count = self.rows // 128
        for k in range(8):
            piece[k] = total[columns(k * count, count)]
        at = base + self.sum.n_sems
        yield from self.swap.run((piece,), outs, (), sems, at, place, pending)


class Product:
    peers = ()
    n_sems = 0

    def __init__(self, depth, width):
        self.ins = [((HALF, depth), BF), ((depth, width), BF)]
        self.outs = [((HALF, width), BF)]
        self.scratch = []

    def run(self, ins, outs, scratch, sems, base, place, pending):
        for k in range(0, HALF, 256):
            outs[0][pl.ds(k, 256), :] = dot_nn(ins[0][pl.ds(k, 256), :], ins[1][...]).astype(BF)
            yield


class SumSmall:
    peers = Swap.peers + SumFew.peers

    def __init__(self, last):
        self.last = last
        self.swap = Swap(16, 512)
        self.sum = SumFew(16, 512)
        self.ins = [((8, D), F32)]
        self.outs = self.sum.outs
        self.scratch = [
            pltpu.VMEM((8, 16, 512), F32),
            pltpu.VMEM((8, 16, 512), BF),
            pltpu.VMEM((8, 16, 512), BF),
            pltpu.VMEM((4, 4, 16, 512), BF),
        ] + self.sum.scratch
        self.n_sems = 8 + self.sum.n_sems

    def run(self, ins, outs, scratch, sems, base, place, pending):
        wide, piece, landed, spread = scratch[:4]
        norm_ref, bias_ref = self.last.sums
        yc = place[0] * 2 + place[1]
        wide[...] = jnp.zeros_like(wide)
        for k in range(8):
            at = columns(k * 256, 256)
            wide[k, 0:8, 0:256] = ins[0][:, at]
            wide[k, 0:2, 0:256] = norm_ref[0:2, at]
        for pair in range(2):
            for kind in range(3):
                wide[yc, 2 + kind : 3 + kind, columns(pair * 128, 128)] = bias_ref[
                    0:1, columns((pair * 3 + kind) * 128, 128)
                ]
        piece[...] = wide[...].astype(BF)
        yield from self.swap.run((piece,), (landed,), (), sems, base, place, pending)
        total = jnp.sum(landed[...].astype(F32), axis=0).astype(BF)
        spread[...] = jnp.broadcast_to(total[None, None], spread.shape)
        yield from self.sum.run((spread,), outs, scratch[4:], sems, base + 8, place, pending)


def both(*parts):
    parts = list(parts)
    while parts:
        for part in list(parts):
            try:
                next(part)
            except StopIteration:
                parts.remove(part)
        yield


def in_order(parts, order):
    for letter in order:
        next(parts["abcdef".index(letter)], None)
    for _ in both(*parts):
        pass


def size(shape, dtype):
    return math.prod(shape) * jnp.dtype(dtype).itemsize


def loaded(part, copies):
    for copy in copies:
        copy.wait()
    yield from part


def stored(part, copies):
    yield from part
    for copy in copies:
        copy.start()


def comm_kernel(parts, order, *refs):
    *refs, sems, move_sems = refs
    refs = list(refs)
    take = lambda count: [refs.pop(0) for _ in range(count)]
    ins = [take(len(p.ins)) for p in parts]
    outs = [take(len(p.outs)) for p in parts]
    scratch = [take(len(p.scratch)) for p in parts]
    loads, stores, moves = [], [], 0
    for p, p_ins, p_outs in zip(parts, ins, outs):
        for refs_of, specs, copies in ((p_ins, p.ins, loads), (p_outs, p.outs, stores)):
            copies.append([])
            for k, spec in enumerate(specs):
                if len(spec) > 2:
                    far, near = refs_of[k], refs.pop(0)
                    ends = (far, near) if copies is loads else (near, far)
                    copies[-1].append(pltpu.make_async_copy(*ends, move_sems.at[moves]))
                    moves += 1
                    refs_of[k] = near
    for copy in sum(loads, []):
        copy.start()
    place = places()
    names = []
    for p in parts:
        names += [n for n in p.peers if n not in names]
    barrier = pltpu.get_barrier_semaphore()
    for name in names:
        pl.semaphore_signal(
            barrier, inc=1, device_id=place[4][name], device_id_type=pl.DeviceIdType.MESH
        )
    pl.semaphore_wait(barrier, len(names))
    base, running, pending = 0, [], []
    for k, p in enumerate(parts):
        p.held = outs[k]
        steps = p.run(ins[k], outs[k], scratch[k], sems, base, place, pending)
        running.append(stored(loaded(steps, loads[k]), stores[k]))
        base += p.n_sems
    in_order(running, order)
    for copy in pending:
        copy.wait_send()
    for copy in sum(stores, []):
        copy.wait()


def comm(collective_id, order, *pairs):
    parts = [p for p, _ in pairs]
    operands = [x.reshape(spec[0]) for p, xs in pairs for x, spec in zip(xs, p.ins)]
    operands = [
        pltpu.with_memory_space_constraint(x, pltpu.HBM) if len(spec) > 2 else x
        for x, spec in zip(operands, [spec for p in parts for spec in p.ins])
    ]
    in_specs = [spec for p in parts for spec in p.ins]
    out_specs = [spec for p in parts for spec in p.outs]
    marked = [spec for p in parts for spec in (*p.ins, *p.outs) if len(spec) > 2]
    where = lambda spec: pl.BlockSpec(memory_space=pltpu.HBM if len(spec) > 2 else pltpu.VMEM)
    held = sum(size(*spec[:2]) for spec in in_specs + out_specs)
    held += sum(size(s.shape, s.dtype) for p in parts for s in p.scratch)
    sent = sum(math.prod(spec[0]) for spec in out_specs) * 2
    return pl.pallas_call(
        functools.partial(comm_kernel, parts, order),
        out_shape=[(pltpu.HBM if len(spec) > 2 else jax.ShapeDtypeStruct)(*spec[:2]) for spec in out_specs],
        in_specs=[where(spec) for spec in in_specs],
        out_specs=[where(spec) for spec in out_specs],
        scratch_shapes=[s for p in parts for s in p.scratch]
        + [pltpu.VMEM(*spec[:2]) for spec in marked]
        + [
            pltpu.SemaphoreType.DMA((2, sum(p.n_sems for p in parts))),
            pltpu.SemaphoreType.DMA((max(1, len(marked)),)),
        ],
        compiler_params=pltpu.CompilerParams(
            collective_id=collective_id, has_side_effects=True, vmem_limit_bytes=held + (8 << 20)
        ),
        cost_estimate=pl.CostEstimate(flops=0, bytes_accessed=20 * sent, transcendentals=0),
    )(*operands)


ROWS = 256


class MakeQkv:
    peers = ()
    n_sems = 0

    def __init__(self, weights, units):
        self.weights, self.units = weights, units
        self.ins = []
        self.outs = [((HALF, D), BF), ((HALF, 768), BF), ((2, 32, HALF), BF)]
        self.scratch = []

    def run(self, ins, outs, scratch, sems, base, place, pending):
        h_ref, out_ref, angles_ref = outs
        w_ref, params_ref = self.weights.held
        (u_ref,) = self.units.held
        yc = place[0] * 2 + place[1]
        xl = lax.axis_index("xl")
        for half in range(2):
            angles_ref[half] = rotary_angles(params_ref, half)
        weight = w_ref[:, :, :, 0:768].reshape(D, 768)
        for k in range(4):
            rows = columns(k * ROWS, ROWS)
            unit = u_ref[2 * k : 2 * k + 2].reshape(ROWS, D).astype(F32)
            h = (unit * params_ref[0:1] + params_ref[1:2]).astype(BF)
            h_ref[rows, :] = h
            mixed = dot_nn(h, weight)
            tables = rotary_tables(angles_ref[xl, :, rows])
            for j in range(6):
                pair, kind = j // 3, j % 3
                at = pl.ds(pl.multiple_of(yc * 256 + pair * 128, 128), 128)
                part = mixed[:, columns(j * 128, 128)] + params_ref[2 + kind : 3 + kind, at]
                if kind < 2:
                    part = rotate(part, *tables)
                out_ref[rows, columns(j * 128, 128)] = part.astype(BF)
        yield


def rowwise(width):
    return pl.BlockSpec((ROWS, width), lambda i: (i, 0))


def fixed(*shape):
    return pl.BlockSpec(shape, lambda i: (0,) * len(shape), pipeline_mode=pl.Buffered(1))


BLOCK = 512
Q, K, V = slice(0, 128), slice(128, 256), slice(256, 384)


def only(x, h):
    lane = lax.broadcasted_iota(jnp.int32, (1, 128), 1)
    return jnp.where((lane >= h * HEAD) & (lane < (h + 1) * HEAD), x, jnp.zeros_like(x))


def rows_of(k):
    return slice(k * BLOCK, (k + 1) * BLOCK)


def allowed_mask(first_len, key_half, kb, query_half, qb, diagonal):
    key = lax.broadcasted_iota(jnp.int32, (BLOCK, BLOCK), 0) + kb * BLOCK
    query = lax.broadcasted_iota(jnp.int32, (BLOCK, BLOCK), 1) + qb * BLOCK
    allowed = None
    if diagonal and kb == qb:
        allowed = key <= query
    if kb == 0:
        length = first_len.astype(jnp.int32)
        same = (key + key_half * HALF >= length) | (query + query_half * HALF < length)
        allowed = same if allowed is None else allowed & same
    return allowed


def lanes(at, width):
    return pl.ds(pl.multiple_of(at * width, 128), width)


class Attend:
    peers = ("pair",)
    n_sems = 6

    def __init__(self):
        self.ins = [((16, D), F32), ((HALF, 768), BF)]
        self.outs = [
            ((HALF, 256), BF),
            ((2, 128, HALF), F32),
            ((2, 8, HALF), F32),
            ((2, HALF, 384), BF),
        ]
        self.scratch = [pltpu.VMEM((2, 8, HALF), F32), pltpu.VMEM((2, HALF, 128), BF)]

    def run(self, ins, outs, scratch, sems, base, place, pending):
        params_ref, qkv_ref = ins
        o_ref, acc_ref, top_ref, x_ref = outs
        total_ref, half_ref = scratch
        pair = place[4]["pair"]
        xl = lax.axis_index("xl")
        first_len = document_marks(params_ref)[0]
        sent = []
        for b in range(2):
            copy = remote(
                qkv_ref.at[rows_of(b), lanes(1 - xl, 384)], x_ref.at[xl, rows_of(b)], sems, base + b, pair
            )
            copy.start()
            sent.append(copy)
        kept = pltpu.make_async_copy(qkv_ref.at[:, lanes(xl, 384)], x_ref.at[xl], sems.at[0, base + 2])
        kept.start()
        kept.wait()
        yield

        def block(query_half, key_half, qb, h, state, diagonal):
            qs = rows_of(qb)
            qh = only(x_ref[query_half, qs, Q] * jnp.asarray(HEAD**-0.5, BF), h)
            top, total, acc = state
            for kb in range(qb + 1 if diagonal else 2):
                ks = rows_of(kb)
                scores = dot_nt(x_ref[key_half, ks, K], qh)
                allowed = allowed_mask(first_len, key_half, kb, query_half, qb, diagonal)
                if allowed is not None:
                    scores = jnp.where(allowed, scores, MASKED)
                new_top = jnp.maximum(top, jnp.max(scores, axis=0, keepdims=True))
                weights = jnp.exp(scores - new_top)
                if allowed is not None:
                    weights = jnp.where(allowed, weights, 0.0)
                shrink = jnp.exp(top - new_top)
                total = total * shrink + jnp.sum(weights, axis=0, keepdims=True)
                part = dot_tn(only(x_ref[key_half, ks, V], h), weights.astype(BF))
                acc = acc * shrink + part[h * HEAD : (h + 1) * HEAD]
                top = new_top
            top_ref[query_half, h : h + 1, qs] = top
            total_ref[query_half, h : h + 1, qs] = total
            acc_ref[query_half, h * HEAD : (h + 1) * HEAD, qs] = acc

        def diagonal(half):
            for qb in range(2):
                for h in range(2):
                    start = (
                        jnp.full((1, BLOCK), MASKED, F32),
                        jnp.zeros((1, BLOCK), F32),
                        jnp.zeros((HEAD, BLOCK), F32),
                    )
                    block(half, half, qb, h, start, True)

        def finish(half):
            for qb in range(2):
                qs = rows_of(qb)
                for h in range(2):
                    hs = slice(h * HEAD, (h + 1) * HEAD)
                    total = total_ref[half, h : h + 1, qs]
                    acc_ref[half, hs, qs] = acc_ref[half, hs, qs] / total
                    top_ref[half, h : h + 1, qs] = top_ref[half, h : h + 1, qs] + jnp.log(total)
                half_ref[half, qs, :] = acc_ref[half, :, qs].T.astype(BF)

        diagonal(xl)
        yield
        for copy in sent:
            copy.wait_recv()
        diagonal(1 - xl)
        yield
        for qb in range(2):
            for h in range(2):
                qs = rows_of(qb)
                state = (
                    top_ref[1, h : h + 1, qs],
                    total_ref[1, h : h + 1, qs],
                    acc_ref[1, h * HEAD : (h + 1) * HEAD, qs],
                )
                block(1, 0, qb, h, state, False)
            yield
        finish(1 - xl)
        back = remote(half_ref.at[1 - xl], o_ref.at[:, lanes(xl, 128)], sems, base + 3, pair)
        back.start()
        finish(xl)
        mine = pltpu.make_async_copy(half_ref.at[xl], o_ref.at[:, lanes(xl, 128)], sems.at[0, base + 4])
        mine.start()
        pending += sent + [back]
        yield
        mine.wait()
        back.wait_recv()


class AttendBack:
    peers = ("pair",)
    n_sems = 6

    def __init__(self):
        self.ins = [
            ((16, D), F32),
            ((2, HALF, 384), BF),
            ((HALF, 256), BF),
            ((2, 128, HALF), F32),
            ((2, 8, HALF), F32),
            ((2, 32, HALF), BF),
        ]
        self.outs = [((HALF, 768), BF)]
        self.scratch = [
            pltpu.VMEM((2, HALF, 128), BF),
            pltpu.VMEM((2, 128, HALF), F32),
            pltpu.VMEM((2, HALF, 128), F32),
            pltpu.VMEM((2, HALF, 128), F32),
            pltpu.VMEM((2, HALF, 384), BF),
        ]

    def run(self, ins, outs, scratch, sems, base, place, pending):
        params_ref, x_ref, own_ref, ot_ref, lse_ref, angles_ref = ins
        (out_ref,) = outs
        do_ref, dqt_ref, dk_ref, dv_ref, half_ref = scratch
        pair = place[4]["pair"]
        xl = lax.axis_index("xl")
        first_len = document_marks(params_ref)[0]
        sent = remote(own_ref.at[:, lanes(1 - xl, 128)], do_ref.at[xl], sems, base, pair)
        sent.start()
        kept = pltpu.make_async_copy(own_ref.at[:, lanes(xl, 128)], do_ref.at[xl], sems.at[0, base + 1])
        kept.start()
        kept.wait()
        yield

        def block(query_half, key_half, qb, h, diagonal):
            qs = rows_of(qb)
            hs = slice(h * HEAD, (h + 1) * HEAD)
            do = do_ref[query_half, qs, :]
            qh = only(x_ref[query_half, qs, Q] * jnp.asarray(HEAD**-0.5, BF), h)
            doh = only(do, h)
            delta = jnp.sum(
                doh.astype(F32).T[hs] * ot_ref[query_half, hs, qs], axis=0, keepdims=True
            )
            lse = lse_ref[query_half, h : h + 1, qs]
            for kb in range(qb + 1 if diagonal else 2):
                ks = rows_of(kb)
                k = x_ref[key_half, ks, K]
                scores = dot_nt(k, qh)
                probs = jnp.exp(scores - lse)
                allowed = allowed_mask(first_len, key_half, kb, query_half, qb, diagonal)
                if allowed is not None:
                    probs = jnp.where(allowed, probs, 0.0)
                pulled = dot_nt(x_ref[key_half, ks, V], doh)
                ds = (probs * (pulled - delta)).astype(BF)
                dv = dot_nn(probs.astype(BF), doh)
                dk = dot_nn(ds, qh)
                dq = dot_tn(only(k, h), ds)[hs]
                if diagonal and h == 0 and qb == kb:
                    dv_ref[key_half, ks, :] = dv
                    dk_ref[key_half, ks, :] = dk
                else:
                    dv_ref[key_half, ks, :] += dv
                    dk_ref[key_half, ks, :] += dk
                if diagonal and kb == 0:
                    dqt_ref[query_half, hs, qs] = dq
                else:
                    dqt_ref[query_half, hs, qs] += dq

        def finish(half):
            for b in range(2):
                bs = rows_of(b)
                cosine, below, above = rotary_tables(angles_ref[half, :, bs])
                dq = dqt_ref[half, :, bs].T * HEAD**-0.5
                half_ref[half, bs, Q] = rotate(dq, cosine, -below, -above).astype(BF)
                half_ref[half, bs, K] = rotate(dk_ref[half, bs, :], cosine, -below, -above).astype(BF)
                half_ref[half, bs, V] = dv_ref[half, bs, :].astype(BF)

        for qb in range(2):
            for h in range(2):
                block(xl, xl, qb, h, True)
        yield
        sent.wait_recv()
        for qb in range(2):
            for h in range(2):
                block(1 - xl, 1 - xl, qb, h, True)
        yield
        for qb in range(2):
            for h in range(2):
                block(1, 0, qb, h, False)
            yield
        finish(1 - xl)
        back = remote(half_ref.at[1 - xl], out_ref.at[:, lanes(xl, 384)], sems, base + 2, pair)
        back.start()
        finish(xl)
        mine = pltpu.make_async_copy(half_ref.at[xl], out_ref.at[:, lanes(xl, 384)], sems.at[0, base + 3])
        mine.start()
        pending += [sent, back]
        yield
        mine.wait()
        back.wait_recv()


def feed_kernel(h_ref, dy_ref, gate_ref, up_ref, down_ref, hid_ref, dg_ref, du_ref, dh_ref):
    gate, up = dot_nn(h_ref[...], gate_ref[...]), dot_nn(h_ref[...], up_ref[...])
    sigmoid = jax.nn.sigmoid(gate)
    activated = gate * sigmoid
    hidden = (activated * up).astype(BF)
    hid_ref[...] = hidden
    d_hidden = dot_nt(dy_ref[...], down_ref[...])
    d_gate = (d_hidden * up * sigmoid * (1.0 + gate * (1.0 - sigmoid))).astype(BF)
    d_up = (d_hidden * activated).astype(BF)
    dg_ref[...] = d_gate
    du_ref[...] = d_up
    dh_ref[...] = (dot_nt(d_gate, gate_ref[...]) + dot_nt(d_up, up_ref[...])).astype(BF)


def feed_call(h, dy, w_gate, w_up, w_down):
    return pl.pallas_call(
        feed_kernel,
        out_shape=(
            jax.ShapeDtypeStruct((HALF, 768), BF),
            jax.ShapeDtypeStruct((HALF, 768), BF),
            jax.ShapeDtypeStruct((HALF, 768), BF),
            jax.ShapeDtypeStruct((HALF, D), BF),
        ),
        grid=(HALF // ROWS,),
        in_specs=[rowwise(D), rowwise(D), fixed(D, 768), fixed(D, 768), fixed(768, D)],
        out_specs=(rowwise(768), rowwise(768), rowwise(768), rowwise(D)),
        compiler_params=pltpu.CompilerParams(vmem_limit_bytes=34 << 20),
        cost_estimate=pl.CostEstimate(
            flops=5 * 2 * HALF * D * 768, bytes_accessed=26 << 20, transcendentals=HALF * 768
        ),
    )(h, dy, w_gate, w_up, w_down)


def wide_update_kernel(qkv_ref, gate_ref, up_ref, *refs):
    ins, outs = refs[:9], refs[9:]

    def update(k, at, gradient):
        new = adamw(*[ref[:, at] for ref in ins[k * 3 : k * 3 + 3]], gradient, D ** (-0.5), 0.1)
        for ref, value in zip(outs[k * 3 : k * 3 + 3], new):
            ref[:, at] = value

    for k in range(8):
        for pair in range(2):
            for kind in range(3):
                update(
                    0,
                    columns(kind * D + k * 256 + pair * 128, 128),
                    qkv_ref[k, :, columns(pair * 384 + kind * 128, 128)].astype(F32),
                )
    pieces = [(o * 44, o % 8, o // 8 * 48, 44) for o in range(128)]
    for w, grad_ref in enumerate((gate_ref, up_ref)):
        for tile in range(FF // 128):
            value = moved(lambda k, at: grad_ref[k, :, at], tile, pieces, 768 - 256)
            update(1 + w, columns(tile * 128, 128), value)


def wide_updates(grads, *states):
    operands = [x for state in states for x in state]
    return pl.pallas_call(
        wide_update_kernel,
        out_shape=[jax.ShapeDtypeStruct(x.shape, F32) for x in operands],
        in_specs=[pl.BlockSpec(memory_space=pltpu.VMEM)] * 12,
        out_specs=[pl.BlockSpec(memory_space=pltpu.VMEM)] * 9,
        compiler_params=pltpu.CompilerParams(vmem_limit_bytes=24 << 20),
        cost_estimate=pl.CostEstimate(flops=20 << 20, bytes_accessed=10 << 20, transcendentals=1 << 20),
    )(*grads, *operands)


TO_HEADS = [(f * 16 + ctx, ctx * 8 + f) for f in range(8) for ctx in range(16)]
TO_OWNER = [(b, a) for a, b in TO_HEADS]


def local(
    hidden_in, out_grad, positions, documents,
    qkv_weight, qkv_first, qkv_second,
    out_weight, out_first, out_second,
    gate_weight, gate_first, gate_second,
    up_weight, up_first, up_second,
    down_weight, down_first, down_second,
    small_params, small_first, small_second,
):
    xh, xl, z = lax.axis_index("xh"), lax.axis_index("xl"), lax.axis_index("z")
    yc = lax.axis_index("y") * 2 + lax.axis_index("core")
    place = (z * 2 + xh) * 2 + xl

    first_here = jnp.sum(1 - documents)
    start_here = positions[0, 0]
    marks = jnp.stack([first_here, start_here // 64, start_here % 64]).astype(BF)
    tile = jnp.concatenate(
        [small_params.astype(BF), jnp.pad(marks, (0, 13))[None]], axis=0
    )
    tile = jnp.where((jnp.arange(8) == yc)[None, :, None], tile[:, None, :], 0)
    tile = jnp.pad(tile.reshape(8, 128), ((0, 8), (0, 0)))
    outer = out_grad.reshape(128, D)
    out_rows = lax.ppermute(out_weight.astype(BF), AXES, TO_HEADS)
    share, units = ShareQkv(), GatherTokens(128, D, normalize=True, far=True)
    w_all, params, u_all, gu_mine, w_out, h1, qkv, angles = comm(
        0,
        "adbccdddccddabccdccaacaaabbabbaabce",
        (share, (qkv_weight, tile)),
        (units, (hidden_in,)),
        (ShareHidden(), (gate_weight, up_weight)),
        (GatherSmall(16, D), (out_rows,)),
        (MakeQkv(share, units), ()),
    )
    u_all, w_qkv, w_out = u_all.reshape(HALF, D), w_all.reshape(D, 896), w_out.reshape(256, D)
    gu_mine = gu_mine.reshape(128, 1536)
    o, attended_t, lse, heads, dy, w_gate = comm(
        1,
        "abcabbccacbbaaccabca",
        (Attend(), (params, qkv)),
        (GatherTokens(128, D, far=True), (outer,)),
        (GatherWeights(128, 768), (gu_mine[:, :768],)),
    )
    dy = dy.reshape(HALF, D)
    branch_part = dot_nn(o, w_out).astype(BF)
    branch, w_up = comm(
        2,
        "ababbbbaabbab",
        (SumTokens(128, D), (branch_part,)),
        (GatherWeights(128, 768), (gu_mine[:, 768:],)),
    )
    rows = hidden_in.reshape(128, D).astype(F32)
    middle = rows + branch
    normed_two, unit_two, scale_two = norm_forward(middle, params[5], params[6])
    down_piece = jnp.pad(down_weight.astype(BF), ((0, 4), (0, 0)))
    h2, w_down = comm(
        3,
        "abbbbaabbaabab",
        (GatherTokens(128, D), (normed_two.astype(BF),)),
        (GatherWeights(48, D), (down_piece,)),
    )
    h2 = h2.reshape(HALF, D)
    w_down = w_down.reshape(768, D)
    hidden, d_gate_low, d_up_low, dh2_part = feed_call(
        h2, dy, w_gate.reshape(D, 768), w_up.reshape(D, 768), w_down
    )

    d_normed_two, g_down, d_gate, d_up = comm(
        4,
        "abbbaccbbaacccbccbbacb",
        (SumTokens(128, D), (dh2_part,)),
        (GradThenSum(768, D, 2), (hidden, dy)),
        (TokenSums(D, 768, 2), (h2, d_gate_low, d_up_low)),
    )
    d_middle_part, d_gain_two, d_shift_two = norm_backward(
        d_normed_two, unit_two, scale_two, params[5]
    )
    d_middle = outer.astype(F32) + d_middle_part
    dx2, g_gate, y_part = comm(
        5,
        "abcbbcaacbbbcaaab",
        (GatherTokens(128, D), (d_middle.astype(BF),)),
        (SumWeights(128, 768), (d_gate,)),
        (Product(768, D), (hidden, w_down)),
    )
    dx2 = dx2.reshape(HALF, D)
    do = dot_nt(dx2, w_out).astype(BF)
    d_qkv_low, block_out, g_up, gate_back = comm(
        7,
        "abcdabaccaaabbcccdbca",
        (AttendBack(), (params, heads, do, attended_t, lse, angles)),
        (SumTokens(128, D, plus=True), (y_part, middle)),
        (SumFew(128, 768), (d_up,)),
        (Swap(16, 768), (g_gate,)),
    )
    d_out = dot_tn(o, dx2).astype(BF)
    zeros = jnp.zeros((5, D), F32)
    last = LastRows()
    input_grad, qkv_back, g_out, g_small, up_back = comm(
        6,
        "ecbbbbbaaccaadbbacdbaaccdddbbcddabdb",
        (last, (d_qkv_low, u_all, w_qkv, hidden_in, d_middle, params)),
        (GradThenSum(D, 768, 4, swap=True), (h1, d_qkv_low)),
        (SumFew(16, D), (d_out,)),
        (SumSmall(last), (jnp.concatenate([zeros, d_gain_two[None], d_shift_two[None], zeros[:1]]),)),
        (Swap(16, 768), (g_up,)),
    )
    block_out, input_grad = block_out.reshape(1, 128, D), input_grad.reshape(1, 128, D)

    small = lax.dynamic_slice_in_dim(g_small, place * 16, 16, axis=1)
    owned = lax.ppermute(
        jnp.concatenate([g_out, jnp.pad(small, ((0, 0), (0, 112)))], axis=1), AXES, TO_OWNER
    )
    g_out, g_small = owned[:, :D].astype(F32), owned[:7, D : D + 16].astype(F32)

    wide = wide_updates(
        (qkv_back, gate_back, up_back),
        (qkv_weight, qkv_first, qkv_second),
        (gate_weight, gate_first, gate_second),
        (up_weight, up_first, up_second),
    )
    updates = (
        wide[0:3],
        adamw(out_weight, out_first, out_second, g_out, (D // 16) ** (-0.5), 0.1),
        wide[3:6],
        wide[6:9],
        adamw(down_weight, down_first, down_second, g_down[:44].astype(F32), FF ** (-0.5), 0.1),
        adamw(small_params, small_first, small_second, g_small, 2.0, 0.0),
    )
    return (block_out, input_grad, *[x for u in updates for x in u])


def solution(mesh):
    fine = Mesh(mesh.devices.reshape(4, 2, 2, 4, 2), AXES)
    tokens = P(("z", "xh"), ("xl", "y", "core"), None)
    marks = P(("z", "xh"), ("xl", "y", "core"))
    rows = P(AXES, None)
    small = P(None, AXES)
    in_specs = (tokens, tokens, marks, marks) + (rows,) * 15 + (small,) * 3
    out_specs = (tokens, tokens) + (rows,) * 15 + (small,) * 3
    return jax.shard_map(local, mesh=fine, in_specs=in_specs, out_specs=out_specs, check_vma=False)
```

```python
import functools
import math

import jax
import jax.numpy as jnp
import numpy as np
from jax import lax
from jax.experimental import pallas as pl
from jax.experimental.pallas import tpu as pltpu
from jax.sharding import Mesh
from jax.sharding import PartitionSpec as P

D = 2048
H = 32
HEAD = 64
FF = 5632
ROT = 16
STEP = 10

NORM_EPS = 1e-05
BETA_ONE = 0.9
BETA_TWO = 0.95
ADAM_EPS = 1e-08
MASKED = -1e30

AXES = ("z", "xh", "xl", "y", "core")
YC = ("y", "core")
ZX = ("z", "xh", "xl")
HALF = 1024
SEQ = 2048
BF = jnp.bfloat16
F32 = jnp.float32


def norm_forward(rows, gain, shift):
    mean = jnp.mean(rows, axis=-1, keepdims=True)
    centred = rows - mean
    scale = lax.rsqrt(jnp.mean(centred * centred, axis=-1, keepdims=True) + NORM_EPS)
    unit = centred * scale
    return (unit * gain + shift, unit, scale)


def norm_backward(gradient, unit, scale, gain):
    along = gradient * gain
    inner = (
        along
        - jnp.mean(along, axis=-1, keepdims=True)
        - unit * jnp.mean(along * unit, axis=-1, keepdims=True)
    )
    return (inner * scale, jnp.sum(gradient * unit, axis=0), jnp.sum(gradient, axis=0))


def adamw(weight, first, second, gradient, rate, decay):
    first_new = BETA_ONE * first + (1.0 - BETA_ONE) * gradient
    second_new = BETA_TWO * second + (1.0 - BETA_TWO) * gradient * gradient
    mean_hat = first_new / (1.0 - BETA_ONE**STEP)
    square_hat = second_new / (1.0 - BETA_TWO**STEP)
    weight_new = weight - rate * (mean_hat / (jnp.sqrt(square_hat) + ADAM_EPS) + decay * weight)
    return (weight_new, first_new, second_new)


def dot_nn(a, b):
    return jnp.dot(a, b, preferred_element_type=F32)


def dot_nt(a, b):
    return lax.dot_general(a, b, (((1,), (1,)), ((), ())), preferred_element_type=F32)


def dot_tn(a, b):
    return lax.dot_general(a, b, (((0,), (0,)), ((), ())), preferred_element_type=F32)


def document_marks(params_ref):
    sequence = lax.axis_index("z") * 2 + lax.axis_index("xh")
    row = params_ref[7:8, pl.ds(pl.multiple_of(sequence * 256, 128), 128)]
    lane = lax.broadcasted_iota(jnp.int32, (1, 128), 1)
    length, high, low = [
        jnp.sum(jnp.where(lane == k, row, 0.0), axis=1, keepdims=True) for k in range(3)
    ]
    return length, high * 64.0 + low


def rotary_angles(params_ref, half):
    length, start = document_marks(params_ref)
    place = lax.broadcasted_iota(jnp.int32, (8, HALF), 1).astype(F32) + half * float(HALF)
    position = jnp.where(place < length, start + place, 4095.0 + place)
    row = lax.broadcasted_iota(jnp.int32, (8, HALF), 0)
    freq = jnp.zeros((8, HALF), F32)
    for k in range(ROT // 2):
        freq = jnp.where(row == k, float(np.float32(10000.0) ** np.float32(-k / (ROT // 2))), freq)
    angle = position * freq
    parts = []
    for value in (jnp.cos(angle), jnp.sin(angle)):
        high = value.astype(BF).astype(F32)
        parts += [high, value - high]
    return jnp.concatenate(parts, axis=0).astype(BF)


def rotary_tables(angles):
    row = lax.broadcasted_iota(jnp.int32, (16, 128), 0) % 8
    lane = lax.broadcasted_iota(jnp.int32, (16, 128), 1) % HEAD
    spread = jnp.where((lane < ROT) & (lane % 8 == row), 1.0, 0.0).astype(BF)
    lane = lax.broadcasted_iota(jnp.int32, (1, 128), 1) % HEAD
    cosine = dot_tn(angles[0:16], spread) + jnp.where(lane < ROT, 0.0, 1.0)
    sine = dot_tn(angles[16:32], spread)
    return cosine, jnp.where(lane < ROT // 2, -sine, 0.0), jnp.where(lane < ROT // 2, 0.0, sine)


def rotate(x, cosine, below, above):
    return x * cosine + pltpu.roll(x, 120, 1) * below + pltpu.roll(x, 8, 1) * above


def remote(src, dst, sems, at, device):
    return pltpu.make_async_remote_copy(
        src_ref=src,
        dst_ref=dst,
        send_sem=sems.at[0, at],
        recv_sem=sems.at[1, at],
        device_id=device,
        device_id_type=pl.DeviceIdType.MESH,
    )


def places():
    y, c, z = lax.axis_index("y"), lax.axis_index("core"), lax.axis_index("z")
    x = lax.axis_index("xh") * 2 + lax.axis_index("xl")
    step = lambda v, k: lax.rem(v + k, 4)
    at_x = lambda v: {"xh": lax.div(v, 2), "xl": lax.rem(v, 2)}
    devices = {
        "twin": {"core": 1 - c},
        "up": {"y": step(y, 1)},
        "down": {"y": step(y, 3)},
        "across": {"y": step(y, 2)},
        "up_twin": {"y": step(y, 1), "core": 1 - c},
        "down_twin": {"y": step(y, 3), "core": 1 - c},
        "across_twin": {"y": step(y, 2), "core": 1 - c},
        "x+": at_x(step(x, 1)),
        "x-": at_x(step(x, 3)),
        "z+": {"z": step(z, 1)},
        "z-": {"z": step(z, 3)},
        "pair": {"xl": 1 - lax.axis_index("xl")},
    }
    return y, c, x, z, devices


def add_low(a, b):
    return (a.astype(F32) + b.astype(F32)).astype(BF)


class RingGather:
    def __init__(self, block, cut, i, plus, minus, sems, base, pending):
        self.lo, self.hi = cut(block(lax.rem(i + 3, 4)))[0], cut(block(lax.rem(i + 1, 4)))[1]
        self.to_plus = remote(block(i), block(i), sems, base, plus)
        self.to_minus = remote(block(i), block(i), sems, base + 1, minus)
        self.pass_plus = remote(self.lo, self.lo, sems, base + 2, plus)
        self.pass_minus = remote(self.hi, self.hi, sems, base + 3, minus)
        pending += [self.to_plus, self.to_minus, self.pass_plus, self.pass_minus]

    def start(self):
        self.to_plus.start()
        self.to_minus.start()

    def before_came(self):
        self.to_plus.wait_recv()
        self.pass_plus.start()

    def after_came(self):
        self.to_minus.wait_recv()
        self.pass_minus.start()

    def finish(self):
        self.pass_plus.wait_recv()
        self.pass_minus.wait_recv()


class RingSum:
    def __init__(self, blocks, cut, plus, minus, acc, near, sems, base, pending):
        across, after, before = blocks
        self.cut, self.after, self.before, self.acc, self.near = cut, after, before, acc, near
        send = lambda src, slot, which, at, device: remote(
            cut(src)[which], cut(near(slot))[which], sems, base + at, device
        )
        self.far_plus = send(across, 0, 0, 0, plus)
        self.far_minus = send(across, 0, 1, 1, minus)
        self.own_plus = send(after, 1, 1, 2, plus)
        self.own_minus = send(before, 2, 0, 3, minus)
        self.sum_plus = send(acc, 1, 0, 4, plus)
        self.sum_minus = send(acc, 2, 1, 5, minus)
        self.coming = [self.own_plus, self.own_minus, self.sum_plus, self.sum_minus]
        pending += [self.far_plus, self.far_minus] + self.coming

    def far(self):
        self.far_plus.start()
        self.far_minus.start()

    def own(self):
        self.own_plus.start()
        self.own_minus.start()

    def middle(self):
        near = self.near(0)
        self.far_plus.wait_recv()
        self.cut(self.acc)[0][...] = add_low(self.cut(self.after)[0][...], self.cut(near)[0][...])
        self.sum_plus.start()
        self.far_minus.wait_recv()
        self.cut(self.acc)[1][...] = add_low(self.cut(self.before)[1][...], self.cut(near)[1][...])
        self.sum_minus.start()

    def finish(self, mine):
        for copy in self.coming:
            copy.wait_recv()
        total = mine[...].astype(F32) + self.near(1)[...].astype(F32) + self.near(2)[...].astype(F32)
        return total.astype(BF)


def ring_gather(block, cut, i, plus, minus, sems, base, pending):
    before, after = lax.rem(i + 3, 4), lax.rem(i + 1, 4)
    to_plus = remote(block(i), block(i), sems, base, plus)
    to_minus = remote(block(i), block(i), sems, base + 1, minus)
    to_plus.start()
    to_minus.start()
    yield
    to_plus.wait_recv()
    lo = cut(block(before))[0]
    pass_plus = remote(lo, lo, sems, base + 2, plus)
    pass_plus.start()
    yield
    to_minus.wait_recv()
    hi = cut(block(after))[1]
    pass_minus = remote(hi, hi, sems, base + 3, minus)
    pass_minus.start()
    pending += [to_plus, to_minus, pass_plus, pass_minus]
    yield
    pass_plus.wait_recv()
    pass_minus.wait_recv()


def ring_scatter(block, cut, i, plus, minus, acc, near, sems, base, pending):
    before, after, across = lax.rem(i + 3, 4), lax.rem(i + 1, 4), lax.rem(i + 2, 4)
    lo, hi = (lambda v: cut(v)[0]), (lambda v: cut(v)[1])
    far_plus = remote(lo(block(across)), lo(near.at[0]), sems, base, plus)
    far_minus = remote(hi(block(across)), hi(near.at[0]), sems, base + 1, minus)
    own_plus = remote(hi(block(after)), hi(near.at[1]), sems, base + 2, plus)
    own_minus = remote(lo(block(before)), lo(near.at[2]), sems, base + 3, minus)
    for copy in (far_plus, far_minus, own_plus, own_minus):
        copy.start()
    yield
    far_plus.wait_recv()
    lo(acc)[...] = add_low(lo(block(after))[...], lo(near.at[0])[...])
    sum_plus = remote(lo(acc), lo(near.at[1]), sems, base + 4, plus)
    sum_plus.start()
    yield
    far_minus.wait_recv()
    hi(acc)[...] = add_low(hi(block(before))[...], hi(near.at[0])[...])
    sum_minus = remote(hi(acc), hi(near.at[2]), sems, base + 5, minus)
    sum_minus.start()
    pending += [far_plus, far_minus, own_plus, own_minus, sum_plus, sum_minus]
    yield
    for copy in (own_plus, own_minus, sum_plus, sum_minus):
        copy.wait_recv()


class GatherTokens:
    peers = ("twin", "up", "down")
    n_sems = 10

    def __init__(self, rows, width, normalize=False, far=False):
        self.ins = [((rows, width), BF, "far")] if far else [((rows, width), BF)]
        self.outs = [((8, rows, width), BF, "far")] if far else [((8, rows, width), BF)]
        self.scratch = [pltpu.VMEM((rows, width), BF)] if normalize else []
        self.rows = rows

    def run(self, ins, outs, scratch, sems, base, place, pending):
        y, c, _, _, to = place
        (x_ref,), (out_ref,) = ins, outs
        if scratch:
            rows = x_ref[...].astype(F32)
            centred = rows - jnp.mean(rows, axis=-1, keepdims=True)
            spread = jnp.mean(centred * centred, axis=-1, keepdims=True)
            (x_ref,) = scratch
            x_ref[...] = (centred * lax.rsqrt(spread + NORM_EPS)).astype(BF)
            yield
        half = self.rows // 2
        lo, hi = pl.ds(0, half), pl.ds(half, half)
        at = lambda k: lax.rem(y + k, 4) * 2 + c
        mine = pltpu.make_async_copy(x_ref, out_ref.at[at(0)], sems.at[0, base + 9])
        s_up = remote(x_ref, out_ref.at[at(0)], sems, base, to["up"])
        s_down = remote(x_ref, out_ref.at[at(0)], sems, base + 1, to["down"])
        s_twin = remote(x_ref, out_ref.at[at(0)], sems, base + 2, to["twin"])
        for copy in (s_up, s_down, s_twin, mine):
            copy.start()
        pass_on = lambda ref, k, device: remote(ref, ref, sems, base + k, to[device])
        yield
        s_up.wait_recv()
        r_up = pass_on(out_ref.at[at(3), lo], 3, "up")
        t_down = pass_on(out_ref.at[at(3)], 5, "twin")
        r_up.start()
        t_down.start()
        yield
        s_down.wait_recv()
        r_down = pass_on(out_ref.at[at(1), hi], 4, "down")
        t_up = pass_on(out_ref.at[at(1)], 6, "twin")
        r_down.start()
        t_up.start()
        yield
        r_up.wait_recv()
        t_lo = pass_on(out_ref.at[at(2), lo], 7, "twin")
        t_lo.start()
        yield
        r_down.wait_recv()
        t_hi = pass_on(out_ref.at[at(2), hi], 8, "twin")
        t_hi.start()
        pending += [s_up, s_down, s_twin, r_up, r_down, t_down, t_up, t_lo, t_hi]
        yield
        for copy in (s_twin, t_down, t_up, t_lo, t_hi):
            copy.wait_recv()
        mine.wait()


class SumTokens:
    peers = ("twin", "up", "down")
    n_sems = 10
    steps = (2, 1, 3, 0)

    def __init__(self, rows, width, plus=False):
        self.ins = [((8, rows, width), BF)] + [((rows, width), F32)] * plus
        self.outs = [((rows, width), BF if plus else F32)]
        self.scratch = [
            pltpu.VMEM((4, rows, width), BF),
            pltpu.VMEM((3, rows, width), BF),
            pltpu.VMEM((rows, width), BF),
            pltpu.VMEM((3, rows, width), BF),
        ]
        self.rows = rows

    def swap(self, k, p_ref, scratch, sems, base, place):
        y, c, _, _, to = place
        at = lax.rem(y + self.steps[k], 4) * 2
        copy = remote(p_ref.at[at + 1 - c], scratch[0].at[k], sems, base + k, to["twin"])
        copy.start()
        return copy

    def rest(self, swaps, p_ref, out_ref, extra, scratch, sems, base, place, pending):
        y, c, _, _, to = place
        from_twin, pair, acc, near = scratch
        half = self.rows // 2
        cut = lambda v: (v.at[pl.ds(0, half)], v.at[pl.ds(half, half)])

        def send(block, slot, which, at, device):
            copy = remote(cut(block)[which], cut(near.at[slot])[which], sems, base + at, to[device])
            copy.start()
            return copy

        for k, off in enumerate(self.steps[:3]):
            swaps[k].wait_recv()
            pair[k] = add_low(p_ref[lax.rem(y + off, 4) * 2 + c], from_twin[k])
            if k == 0:
                far_plus = send(pair.at[0], 0, 0, 4, "up")
                far_minus = send(pair.at[0], 0, 1, 5, "down")
            elif k == 1:
                own_plus = send(pair.at[1], 1, 1, 6, "up")
            else:
                own_minus = send(pair.at[2], 2, 0, 7, "down")
        yield
        far_plus.wait_recv()
        cut(acc)[0][...] = add_low(cut(pair.at[1])[0][...], cut(near.at[0])[0][...])
        sum_plus = send(acc, 1, 0, 8, "up")
        yield
        far_minus.wait_recv()
        cut(acc)[1][...] = add_low(cut(pair.at[2])[1][...], cut(near.at[0])[1][...])
        sum_minus = send(acc, 2, 1, 9, "down")
        swaps[3].wait_recv()
        total = p_ref[y * 2 + c].astype(F32) + from_twin[3].astype(F32)
        if extra is not None:
            total = total + extra[...]
        pending += list(swaps) + [far_plus, far_minus, own_plus, own_minus, sum_plus, sum_minus]
        yield
        for copy in (own_plus, own_minus, sum_plus, sum_minus):
            copy.wait_recv()
        total = total + (near[1].astype(F32) + near[2].astype(F32))
        out_ref[...] = total.astype(out_ref.dtype)

    def run(self, ins, outs, scratch, sems, base, place, pending):
        swaps = [self.swap(k, ins[0], scratch, sems, base, place) for k in range(4)]
        yield
        extra = ins[1] if len(ins) > 1 else None
        yield from self.rest(swaps, ins[0], outs[0], extra, scratch, sems, base, place, pending)


class LastRows:
    peers = SumTokens.peers
    n_sems = SumTokens.n_sems

    def __init__(self):
        self.sum = SumTokens(128, D)
        self.ins = [
            ((HALF, 768), BF),
            ((HALF, D), BF),
            ((D, 896), BF),
            ((128, D), BF),
            ((128, D), F32),
            ((16, D), F32),
        ]
        self.outs = [((128, D), F32)]
        self.scratch = [
            pltpu.VMEM((8, 128, D), BF),
            pltpu.VMEM((128, D), F32),
            pltpu.VMEM((8, D), F32),
            pltpu.VMEM((8, 768), F32),
        ] + self.sum.scratch

    def run(self, ins, outs, scratch, sems, base, place, pending):
        d_ref, u_ref, w_ref, x_ref, d_middle_ref, params_ref = ins
        p_ref, total_ref, norm_ref, bias_ref = scratch[:4]
        self.sums = norm_ref, bias_ref
        y, c = place[:2]
        norm_ref[...] = jnp.zeros_like(norm_ref)
        bias_ref[...] = jnp.zeros_like(bias_ref)

        def two_blocks(at):
            rows = pl.ds(pl.multiple_of(at * 128, 256), 256)
            d = d_ref[rows, :]
            dh = dot_nt(d, w_ref[:, 0:768])
            p_ref[pl.ds(at, 2)] = dh.astype(BF).reshape(2, 128, D)
            norm_ref[0:1] += jnp.sum(dh * u_ref[rows, :].astype(F32), axis=0, keepdims=True)
            norm_ref[1:2] += jnp.sum(dh, axis=0, keepdims=True)
            bias_ref[0:1] += jnp.sum(d.astype(F32), axis=0, keepdims=True)

        swaps = []
        for k, off in enumerate(self.sum.steps):
            at = lax.rem(y + off, 4) * 2
            two_blocks(at)
            swaps.append(self.sum.swap(k, p_ref, scratch[4:], sems, base, place))
            yield
        yield from self.sum.rest(
            swaps, p_ref, total_ref, None, scratch[4:], sems, base, place, pending
        )
        rows = x_ref[...].astype(F32)
        centred = rows - jnp.mean(rows, axis=-1, keepdims=True)
        scale = lax.rsqrt(jnp.mean(centred * centred, axis=-1, keepdims=True) + NORM_EPS)
        unit = centred * scale
        along = total_ref[...] * params_ref[0:1]
        inner = (
            along
            - jnp.mean(along, axis=-1, keepdims=True)
            - unit * jnp.mean(along * unit, axis=-1, keepdims=True)
        )
        outs[0][...] = d_middle_ref[...] + inner * scale


def rows_or_columns(rows, width):
    if rows % 32 == 0:
        return lambda v: (v.at[pl.ds(0, rows // 2)], v.at[pl.ds(rows // 2, rows // 2)])
    return lambda v: (v.at[:, pl.ds(0, width // 2)], v.at[:, pl.ds(width // 2, width // 2)])


class GatherWeights:
    peers = ("x+", "x-", "z+", "z-")
    n_sems = 41

    def __init__(self, rows, width):
        self.ins = [((rows, width), BF)]
        self.outs = [((4, 4, rows, width), BF)]
        self.scratch = []
        self.rows, self.width = rows, width

    def rings(self, out_ref, sems, base, place, pending):
        _, _, x, z, to = place
        first = self.width // 256 * 128

        def one(order, base):
            width = self.width - first if order else first
            part = pl.ds(order * first, width)
            cut = rows_or_columns(self.rows, width)
            if order == 0:
                block = lambda k, j: out_ref.at[k, j, pl.ds(0, self.rows), part]
                i, k, ring, other = x, z, (to["x+"], to["x-"]), (to["z+"], to["z-"])
            else:
                block = lambda k, j: out_ref.at[j, k, pl.ds(0, self.rows), part]
                i, k, ring, other = z, x, (to["z+"], to["z-"]), (to["x+"], to["x-"])
            main = RingGather(lambda j: block(k, j), cut, i, *ring, sems, base, pending)
            mine, after, across, before = [
                RingGather(
                    lambda q, j=lax.rem(i + n, 4): block(q, j), cut, k, *other, sems, base + 4 + 4 * n, pending
                )
                for n in range(4)
            ]
            main.start()
            mine.start()
            yield
            main.before_came()
            before.start()
            yield
            main.after_came()
            after.start()
            yield
            mine.before_came()
            mine.after_came()
            yield
            main.finish()
            across.start()
            yield
            for part_ring in (before, after):
                part_ring.before_came()
                part_ring.after_came()
            yield
            across.before_came()
            across.after_came()
            yield
            for part_ring in (mine, before, after, across):
                part_ring.finish()

        yield from both(one(0, base), one(1, base + 20))

    def run(self, ins, outs, scratch, sems, base, place, pending):
        _, _, x, z, _ = place
        (x_ref,), (out_ref,) = ins, outs
        mine = pltpu.make_async_copy(x_ref, out_ref.at[z, x], sems.at[0, base + 40])
        mine.start()
        mine.wait()
        yield from self.rings(out_ref, sems, base, place, pending)


class SumWeights:
    peers = ("x+", "x-", "z+", "z-")
    n_sems = 60

    def __init__(self, rows, width):
        self.ins = [((4, 4, rows, width), BF)]
        self.outs = [((rows, width), BF)]
        self.rows, self.width = rows, width
        first = width // 256 * 128
        self.widths = (first, width - first)
        self.scratch = []
        for w in self.widths:
            self.scratch += [
                pltpu.VMEM((4, rows, w), BF),
                pltpu.VMEM((3, 4, rows, w), BF),
                pltpu.VMEM((4, rows, w), BF),
                pltpu.VMEM((rows, w), BF),
                pltpu.VMEM((3, rows, w), BF),
            ]

    def run(self, ins, outs, scratch, sems, base, place, pending):
        _, _, x, z, to = place
        (p_ref,), (out_ref,) = ins, outs
        every = pl.ds(0, self.rows)

        def one(order, bufs, base):
            acc, near, total, acc_two, near_two = bufs
            width = self.widths[order]
            part = pl.ds(order * self.widths[0], width)
            cut = rows_or_columns(self.rows, width)
            if order == 0:
                block = lambda k, j: p_ref.at[k, j, every, part]
                i, k, ring, other = x, z, (to["x+"], to["x-"]), (to["z+"], to["z-"])
            else:
                block = lambda k, j: p_ref.at[j, k, every, part]
                i, k, ring, other = z, x, (to["z+"], to["z-"]), (to["x+"], to["x-"])
            firsts = []
            for n, off in enumerate((2, 1, 3, 0)):
                at = lax.rem(k + off, 4)
                blocks = [block(at, lax.rem(i + m, 4)) for m in (2, 1, 3)]
                firsts.append(
                    RingSum(
                        blocks, cut, *ring, acc.at[n], lambda s, n=n: near.at[s, n], sems, base + 6 * n, pending
                    )
                )
            second = RingSum(
                [total.at[n] for n in range(3)], cut, *other, acc_two, lambda s: near_two.at[s], sems,
                base + 24, pending,
            )

            def complete(n):
                total[n] = firsts[n].finish(block(lax.rem(k + (2, 1, 3, 0)[n], 4), i))

            for one_ring in firsts:
                one_ring.far()
                one_ring.own()
            yield
            firsts[0].middle()
            firsts[1].middle()
            yield
            firsts[2].middle()
            firsts[3].middle()
            yield
            complete(0)
            second.far()
            yield
            complete(1)
            complete(2)
            second.own()
            yield
            second.middle()
            complete(3)
            yield
            out_ref[every, part] = second.finish(total.at[3])

        yield from both(one(0, scratch[:5], base), one(1, scratch[5:], base + 30))


def firsts(v):
    return v.at[pl.ds(0, 2)], v.at[pl.ds(2, 2)]


class GatherSmall:
    peers = ("x+", "x-", "z+", "z-")
    n_sems = 17

    def __init__(self, rows, width):
        self.ins = [((rows, width), BF)]
        self.outs = [((4, 4, rows, width), BF)]
        self.scratch = []
        self.rows, self.width = rows, width

    def rings(self, out_ref, sems, base, place, pending):
        _, _, x, z, to = place
        first = self.width // 256 * 128
        a, b = pl.ds(0, first), pl.ds(first, self.width - first)
        every = pl.ds(0, self.rows)
        cut_a = rows_or_columns(self.rows, first)
        cut_b = rows_or_columns(self.rows, self.width - first)

        def along_x_first():
            yield from ring_gather(
                lambda j: out_ref.at[z, j, every, a], cut_a, x, to["x+"], to["x-"], sems, base, pending
            )
            yield from ring_gather(
                lambda j: out_ref.at[j, pl.ds(0, 4), every, a], firsts, z, to["z+"], to["z-"], sems, base + 4,
                pending,
            )

        def along_z_first():
            yield from ring_gather(
                lambda j: out_ref.at[j, x, every, b], cut_b, z, to["z+"], to["z-"], sems, base + 8, pending
            )
            yield from ring_gather(
                lambda j: out_ref.at[pl.ds(0, 4), j, every, b], firsts, x, to["x+"], to["x-"], sems,
                base + 12, pending,
            )

        yield from both(along_x_first(), along_z_first())

    def run(self, ins, outs, scratch, sems, base, place, pending):
        _, _, x, z, _ = place
        (x_ref,), (out_ref,) = ins, outs
        mine = pltpu.make_async_copy(x_ref, out_ref.at[z, x], sems.at[0, base + 16])
        mine.start()
        mine.wait()
        yield from self.rings(out_ref, sems, base, place, pending)


class SumFew:
    peers = ("x+", "x-", "z+", "z-")
    n_sems = 24

    def __init__(self, rows, width):
        self.ins = [((4, 4, rows, width), BF)]
        self.outs = [((rows, width), BF)]
        self.rows, self.width = rows, width
        first = width // 256 * 128
        self.widths = (first, width - first)
        self.scratch = []
        for w in self.widths:
            self.scratch += [
                pltpu.VMEM((4, rows, w), BF),
                pltpu.VMEM((3, 4, rows, w), BF),
                pltpu.VMEM((4, rows, w), BF),
                pltpu.VMEM((rows, w), BF),
                pltpu.VMEM((3, rows, w), BF),
            ]

    def run(self, ins, outs, scratch, sems, base, place, pending):
        _, _, x, z, to = place
        (p_ref,), (out_ref,) = ins, outs
        every = pl.ds(0, self.rows)

        def one(order, bufs, base):
            acc, near, total, acc_two, near_two = bufs
            width = self.widths[order]
            columns = pl.ds(order * self.widths[0], width)
            cut = rows_or_columns(self.rows, width)
            four = pl.ds(0, 4)
            if order == 0:
                block = lambda j: p_ref.at[four, j, every, columns]
                i, k, far, close = x, z, ("x+", "x-"), ("z+", "z-")
            else:
                block = lambda j: p_ref.at[j, four, every, columns]
                i, k, far, close = z, x, ("z+", "z-"), ("x+", "x-")
            yield from ring_scatter(
                block, firsts, i, to[far[0]], to[far[1]], acc, near, sems, base, pending
            )
            total[...] = (
                block(i)[...].astype(F32) + near[1].astype(F32) + near[2].astype(F32)
            ).astype(BF)
            yield from ring_scatter(
                lambda j: total.at[j], cut, k, to[close[0]], to[close[1]], acc_two, near_two, sems,
                base + 6, pending,
            )
            out_ref[every, columns] = (
                total[k].astype(F32) + near_two[1].astype(F32) + near_two[2].astype(F32)
            ).astype(BF)

        yield from both(one(0, scratch[:5], base), one(1, scratch[5:], base + 12))


class Swap:
    peers = ("twin", "up", "down", "across", "up_twin", "down_twin", "across_twin")
    n_sems = 8
    steps = ((0, 1), (1, 0), (3, 0), (2, 0), (1, 1), (3, 1), (2, 1))

    def __init__(self, rows, width):
        self.ins = [((8, rows, width), BF)]
        self.outs = [((8, rows, width), BF)]
        self.scratch = []

    def send(self, x_ref, out_ref, sems, base, place):
        y, c, _, _, to = place
        me = y * 2 + c
        copies = [pltpu.make_async_copy(x_ref.at[me], out_ref.at[me], sems.at[0, base + 7])]
        for k, (name, (up, other)) in enumerate(zip(self.peers, self.steps)):
            at = lax.rem(y + up, 4) * 2 + (1 - c if other else c)
            copies.append(remote(x_ref.at[at], out_ref.at[me], sems, base + k, to[name]))
        for copy in copies:
            copy.start()
        return copies

    def run(self, ins, outs, scratch, sems, base, place, pending):
        copies = self.send(ins[0], outs[0], sems, base, place)
        yield
        copies[0].wait()
        for copy in copies[1:]:
            copy.wait_recv()
        pending += copies[1:]


def columns(at, width):
    return slice(at, at + width)


class ShareQkv:
    peers = Swap.peers + GatherWeights.peers

    def __init__(self):
        self.swap = Swap(16, 896)
        self.gather = GatherWeights(128, 896)
        self.ins = [((16, 6144), F32, "far"), ((16, 128), BF)]
        self.outs = [(*self.gather.outs[0], "far"), ((16, 16 * 128), F32)]
        self.scratch = [pltpu.VMEM((8, 16, 896), BF)] * 2
        self.n_sems = 16 + self.gather.n_sems

    def run(self, ins, outs, scratch, sems, base, place, pending):
        _, _, x, z, _ = place
        weight_ref, tile_ref = ins
        (out_ref, tiles_ref), (piece, landed) = outs, scratch
        for k in range(8):
            for pair in range(2):
                for kind in range(3):
                    piece[k, :, columns(pair * 384 + kind * 128, 128)] = weight_ref[
                        :, columns(kind * D + k * 256 + pair * 128, 128)
                    ].astype(BF)
            piece[k, :, columns(768, 128)] = tile_ref[...]
        yield from self.swap.run((piece,), (landed,), (), sems, base, place, pending)
        for k in range(8):
            out_ref[z, x, columns(k * 16, 16)] = landed[k]
        yield from self.gather.rings(out_ref, sems, base + 16, place, pending)
        for k in range(16):
            tiles = [
                out_ref[k // 4, k % 4, columns(j * 16, 16), columns(768, 128)].astype(F32)
                for j in range(8)
            ]
            tiles_ref[:, columns(k * 128, 128)] = sum(tiles[1:], tiles[0])


def moved(read, tile, pieces, last):
    lane = lax.broadcasted_iota(jnp.int32, (16, 128), 1)
    value = jnp.zeros((16, 128), F32)
    for there, source, here, width in pieces:
        at = there - tile * 128
        if at + width <= 0 or at >= 128:
            continue
        start = min(here // 128 * 128, last)
        window = read(source, columns(start, 256)).astype(F32)
        shift = (at - (here - start)) % 256
        window = (pltpu.roll(window, shift, 1) if shift else window)[:, 0:128]
        value = jnp.where((lane >= at) & (lane < at + width), window, value)
    return value


class ShareHidden:
    peers = Swap.peers

    def __init__(self):
        self.swap = Swap(16, 1536)
        self.ins = [((16, FF), F32, "far")] * 2
        self.outs = self.swap.outs
        self.scratch = [pltpu.VMEM((8, 16, 1536), BF)]
        self.n_sems = self.swap.n_sems

    def run(self, ins, outs, scratch, sems, base, place, pending):
        (piece,) = scratch
        for k in range(8):
            pieces = [(j * 48, None, (j * 8 + k) * 44, 44) for j in range(16)]
            for w, ref in enumerate(ins):
                for tile in range(6):
                    value = moved(lambda _, at: ref[:, at], tile, pieces, FF - 256)
                    piece[k, :, columns(w * 768 + tile * 128, 128)] = value.astype(BF)
            yield
        yield from self.swap.run((piece,), outs, (), sems, base, place, pending)


class TokenSums:
    peers = ()
    n_sems = 0

    def __init__(self, rows, width, count, step=256):
        self.ins = [((HALF, rows), BF)] + [((HALF, width), BF)] * count
        self.outs = [((rows, width), BF)] * count
        self.scratch = []
        self.steps = [pl.ds(k, step) for k in range(0, rows, step)]

    def run(self, ins, outs, scratch, sems, base, place, pending):
        for columns in self.steps:
            for b_ref, out_ref in zip(ins[1:], outs):
                out_ref[columns, :] = dot_tn(ins[0][:, columns], b_ref[...]).astype(BF)
            yield


class GradThenSum:
    peers = SumWeights.peers

    def __init__(self, rows, width, steps, swap=False):
        self.sum = SumWeights(rows // 16, width)
        self.swap = Swap(rows // 128, width) if swap else None
        self.ins = [((HALF, rows), BF), ((HALF, width), BF)]
        self.outs = self.swap.outs if swap else self.sum.outs
        self.scratch = [pltpu.VMEM((4, 4, rows // 16, width), BF)] + self.sum.scratch
        self.n_sems = self.sum.n_sems
        if swap:
            self.peers = Swap.peers + SumWeights.peers
            self.scratch += [pltpu.VMEM((rows // 16, width), BF), pltpu.VMEM((8, rows // 128, width), BF)]
            self.n_sems += 8
        self.rows, self.steps = rows, steps

    def run(self, ins, outs, scratch, sems, base, place, pending):
        terms = scratch[0]
        block, step = self.rows // 16, self.rows // self.steps
        for k in range(self.steps):
            part = dot_tn(ins[0][:, columns(k * step, step)], ins[1][...]).astype(BF)
            for j in range(step // block):
                at = k * step // block + j
                terms[at // 4, at % 4] = part[columns(j * block, block)]
            yield
        if self.swap is None:
            yield from self.sum.run((terms,), outs, scratch[1:], sems, base, place, pending)
            return
        *buffers, total, piece = scratch[1:]
        yield from self.sum.run((terms,), (total,), buffers, sems, base, place, pending)
        count = self.rows // 128
        for k in range(8):
            piece[k] = total[columns(k * count, count)]
        at = base + self.sum.n_sems
        yield from self.swap.run((piece,), outs, (), sems, at, place, pending)


class Product:
    peers = ()
    n_sems = 0

    def __init__(self, depth, width):
        self.ins = [((HALF, depth), BF), ((depth, width), BF)]
        self.outs = [((HALF, width), BF)]
        self.scratch = []

    def run(self, ins, outs, scratch, sems, base, place, pending):
        for k in range(0, HALF, 256):
            outs[0][pl.ds(k, 256), :] = dot_nn(ins[0][pl.ds(k, 256), :], ins[1][...]).astype(BF)
            yield


class SumSmall:
    peers = Swap.peers + SumFew.peers

    def __init__(self, last):
        self.last = last
        self.swap = Swap(16, 512)
        self.sum = SumFew(16, 512)
        self.ins = [((8, D), F32)]
        self.outs = self.sum.outs
        self.scratch = [
            pltpu.VMEM((8, 16, 512), F32),
            pltpu.VMEM((8, 16, 512), BF),
            pltpu.VMEM((8, 16, 512), BF),
            pltpu.VMEM((4, 4, 16, 512), BF),
        ] + self.sum.scratch
        self.n_sems = 8 + self.sum.n_sems

    def run(self, ins, outs, scratch, sems, base, place, pending):
        wide, piece, landed, spread = scratch[:4]
        norm_ref, bias_ref = self.last.sums
        yc = place[0] * 2 + place[1]
        wide[...] = jnp.zeros_like(wide)
        for k in range(8):
            at = columns(k * 256, 256)
            wide[k, 0:8, 0:256] = ins[0][:, at]
            wide[k, 0:2, 0:256] = norm_ref[0:2, at]
        for pair in range(2):
            for kind in range(3):
                wide[yc, 2 + kind : 3 + kind, columns(pair * 128, 128)] = bias_ref[
                    0:1, columns((pair * 3 + kind) * 128, 128)
                ]
        piece[...] = wide[...].astype(BF)
        yield from self.swap.run((piece,), (landed,), (), sems, base, place, pending)
        total = jnp.sum(landed[...].astype(F32), axis=0).astype(BF)
        spread[...] = jnp.broadcast_to(total[None, None], spread.shape)
        yield from self.sum.run((spread,), outs, scratch[4:], sems, base + 8, place, pending)


def both(*parts):
    parts = list(parts)
    while parts:
        for part in list(parts):
            try:
                next(part)
            except StopIteration:
                parts.remove(part)
        yield


def in_order(parts, order):
    for letter in order:
        next(parts["abcdef".index(letter)], None)
    for _ in both(*parts):
        pass


def size(shape, dtype):
    return math.prod(shape) * jnp.dtype(dtype).itemsize


def far(part, *which):
    part.ins = [(*spec[:2], "far") if k in which else spec for k, spec in enumerate(part.ins)]
    return part


def loaded(part, copies):
    for copy in copies:
        copy.wait()
    yield from part


def stored(part, copies):
    yield from part
    for copy in copies:
        copy.start()


def comm_kernel(parts, order, *refs):
    *refs, sems, move_sems = refs
    refs = list(refs)
    take = lambda count: [refs.pop(0) for _ in range(count)]
    ins = [take(len(p.ins)) for p in parts]
    outs = [take(len(p.outs)) for p in parts]
    scratch = [take(len(p.scratch)) for p in parts]
    loads, stores, moves = [], [], 0
    for p, p_ins, p_outs in zip(parts, ins, outs):
        for refs_of, specs, copies in ((p_ins, p.ins, loads), (p_outs, p.outs, stores)):
            copies.append([])
            for k, spec in enumerate(specs):
                if len(spec) > 2:
                    far, near = refs_of[k], refs.pop(0)
                    ends = (far, near) if copies is loads else (near, far)
                    copies[-1].append(pltpu.make_async_copy(*ends, move_sems.at[moves]))
                    moves += 1
                    refs_of[k] = near
    for copy in sum(loads, []):
        copy.start()
    place = places()
    names = []
    for p in parts:
        names += [n for n in p.peers if n not in names]
    barrier = pltpu.get_barrier_semaphore()
    for name in names:
        pl.semaphore_signal(
            barrier, inc=1, device_id=place[4][name], device_id_type=pl.DeviceIdType.MESH
        )
    pl.semaphore_wait(barrier, len(names))
    base, running, pending = 0, [], []
    for k, p in enumerate(parts):
        p.held = outs[k]
        steps = p.run(ins[k], outs[k], scratch[k], sems, base, place, pending)
        running.append(stored(loaded(steps, loads[k]), stores[k]))
        base += p.n_sems
    in_order(running, order)
    for copy in pending:
        copy.wait_send()
    for copy in sum(stores, []):
        copy.wait()


def comm(collective_id, order, *pairs):
    parts = [p for p, _ in pairs]
    operands = [x.reshape(spec[0]) for p, xs in pairs for x, spec in zip(xs, p.ins)]
    operands = [
        pltpu.with_memory_space_constraint(x, pltpu.HBM) if len(spec) > 2 else x
        for x, spec in zip(operands, [spec for p in parts for spec in p.ins])
    ]
    in_specs = [spec for p in parts for spec in p.ins]
    out_specs = [spec for p in parts for spec in p.outs]
    marked = [spec for p in parts for spec in (*p.ins, *p.outs) if len(spec) > 2]
    where = lambda spec: pl.BlockSpec(memory_space=pltpu.HBM if len(spec) > 2 else pltpu.VMEM)
    held = sum(size(*spec[:2]) for spec in in_specs + out_specs)
    held += sum(size(s.shape, s.dtype) for p in parts for s in p.scratch)
    sent = sum(math.prod(spec[0]) for spec in out_specs) * 2
    return pl.pallas_call(
        functools.partial(comm_kernel, parts, order),
        out_shape=[(pltpu.HBM if len(spec) > 2 else jax.ShapeDtypeStruct)(*spec[:2]) for spec in out_specs],
        in_specs=[where(spec) for spec in in_specs],
        out_specs=[where(spec) for spec in out_specs],
        scratch_shapes=[s for p in parts for s in p.scratch]
        + [pltpu.VMEM(*spec[:2]) for spec in marked]
        + [
            pltpu.SemaphoreType.DMA((2, sum(p.n_sems for p in parts))),
            pltpu.SemaphoreType.DMA((max(1, len(marked)),)),
        ],
        compiler_params=pltpu.CompilerParams(
            collective_id=collective_id, has_side_effects=True, vmem_limit_bytes=held + (8 << 20)
        ),
        cost_estimate=pl.CostEstimate(flops=0, bytes_accessed=20 * sent, transcendentals=0),
    )(*operands)


ROWS = 256


class MakeQkv:
    peers = ()
    n_sems = 0

    def __init__(self, weights, units):
        self.weights, self.units = weights, units
        self.ins = []
        self.outs = [((HALF, D), BF), ((HALF, 768), BF), ((2, 32, HALF), BF)]
        self.scratch = []

    def run(self, ins, outs, scratch, sems, base, place, pending):
        h_ref, out_ref, angles_ref = outs
        w_ref, params_ref = self.weights.held
        (u_ref,) = self.units.held
        yc = place[0] * 2 + place[1]
        xl = lax.axis_index("xl")
        for half in range(2):
            angles_ref[half] = rotary_angles(params_ref, half)
        weight = w_ref[:, :, :, 0:768].reshape(D, 768)
        for k in range(4):
            rows = columns(k * ROWS, ROWS)
            unit = u_ref[2 * k : 2 * k + 2].reshape(ROWS, D).astype(F32)
            h = (unit * params_ref[0:1] + params_ref[1:2]).astype(BF)
            h_ref[rows, :] = h
            mixed = dot_nn(h, weight)
            tables = rotary_tables(angles_ref[xl, :, rows])
            for j in range(6):
                pair, kind = j // 3, j % 3
                at = pl.ds(pl.multiple_of(yc * 256 + pair * 128, 128), 128)
                part = mixed[:, columns(j * 128, 128)] + params_ref[2 + kind : 3 + kind, at]
                if kind < 2:
                    part = rotate(part, *tables)
                out_ref[rows, columns(j * 128, 128)] = part.astype(BF)
        yield


def rowwise(width):
    return pl.BlockSpec((ROWS, width), lambda i: (i, 0))


def fixed(*shape):
    return pl.BlockSpec(shape, lambda i: (0,) * len(shape), pipeline_mode=pl.Buffered(1))


BLOCK = 512
Q, K, V = slice(0, 128), slice(128, 256), slice(256, 384)


def only(x, h):
    lane = lax.broadcasted_iota(jnp.int32, (1, 128), 1)
    return jnp.where((lane >= h * HEAD) & (lane < (h + 1) * HEAD), x, jnp.zeros_like(x))


def rows_of(k):
    return slice(k * BLOCK, (k + 1) * BLOCK)


def allowed_mask(first_len, key_half, kb, query_half, qb, diagonal):
    key = lax.broadcasted_iota(jnp.int32, (BLOCK, BLOCK), 0) + kb * BLOCK
    query = lax.broadcasted_iota(jnp.int32, (BLOCK, BLOCK), 1) + qb * BLOCK
    allowed = None
    if diagonal and kb == qb:
        allowed = key <= query
    if kb == 0:
        length = first_len.astype(jnp.int32)
        same = (key + key_half * HALF >= length) | (query + query_half * HALF < length)
        allowed = same if allowed is None else allowed & same
    return allowed


def lanes(at, width):
    return pl.ds(pl.multiple_of(at * width, 128), width)


class Attend:
    peers = ("pair",)
    n_sems = 6

    def __init__(self):
        self.ins = [((16, D), F32), ((HALF, 768), BF)]
        self.outs = [
            ((HALF, 256), BF),
            ((2, 128, HALF), F32),
            ((2, 8, HALF), F32),
            ((2, HALF, 384), BF),
        ]
        self.scratch = [pltpu.VMEM((2, 8, HALF), F32), pltpu.VMEM((2, HALF, 128), BF)]

    def run(self, ins, outs, scratch, sems, base, place, pending):
        params_ref, qkv_ref = ins
        o_ref, acc_ref, top_ref, x_ref = outs
        total_ref, half_ref = scratch
        pair = place[4]["pair"]
        xl = lax.axis_index("xl")
        first_len = document_marks(params_ref)[0]
        sent = []
        for b in range(2):
            copy = remote(
                qkv_ref.at[rows_of(b), lanes(1 - xl, 384)], x_ref.at[xl, rows_of(b)], sems, base + b, pair
            )
            copy.start()
            sent.append(copy)
        kept = pltpu.make_async_copy(qkv_ref.at[:, lanes(xl, 384)], x_ref.at[xl], sems.at[0, base + 2])
        kept.start()
        kept.wait()
        yield

        def block(query_half, key_half, qb, h, state, diagonal):
            qs = rows_of(qb)
            qh = only(x_ref[query_half, qs, Q] * jnp.asarray(HEAD**-0.5, BF), h)
            top, total, acc = state
            for kb in range(qb + 1 if diagonal else 2):
                ks = rows_of(kb)
                scores = dot_nt(x_ref[key_half, ks, K], qh)
                allowed = allowed_mask(first_len, key_half, kb, query_half, qb, diagonal)
                if allowed is not None:
                    scores = jnp.where(allowed, scores, MASKED)
                new_top = jnp.maximum(top, jnp.max(scores, axis=0, keepdims=True))
                weights = jnp.exp(scores - new_top)
                if allowed is not None:
                    weights = jnp.where(allowed, weights, 0.0)
                shrink = jnp.exp(top - new_top)
                total = total * shrink + jnp.sum(weights, axis=0, keepdims=True)
                part = dot_tn(only(x_ref[key_half, ks, V], h), weights.astype(BF))
                acc = acc * shrink + part[h * HEAD : (h + 1) * HEAD]
                top = new_top
            top_ref[query_half, h : h + 1, qs] = top
            total_ref[query_half, h : h + 1, qs] = total
            acc_ref[query_half, h * HEAD : (h + 1) * HEAD, qs] = acc

        def diagonal(half):
            for qb in range(2):
                for h in range(2):
                    start = (
                        jnp.full((1, BLOCK), MASKED, F32),
                        jnp.zeros((1, BLOCK), F32),
                        jnp.zeros((HEAD, BLOCK), F32),
                    )
                    block(half, half, qb, h, start, True)

        def finish(half):
            for qb in range(2):
                qs = rows_of(qb)
                for h in range(2):
                    hs = slice(h * HEAD, (h + 1) * HEAD)
                    total = total_ref[half, h : h + 1, qs]
                    acc_ref[half, hs, qs] = acc_ref[half, hs, qs] / total
                    top_ref[half, h : h + 1, qs] = top_ref[half, h : h + 1, qs] + jnp.log(total)
                half_ref[half, qs, :] = acc_ref[half, :, qs].T.astype(BF)

        diagonal(xl)
        yield
        for copy in sent:
            copy.wait_recv()
        diagonal(1 - xl)
        yield
        for qb in range(2):
            for h in range(2):
                qs = rows_of(qb)
                state = (
                    top_ref[1, h : h + 1, qs],
                    total_ref[1, h : h + 1, qs],
                    acc_ref[1, h * HEAD : (h + 1) * HEAD, qs],
                )
                block(1, 0, qb, h, state, False)
            yield
        finish(1 - xl)
        back = remote(half_ref.at[1 - xl], o_ref.at[:, lanes(xl, 128)], sems, base + 3, pair)
        back.start()
        finish(xl)
        mine = pltpu.make_async_copy(half_ref.at[xl], o_ref.at[:, lanes(xl, 128)], sems.at[0, base + 4])
        mine.start()
        pending += sent + [back]
        yield
        mine.wait()
        back.wait_recv()


class AttendBack:
    peers = ("pair",)
    n_sems = 6

    def __init__(self):
        self.ins = [
            ((16, D), F32),
            ((2, HALF, 384), BF),
            ((HALF, 256), BF),
            ((2, 128, HALF), F32),
            ((2, 8, HALF), F32),
            ((2, 32, HALF), BF),
        ]
        self.outs = [((HALF, 768), BF)]
        self.scratch = [
            pltpu.VMEM((2, HALF, 128), BF),
            pltpu.VMEM((2, 128, HALF), F32),
            pltpu.VMEM((2, HALF, 128), F32),
            pltpu.VMEM((2, HALF, 128), F32),
            pltpu.VMEM((2, HALF, 384), BF),
        ]

    def run(self, ins, outs, scratch, sems, base, place, pending):
        params_ref, x_ref, own_ref, ot_ref, lse_ref, angles_ref = ins
        (out_ref,) = outs
        do_ref, dqt_ref, dk_ref, dv_ref, half_ref = scratch
        pair = place[4]["pair"]
        xl = lax.axis_index("xl")
        first_len = document_marks(params_ref)[0]
        sent = remote(own_ref.at[:, lanes(1 - xl, 128)], do_ref.at[xl], sems, base, pair)
        sent.start()
        kept = pltpu.make_async_copy(own_ref.at[:, lanes(xl, 128)], do_ref.at[xl], sems.at[0, base + 1])
        kept.start()
        kept.wait()
        yield

        def block(query_half, key_half, qb, h, diagonal):
            qs = rows_of(qb)
            hs = slice(h * HEAD, (h + 1) * HEAD)
            do = do_ref[query_half, qs, :]
            qh = only(x_ref[query_half, qs, Q] * jnp.asarray(HEAD**-0.5, BF), h)
            doh = only(do, h)
            delta = jnp.sum(
                doh.astype(F32).T[hs] * ot_ref[query_half, hs, qs], axis=0, keepdims=True
            )
            lse = lse_ref[query_half, h : h + 1, qs]
            for kb in range(qb + 1 if diagonal else 2):
                ks = rows_of(kb)
                k = x_ref[key_half, ks, K]
                scores = dot_nt(k, qh)
                probs = jnp.exp(scores - lse)
                allowed = allowed_mask(first_len, key_half, kb, query_half, qb, diagonal)
                if allowed is not None:
                    probs = jnp.where(allowed, probs, 0.0)
                pulled = dot_nt(x_ref[key_half, ks, V], doh)
                ds = (probs * (pulled - delta)).astype(BF)
                dv = dot_nn(probs.astype(BF), doh)
                dk = dot_nn(ds, qh)
                dq = dot_tn(only(k, h), ds)[hs]
                if diagonal and h == 0 and qb == kb:
                    dv_ref[key_half, ks, :] = dv
                    dk_ref[key_half, ks, :] = dk
                else:
                    dv_ref[key_half, ks, :] += dv
                    dk_ref[key_half, ks, :] += dk
                if diagonal and kb == 0:
                    dqt_ref[query_half, hs, qs] = dq
                else:
                    dqt_ref[query_half, hs, qs] += dq

        def finish(half):
            for b in range(2):
                bs = rows_of(b)
                cosine, below, above = rotary_tables(angles_ref[half, :, bs])
                dq = dqt_ref[half, :, bs].T * HEAD**-0.5
                half_ref[half, bs, Q] = rotate(dq, cosine, -below, -above).astype(BF)
                half_ref[half, bs, K] = rotate(dk_ref[half, bs, :], cosine, -below, -above).astype(BF)
                half_ref[half, bs, V] = dv_ref[half, bs, :].astype(BF)

        for qb in range(2):
            for h in range(2):
                block(xl, xl, qb, h, True)
        yield
        sent.wait_recv()
        for qb in range(2):
            for h in range(2):
                block(1 - xl, 1 - xl, qb, h, True)
        yield
        for qb in range(2):
            for h in range(2):
                block(1, 0, qb, h, False)
            yield
        finish(1 - xl)
        back = remote(half_ref.at[1 - xl], out_ref.at[:, lanes(xl, 384)], sems, base + 2, pair)
        back.start()
        finish(xl)
        mine = pltpu.make_async_copy(half_ref.at[xl], out_ref.at[:, lanes(xl, 384)], sems.at[0, base + 3])
        mine.start()
        pending += [sent, back]
        yield
        mine.wait()
        back.wait_recv()


def feed_kernel(h_ref, dy_ref, gate_ref, up_ref, down_ref, hid_ref, dg_ref, du_ref, dh_ref):
    gate, up = dot_nn(h_ref[...], gate_ref[...]), dot_nn(h_ref[...], up_ref[...])
    sigmoid = jax.nn.sigmoid(gate)
    activated = gate * sigmoid
    hidden = (activated * up).astype(BF)
    hid_ref[...] = hidden
    d_hidden = dot_nt(dy_ref[...], down_ref[...])
    d_gate = (d_hidden * up * sigmoid * (1.0 + gate * (1.0 - sigmoid))).astype(BF)
    d_up = (d_hidden * activated).astype(BF)
    dg_ref[...] = d_gate
    du_ref[...] = d_up
    dh_ref[...] = (dot_nt(d_gate, gate_ref[...]) + dot_nt(d_up, up_ref[...])).astype(BF)


def feed_call(h, dy, w_gate, w_up, w_down):
    return pl.pallas_call(
        feed_kernel,
        out_shape=(
            jax.ShapeDtypeStruct((HALF, 768), BF),
            jax.ShapeDtypeStruct((HALF, 768), BF),
            jax.ShapeDtypeStruct((HALF, 768), BF),
            pltpu.HBM((HALF, D), BF),
        ),
        grid=(HALF // ROWS,),
        in_specs=[rowwise(D), rowwise(D), fixed(D, 768), fixed(D, 768), fixed(768, D)],
        out_specs=(rowwise(768), rowwise(768), rowwise(768), rowwise(D)),
        compiler_params=pltpu.CompilerParams(vmem_limit_bytes=34 << 20),
        cost_estimate=pl.CostEstimate(
            flops=5 * 2 * HALF * D * 768, bytes_accessed=26 << 20, transcendentals=HALF * 768
        ),
    )(h, dy, w_gate, w_up, w_down)


def wide_update_kernel(qkv_ref, gate_ref, up_ref, *refs):
    ins, outs = refs[:9], refs[9:]

    def update(k, at, gradient):
        new = adamw(*[ref[:, at] for ref in ins[k * 3 : k * 3 + 3]], gradient, D ** (-0.5), 0.1)
        for ref, value in zip(outs[k * 3 : k * 3 + 3], new):
            ref[:, at] = value

    for k in range(8):
        for pair in range(2):
            for kind in range(3):
                update(
                    0,
                    columns(kind * D + k * 256 + pair * 128, 128),
                    qkv_ref[k, :, columns(pair * 384 + kind * 128, 128)].astype(F32),
                )
    pieces = [(o * 44, o % 8, o // 8 * 48, 44) for o in range(128)]
    for w, grad_ref in enumerate((gate_ref, up_ref)):
        for tile in range(FF // 128):
            value = moved(lambda k, at: grad_ref[k, :, at], tile, pieces, 768 - 256)
            update(1 + w, columns(tile * 128, 128), value)


def wide_updates(grads, *states):
    operands = [x for state in states for x in state]
    return pl.pallas_call(
        wide_update_kernel,
        out_shape=[jax.ShapeDtypeStruct(x.shape, F32) for x in operands],
        in_specs=[pl.BlockSpec(memory_space=pltpu.VMEM)] * 12,
        out_specs=[pl.BlockSpec(memory_space=pltpu.VMEM)] * 9,
        compiler_params=pltpu.CompilerParams(vmem_limit_bytes=24 << 20),
        cost_estimate=pl.CostEstimate(flops=20 << 20, bytes_accessed=10 << 20, transcendentals=1 << 20),
    )(*grads, *operands)


TO_HEADS = [(f * 16 + ctx, ctx * 8 + f) for f in range(8) for ctx in range(16)]
TO_OWNER = [(b, a) for a, b in TO_HEADS]


def local(
    hidden_in, out_grad, positions, documents,
    qkv_weight, qkv_first, qkv_second,
    out_weight, out_first, out_second,
    gate_weight, gate_first, gate_second,
    up_weight, up_first, up_second,
    down_weight, down_first, down_second,
    small_params, small_first, small_second,
):
    xh, xl, z = lax.axis_index("xh"), lax.axis_index("xl"), lax.axis_index("z")
    yc = lax.axis_index("y") * 2 + lax.axis_index("core")
    place = (z * 2 + xh) * 2 + xl

    first_here = jnp.sum(1 - documents)
    start_here = positions[0, 0]
    marks = jnp.stack([first_here, start_here // 64, start_here % 64]).astype(BF)
    tile = jnp.concatenate(
        [small_params.astype(BF), jnp.pad(marks, (0, 13))[None]], axis=0
    )
    tile = jnp.where((jnp.arange(8) == yc)[None, :, None], tile[:, None, :], 0)
    tile = jnp.pad(tile.reshape(8, 128), ((0, 8), (0, 0)))
    outer = out_grad.reshape(128, D)
    out_rows = lax.ppermute(out_weight.astype(BF), AXES, TO_HEADS)
    share, units = ShareQkv(), GatherTokens(128, D, normalize=True, far=True)
    w_all, params, u_all, gu_mine, w_out, h1, qkv, angles = comm(
        0,
        "adbccdddccddabccdccaacaaabbabbaabce",
        (share, (qkv_weight, tile)),
        (units, (hidden_in,)),
        (ShareHidden(), (gate_weight, up_weight)),
        (GatherSmall(16, D), (out_rows,)),
        (MakeQkv(share, units), ()),
    )
    u_all, w_qkv, w_out = u_all.reshape(HALF, D), w_all.reshape(D, 896), w_out.reshape(256, D)
    gu_mine = gu_mine.reshape(128, 1536)
    o, attended_t, lse, heads, dy, w_gate = comm(
        1,
        "abcabbccacbbaaccabca",
        (Attend(), (params, qkv)),
        (GatherTokens(128, D, far=True), (outer,)),
        (GatherWeights(128, 768), (gu_mine[:, :768],)),
    )
    dy = dy.reshape(HALF, D)
    branch_part = dot_nn(o, w_out).astype(BF)
    branch, w_up = comm(
        2,
        "ababbbbaabbab",
        (SumTokens(128, D), (branch_part,)),
        (GatherWeights(128, 768), (gu_mine[:, 768:],)),
    )
    rows = hidden_in.reshape(128, D).astype(F32)
    middle = rows + branch
    normed_two, unit_two, scale_two = norm_forward(middle, params[5], params[6])
    down_piece = jnp.pad(down_weight.astype(BF), ((0, 4), (0, 0)))
    h2, w_down = comm(
        3,
        "abbbbaabbaabab",
        (GatherTokens(128, D), (normed_two.astype(BF),)),
        (GatherWeights(48, D), (down_piece,)),
    )
    h2 = h2.reshape(HALF, D)
    w_down = w_down.reshape(768, D)
    hidden, d_gate_low, d_up_low, dh2_part = feed_call(
        h2, dy, w_gate.reshape(D, 768), w_up.reshape(D, 768), w_down
    )

    d_normed_two, g_down, d_gate, d_up = comm(
        4,
        "abbbaccbbaacccbccbbacb",
        (far(SumTokens(128, D), 0), (dh2_part,)),
        (far(GradThenSum(768, D, 2), 1), (hidden, dy)),
        (far(TokenSums(D, 768, 2), 0), (h2, d_gate_low, d_up_low)),
    )
    d_middle_part, d_gain_two, d_shift_two = norm_backward(
        d_normed_two, unit_two, scale_two, params[5]
    )
    d_middle = outer.astype(F32) + d_middle_part
    dx2, g_gate, y_part = comm(
        5,
        "abcbbcaacbbbcaaab",
        (GatherTokens(128, D), (d_middle.astype(BF),)),
        (SumWeights(128, 768), (d_gate,)),
        (Product(768, D), (hidden, w_down)),
    )
    dx2 = dx2.reshape(HALF, D)
    do = dot_nt(dx2, w_out).astype(BF)
    d_qkv_low, block_out, g_up, gate_back = comm(
        7,
        "abcdabaccaaabbcccdbca",
        (AttendBack(), (params, heads, do, attended_t, lse, angles)),
        (SumTokens(128, D, plus=True), (y_part, middle)),
        (SumFew(128, 768), (d_up,)),
        (Swap(16, 768), (g_gate,)),
    )
    d_out = dot_tn(o, dx2).astype(BF)
    zeros = jnp.zeros((5, D), F32)
    last = LastRows()
    input_grad, qkv_back, g_out, g_small, up_back = comm(
        6,
        "ecbbbbbaaccaadbbacdbaaccdddbbcddabdb",
        (far(last, 1, 2), (d_qkv_low, u_all, w_qkv, hidden_in, d_middle, params)),
        (far(GradThenSum(D, 768, 4, swap=True), 0), (h1, d_qkv_low)),
        (SumFew(16, D), (d_out,)),
        (SumSmall(last), (jnp.concatenate([zeros, d_gain_two[None], d_shift_two[None], zeros[:1]]),)),
        (Swap(16, 768), (g_up,)),
    )
    block_out, input_grad = block_out.reshape(1, 128, D), input_grad.reshape(1, 128, D)

    small = lax.dynamic_slice_in_dim(g_small, place * 16, 16, axis=1)
    owned = lax.ppermute(
        jnp.concatenate([g_out, jnp.pad(small, ((0, 0), (0, 112)))], axis=1), AXES, TO_OWNER
    )
    g_out, g_small = owned[:, :D].astype(F32), owned[:7, D : D + 16].astype(F32)

    wide = wide_updates(
        (qkv_back, gate_back, up_back),
        (qkv_weight, qkv_first, qkv_second),
        (gate_weight, gate_first, gate_second),
        (up_weight, up_first, up_second),
    )
    updates = (
        wide[0:3],
        adamw(out_weight, out_first, out_second, g_out, (D // 16) ** (-0.5), 0.1),
        wide[3:6],
        wide[6:9],
        adamw(down_weight, down_first, down_second, g_down[:44].astype(F32), FF ** (-0.5), 0.1),
        adamw(small_params, small_first, small_second, g_small, 2.0, 0.0),
    )
    return (block_out, input_grad, *[x for u in updates for x in u])


def solution(mesh):
    fine = Mesh(mesh.devices.reshape(4, 2, 2, 4, 2), AXES)
    tokens = P(("z", "xh"), ("xl", "y", "core"), None)
    marks = P(("z", "xh"), ("xl", "y", "core"))
    rows = P(AXES, None)
    small = P(None, AXES)
    in_specs = (tokens, tokens, marks, marks) + (rows,) * 15 + (small,) * 3
    out_specs = (tokens, tokens) + (rows,) * 15 + (small,) * 3
    return jax.shard_map(local, mesh=fine, in_specs=in_specs, out_specs=out_specs, check_vma=False)
```
